128 devices in a mesh: seq: 32 (over z, y, core), head: 4 (over x).
Axes of the slice: x: 4, y: 4, z: 4, core: 2. Of those that a mesh axis runs over, the one named last changes fastest.
Arguments:
- query: bfloat16 [65536, 1024], P('seq', 'head'), may hold values from -6 to 6
- keys: bfloat16 [65536, 1024], P('seq', 'head'), may hold values from -6 to 6
- values: bfloat16 [65536, 1024], P('seq', 'head'), may hold values from -6 to 6
- output: bfloat16 [65536, 1024], P('seq', 'head'), may hold values from -6 to 6
- d_out: bfloat16 [65536, 1024], P(('seq', 'head')), may hold values from -1.5 to 1.5
- row_logsum: float32 [8, 65536], P('head', 'seq'), may hold values from 3.5 to 4.5
- selected: int32 [128, 3], replicated, may hold values from 0 to 123, as said below
Outputs:
- query_grad: bfloat16 [65536, 1024], P('seq', 'head')
- key_grad: bfloat16 [65536, 1024], P('seq', 'head')
- value_grad: bfloat16 [65536, 1024], P('seq', 'head')
The draws below stay inside these ranges and needn't reach their ends.
Inputs may be any that keep to these rules, and one draw needn't show every extreme that they name: `selected`: each nonzero entry of row g names a block other than block 0 that is held by a seq index lower than the seq index holding block g. Among the 12 entries of the query blocks of one seq index, at most one names a block of any one other seq index.
All inputs are finite; a program needn't handle non-finite values.
Results may differ from the reference program's by a relative error of at most 0.0063.
Values may be sent and summed in bfloat16 or wider, within the bound.
A program may use at most 192 MiB of HBM per device.

```python
import math
import jax
import jax.numpy as jnp
from jax import lax

BLOCK = 512
HD = 128
SEL = 3
BLK_DEV = 4
NBLK = 128
TOKENS = 65536
HEADS = 8


def draw_selected(key, part):
    key = jax.random.fold_in(key, 7)
    key_heat, key_noise, key_offset, key_order = jax.random.split(key, 4)
    seq_count = NBLK // BLK_DEV
    picks = SEL * BLK_DEV
    devices = jnp.arange(seq_count, dtype=jnp.int32)
    heat = jax.random.randint(key_heat, (seq_count,), 0, 4)
    noise = jax.random.randint(key_noise, (seq_count, seq_count), 0, 4096)
    allowed = devices[None, :] < devices[:, None]
    score = (heat[None, :] * 4096 + noise) * seq_count + devices[None, :]
    score = jnp.where(allowed, score + 16 * 4096 * seq_count, score)
    forced = (devices[:, None] == seq_count - 1) & (devices[None, :] == 0)
    score = jnp.where(forced, score + 32 * 4096 * seq_count, score)
    count = min(picks, seq_count)
    top_scores, chosen = lax.top_k(score, count)
    valid = jnp.take_along_axis(allowed, chosen, axis=1)
    offset_raw = jax.random.randint(key_offset, (seq_count, count), 0, BLK_DEV)
    offset = jnp.where(chosen == 0, 1 + offset_raw % (BLK_DEV - 1), offset_raw)
    blocks = jnp.where(valid, chosen * BLK_DEV + offset, 0).astype(jnp.int32)
    blocks = jnp.concatenate([blocks, jnp.zeros((seq_count, picks - count), jnp.int32)], axis=1)
    order_keys = jax.random.randint(key_order, (seq_count, picks), 0, 4096) * picks + jnp.arange(picks, dtype=jnp.int32)[None, :]
    order = jnp.argsort(order_keys, axis=1, stable=True)
    blocks = jnp.take_along_axis(blocks, order, axis=1)
    return blocks.reshape(NBLK, SEL).astype(jnp.int32)


def shard_levels(key, extent, cuts, low, high):
    loudness, own = 1.0, jax.random.fold_in(key, 6)
    for axis_at, parts in cuts:
        steps = jnp.exp(jax.random.uniform(jax.random.fold_in(own, axis_at), (parts,), jnp.float32, low / len(cuts), high / len(cuts)))
        loudness = loudness * jnp.repeat(steps, extent[axis_at] // parts).reshape([-1 if axis == axis_at else 1 for axis in range(len(extent))])
    return loudness


def centred(rng, shape, spread, limit, pieces=(), held_as=jnp.bfloat16):
    array = spread * jax.random.normal(rng, shape, jnp.float32)
    if pieces:
        array = array * shard_levels(rng, shape, pieces, -0.22, 0.18)
    return jnp.clip(array, -limit, limit).astype(held_as)


def setup_inputs(seed: int = 0) -> dict:
    arg_keys = jax.random.split(jax.random.key(seed), 8)
    return {
        "query": centred(arg_keys[0], (TOKENS, HEADS * HD), 1.0, 6.0, ((0, 32), (1, 4))),
        "keys": centred(arg_keys[1], (TOKENS, HEADS * HD), 1.0, 6.0, ((0, 32), (1, 4))),
        "values": centred(arg_keys[2], (TOKENS, HEADS * HD), 1.0, 6.0, ((0, 32), (1, 4))),
        "output": centred(arg_keys[3], (TOKENS, HEADS * HD), 1.0, 6.0, ((0, 32), (1, 4))),
        "d_out": centred(arg_keys[4], (TOKENS, HEADS * HD), 0.25, 1.5, ((0, 128),)),
        "row_logsum": jnp.clip(3.5 + 1.0 * jax.random.uniform(arg_keys[5], (HEADS, TOKENS), jnp.float32) ** shard_levels(arg_keys[5], (HEADS, TOKENS), ((0, 4), (1, 32)), -0.2, 0.2), 3.5, 4.5),
        "selected": draw_selected(jax.random.fold_in(arg_keys[7], 71), 0),
    }


def reference(query, keys, values, output, d_out, row_logsum, selected):
    scale = 1.0 / math.sqrt(HD)
    query_all = query.reshape(NBLK, BLOCK, HEADS, HD)
    key_all = keys.reshape(NBLK, BLOCK, HEADS, HD)
    value_all = values.reshape(NBLK, BLOCK, HEADS, HD)
    grad_all = d_out.reshape(NBLK, BLOCK, HEADS, HD)
    out_all = output.reshape(NBLK, BLOCK, HEADS, HD)
    delta = lax.optimization_barrier(jnp.sum(grad_all.astype(jnp.float32) * out_all.astype(jnp.float32), axis=3))
    delta = jnp.transpose(delta, (0, 2, 1))
    logsum = jnp.transpose(row_logsum.reshape(HEADS, NBLK, BLOCK), (1, 0, 2))
    positions = jnp.arange(BLOCK, dtype=jnp.int32)
    causal = positions[None, :] <= positions[:, None]
    slots = jnp.arange(SEL + 2, dtype=jnp.int32)

    def step(carry, block_id):
        key_total, value_total = carry
        chosen = selected[block_id].astype(jnp.int32)
        indices = jnp.concatenate([jnp.stack([block_id, jnp.zeros((), jnp.int32)]).astype(jnp.int32), chosen])
        active = jnp.concatenate([jnp.ones((1,), bool), jnp.reshape(block_id >= 1, (1,)), chosen > 0])
        mask = jnp.where((slots == 0)[None, :, None], causal[:, None, :], active[None, :, None])
        query_blk = query_all[block_id].astype(jnp.float32)
        grad_blk = grad_all[block_id].astype(jnp.float32)
        key_stack = key_all[indices].astype(jnp.float32)
        value_stack = value_all[indices].astype(jnp.float32)
        scores = jnp.einsum('ihd,bjhd->hibj', query_blk, key_stack) * scale
        weights = jnp.where(mask[None], jnp.exp(scores - logsum[block_id][:, :, None, None]), 0.0)
        weight_grad = jnp.einsum('ihd,bjhd->hibj', grad_blk, value_stack)
        score_grad = (weights * (weight_grad - delta[block_id][:, :, None, None])).astype(jnp.bfloat16)
        weights_low = weights.astype(jnp.bfloat16)
        score_float = score_grad.astype(jnp.float32)
        query_grad = jnp.einsum('hibj,bjhd->ihd', score_float, key_stack) * scale
        key_term = jnp.einsum('hibj,ihd->bjhd', score_float, query_blk) * scale
        value_term = jnp.einsum('hibj,ihd->bjhd', weights_low.astype(jnp.float32), grad_blk)
        keep = (slots < 2)[:, None, None, None]
        key_round = lax.optimization_barrier(key_term.astype(jnp.bfloat16)).astype(jnp.float32)
        value_round = lax.optimization_barrier(value_term.astype(jnp.bfloat16)).astype(jnp.float32)
        key_term = jnp.where(keep, key_term, key_round)
        value_term = jnp.where(keep, value_term, value_round)
        key_total = key_total.at[indices].add(key_term)
        value_total = value_total.at[indices].add(value_term)
        return ((key_total, value_total), query_grad.astype(jnp.bfloat16))
    zeros = jnp.zeros((NBLK, BLOCK, HEADS, HD), jnp.float32)
    (key_total, value_total), query_grad = lax.scan(step, (zeros, zeros), jnp.arange(NBLK, dtype=jnp.int32))
    return (query_grad.reshape(TOKENS, HEADS * HD), key_total.reshape(TOKENS, HEADS * HD).astype(jnp.bfloat16), value_total.reshape(TOKENS, HEADS * HD).astype(jnp.bfloat16))
```

```python
import functools
import math

import jax
import jax.numpy as jnp
from jax import lax
from jax.experimental import pallas as pl
from jax.experimental.pallas import tpu as pltpu
from jax.sharding import PartitionSpec as P

MESH = pl.DeviceIdType.MESH
BLOCK = 512
HD = 128
WIDTH = 256
BLK_DEV = 4
RING = 4
NSLOT = 33
FIRST = 32
LOG2E = math.log2(math.e)
MIB = 1024 * 1024


def place():
    seq = lax.axis_index("seq")
    return lax.div(seq, 8), lax.rem(lax.div(seq, 2), 4), lax.rem(seq, 2), lax.axis_index("head")


def device(z, y, c, x):
    return ((z * 4 + y) * 2 + c, x)


def after(index, step):
    return lax.rem(index + step, RING)


def neighbours(z, y, c, x):
    return {
        "sib": device(z, y, 1 - c, x),
        "zr": device(after(z, 1), y, c, x),
        "zl": device(after(z, 3), y, c, x),
        "yr": device(z, after(y, 1), c, x),
        "yl": device(z, after(y, 3), c, x),
    }


def greet(devices):
    barrier = pltpu.get_barrier_semaphore()
    for target in devices:
        pl.semaphore_signal(barrier, inc=1, device_id=target, device_id_type=MESH)
    pl.semaphore_wait(barrier, len(devices))


def gather_kernel(
    keys, values, query, d_out, output, logsum,
    kg, vg, qg, gg, sg,
    grad, outv, stats, send, recv, local,
):
    z, y, c, x = place()
    near = neighbours(z, y, c, x)
    others = [((z * 4 + y) * 2 + c, after(x, step)) for step in (1, 2, 3)]
    greet(list(near.values()) + others)
    started = []

    def remote(index, src, dst, target):
        return pltpu.make_async_remote_copy(
            src_ref=src, dst_ref=dst, send_sem=send.at[index], recv_sem=recv.at[index],
            device_id=target, device_id_type=MESH,
        )

    def go(index, src, dst, target):
        copy = remote(index, src, dst, target)
        copy.start()
        started.append(copy)
        return copy

    def column(z_at, c_at):
        return pl.ds((z_at * 2 + c_at) * BLK_DEV, BLK_DEV)

    def row(y_at):
        return pl.ds(y_at * BLK_DEV, BLK_DEV)

    zl, zr, zo = after(z, 3), after(z, 1), after(z, 2)
    yl, yr = after(y, 3), after(y, 1)
    root = (z == 0) & (y == 0) & (c == 0)
    for step in (1, 2, 3):
        to = after(x, step)
        go(
            22 + step,
            d_out.at[:, pl.ds(pl.multiple_of(to * WIDTH, WIDTH), WIDTH)],
            grad.at[x],
            others[step - 1],
        )
    locals_ = [
        pltpu.make_async_copy(
            d_out.at[:, pl.ds(pl.multiple_of(x * WIDTH, WIDTH), WIDTH)], grad.at[x], local.at[0]
        ),
        pltpu.make_async_copy(output, outv, local.at[1]),
        pltpu.make_async_copy(keys, kg.at[column(z, c)], local.at[2]),
        pltpu.make_async_copy(values, vg.at[column(z, c)], local.at[3]),
        pltpu.make_async_copy(query, qg.at[row(y)], local.at[4]),
    ]
    for copy in locals_:
        copy.start()
    first_own = [
        pltpu.make_async_copy(keys.at[0], kg.at[FIRST], local.at[5]),
        pltpu.make_async_copy(values.at[0], vg.at[FIRST], local.at[6]),
    ]

    @pl.when(root)
    def _():
        for copy in first_own:
            copy.start()
        for copy in first_own:
            copy.wait()

    def first_copies(slot, target):
        return [
            pltpu.make_async_remote_copy(
                src_ref=ref.at[FIRST], dst_ref=ref.at[FIRST],
                send_sem=send.at[28 + 2 * slot + part], recv_sem=recv.at[26 + part],
                device_id=target, device_id_type=MESH,
            )
            for part, ref in enumerate((kg, vg))
        ]

    first_sends = [
        ((z == 0) & (c == 0) & (y <= 1), first_copies(0, near["yr"])),
        ((z == 0) & (c == 0) & (y == 0), first_copies(1, near["yl"])),
        ((c == 0) & (z <= 1), first_copies(2, near["zr"])),
        ((c == 0) & (z == 0), first_copies(3, near["zl"])),
        (c == 0, first_copies(4, near["sib"])),
    ]

    def send_first():
        for condition, copies in first_sends:
            @pl.when(condition)
            def _(copies=copies):
                for copy in copies:
                    copy.start()

    @pl.when(root)
    def _():
        send_first()

    own = column(z, c)
    go(0, keys, kg.at[own], near["zr"])
    go(1, values, vg.at[own], near["zl"])
    go(2, values, vg.at[own], near["zr"])
    go(3, keys, kg.at[own], near["zl"])
    go(4, keys, kg.at[own], near["sib"])
    go(5, values, vg.at[own], near["sib"])
    go(14, query, qg.at[row(y)], near["yr"])
    go(15, query, qg.at[row(y)], near["yl"])

    locals_[0].wait()
    locals_[1].wait()
    for step in (1, 2, 3):
        remote(22 + step, grad.at[x], grad.at[x], others[step - 1]).wait_recv()
    go(16, grad, gg.at[row(y)], near["yl"])
    go(17, grad, gg.at[row(y)], near["yr"])
    keep = pltpu.make_async_copy(grad, gg.at[row(y)], local.at[7])
    keep.start()
    ones = jnp.ones((8, HD), jnp.bfloat16)
    contract = (((1,), (1,)), ((), ()))
    stats[...] = jnp.zeros_like(stats)
    for block in range(BLK_DEV):
        for head in range(2):
            part = pl.ds(head * HD, HD)
            product = grad[block, :, part].astype(jnp.float32) * outv[block, :, part].astype(jnp.float32)
            high = product.astype(jnp.bfloat16)
            low = (product - high.astype(jnp.float32)).astype(jnp.bfloat16)
            total = lax.dot_general(ones, high, contract, preferred_element_type=jnp.float32)
            total += lax.dot_general(ones, low, contract, preferred_element_type=jnp.float32)
            stats[block, pl.ds(2 + head, 1), :] = total[0:1]
            stats[block, pl.ds(head, 1), :] = (
                logsum[pl.ds(head, 1), pl.ds(block * BLOCK, BLOCK)] * LOG2E
            )
    go(18, stats, sg.at[row(y)], near["yr"])
    go(19, stats, sg.at[row(y)], near["yl"])
    keep_stats = pltpu.make_async_copy(stats, sg.at[row(y)], local.at[8])
    keep_stats.start()

    @pl.when(jnp.logical_not(root))
    def _():
        for copy in first_copies(0, near["sib"]):
            copy.wait_recv()
        send_first()

    def arrived(index, ref, piece, source):
        remote(index, ref.at[piece], ref.at[piece], source).wait_recv()

    def forward(index, ref, piece, target):
        go(index, ref.at[piece], ref.at[piece], target)

    left_k, right_k = column(zl, c), column(zr, c)
    arrived(0, kg, left_k, near["zl"])
    forward(6, kg, left_k, near["zr"])
    forward(8, kg, left_k, near["sib"])
    arrived(1, vg, right_k, near["zr"])
    forward(7, vg, right_k, near["zl"])
    forward(9, vg, right_k, near["sib"])
    arrived(14, qg, row(yl), near["yl"])
    forward(20, qg, row(yl), near["yr"])
    arrived(16, gg, row(yr), near["yr"])
    forward(21, gg, row(yr), near["yl"])
    arrived(18, sg, row(yl), near["yl"])
    forward(22, sg, row(yl), near["yr"])
    arrived(2, vg, left_k, near["zl"])
    forward(10, vg, left_k, near["sib"])
    arrived(3, kg, right_k, near["zr"])
    forward(11, kg, right_k, near["sib"])
    far_k = column(zo, c)
    arrived(6, kg, far_k, near["zl"])
    forward(12, kg, far_k, near["sib"])
    arrived(7, vg, far_k, near["zr"])
    forward(13, vg, far_k, near["sib"])
    arrived(15, qg, row(yr), near["yr"])
    arrived(17, gg, row(yl), near["yl"])
    arrived(19, sg, row(yr), near["yr"])
    arrived(20, qg, row(after(y, 2)), near["yl"])
    arrived(21, gg, row(after(y, 2)), near["yr"])
    arrived(22, sg, row(after(y, 2)), near["yl"])
    for index, ref, z_at in (
        (4, kg, z), (5, vg, z), (8, kg, zl), (9, vg, zr),
        (10, vg, zl), (11, kg, zr), (12, kg, zo), (13, vg, zo),
    ):
        arrived(index, ref, column(z_at, 1 - c), near["sib"])
    for copy in locals_[2:] + [keep, keep_stats]:
        copy.wait()
    for copy in started:
        copy.wait_send()
    for condition, copies in first_sends:
        @pl.when(condition)
        def _(copies=copies):
            for copy in copies:
                copy.wait_send()


def pair_kernel(
    selected, kg, vg, qg, gg, sg,
    pk, pv, pq,
    table, items, kbuf, vbuf, qbuf, gbuf, dq, dk, dv, kout, vout, qout, zero,
    in_sem, out_sem, q_sem, zero_sem,
):
    z, y, c, _ = place()
    scale = 1.0 / math.sqrt(HD)

    def clear(at, carry):
        table[at] = 0
        return carry

    lax.fori_loop(0, NSLOT * 4, clear, 0)
    for yq in range(4):
        def enter(at, carry, yq=yq):
            block = lax.div(at, 3)
            chosen = selected[(((z * 4 + yq) * 2 + c) * BLK_DEV + block) * 3 + lax.rem(at, 3)]
            owner = lax.div(chosen, BLK_DEV)
            here = (chosen > 0) & (lax.rem(lax.div(owner, 2), 4) == y)
            slot = (lax.div(owner, 8) * 2 + lax.rem(owner, 2)) * BLK_DEV + lax.rem(chosen, BLK_DEV)

            @pl.when(here)
            def _():
                table[slot * 4 + yq] = 1 + yq * BLK_DEV + block
            return carry

        lax.fori_loop(0, BLK_DEV * 3, enter, 0)
    for block in range(BLK_DEV):
        mine = (z * 2 + c) * BLK_DEV + block
        table[mine * 4 + y] = 1 + y * BLK_DEV + block + 64
        later = ((z * 4 + y) * 2 + c) * BLK_DEV + block > 0
        table[FIRST * 4 + block] = jnp.where(later, 1 + y * BLK_DEV + block, 0)

    def compact(at, count):
        entry = table[at]
        items[count] = at * 128 + entry
        return count + jnp.where(entry > 0, 1, 0)

    count = lax.fori_loop(0, NSLOT * 4, compact, 0)
    items[count] = -1

    zero[...] = jnp.zeros_like(zero)

    def idle(slot):
        return (
            table[slot * 4] + table[slot * 4 + 1] + table[slot * 4 + 2] + table[slot * 4 + 3]
        ) == 0

    def blank(slot):
        return [
            pltpu.make_async_copy(zero, ref.at[slot], zero_sem.at[slot, part])
            for part, ref in enumerate((pk, pv))
        ]

    def start_blank(slot, carry):
        @pl.when(idle(slot))
        def _():
            for copy in blank(slot):
                copy.start()
        return carry

    lax.fori_loop(0, NSLOT, start_blank, 0)

    def decode(item):
        slot = lax.div(item, 512)
        entry = lax.rem(item, 128) - 1
        return slot, lax.rem(entry, 64), entry >= 64

    def loads(at):
        slot, block, _ = decode(items[at])
        side = lax.rem(at, 2)
        return [
            pltpu.make_async_copy(kg.at[slot], kbuf.at[side], in_sem.at[side, 0]),
            pltpu.make_async_copy(vg.at[slot], vbuf.at[side], in_sem.at[side, 1]),
            pltpu.make_async_copy(qg.at[block], qbuf.at[side], in_sem.at[side, 2]),
            pltpu.make_async_copy(gg.at[block], gbuf.at[side], in_sem.at[side, 3]),
        ]

    for copy in loads(0):
        copy.start()
    dq[...] = jnp.zeros_like(dq)

    nt = (((1,), (1,)), ((), ()))
    nn = (((1,), (0,)), ((), ()))
    tn = (((0,), (0,)), ((), ()))

    def dot(a, b, dims):
        return lax.dot_general(a, b, dims, preferred_element_type=jnp.float32)

    def work(side, block, causal):
        for head in range(2):
            part = pl.ds(head * HD, HD)
            k, v = kbuf[side, :, part], vbuf[side, :, part]
            q, g = qbuf[side, :, part], gbuf[side, :, part]
            lse = sg[block, pl.ds(head, 1), :]
            delta = sg[block, pl.ds(2 + head, 1), :]
            p = jnp.exp2(dot(k, q, nt) * (scale * LOG2E) - lse)
            if causal:
                key_at = lax.broadcasted_iota(jnp.int32, (BLOCK, BLOCK), 0)
                query_at = lax.broadcasted_iota(jnp.int32, (BLOCK, BLOCK), 1)
                p = jnp.where(key_at <= query_at, p, 0.0)
            ds = (p * (dot(v, g, nt) - delta)).astype(jnp.bfloat16)
            dv[:, part] += dot(p.astype(jnp.bfloat16), g, nn)
            dk[:, part] += dot(ds, q, nn)
            dq[block, :, part] += dot(ds, k, tn)

    outs = [
        pltpu.make_async_copy(kout, pk.at[0], out_sem.at[0]),
        pltpu.make_async_copy(vout, pv.at[0], out_sem.at[1]),
    ]

    def item_step(at, carry):
        opened, written = carry
        slot, block, causal = decode(items[at])
        following = items[at + 1]
        side = lax.rem(at, 2)

        @pl.when(following >= 0)
        def _():
            for copy in loads(at + 1):
                copy.start()

        for copy in loads(at):
            copy.wait()

        @pl.when(slot != opened)
        def _():
            dk[...] = jnp.zeros_like(dk)
            dv[...] = jnp.zeros_like(dv)

        @pl.when(causal)
        def _():
            work(side, block, True)

        @pl.when(jnp.logical_not(causal))
        def _():
            work(side, block, False)

        closing = (following < 0) | (lax.div(following, 512) != slot)

        @pl.when(closing)
        def _():
            @pl.when(written > 0)
            def _():
                for copy in outs:
                    copy.wait()
            kout[...] = (dk[...] * scale).astype(jnp.bfloat16)
            vout[...] = dv[...].astype(jnp.bfloat16)
            pltpu.make_async_copy(kout, pk.at[slot], out_sem.at[0]).start()
            pltpu.make_async_copy(vout, pv.at[slot], out_sem.at[1]).start()

        return slot, written + jnp.where(closing, 1, 0)

    lax.fori_loop(0, count, item_step, (-1, 0))

    def finish(block, carry):
        qout[block] = (dq[block] * scale).astype(jnp.bfloat16)
        pltpu.make_async_copy(qout.at[block], pq.at[block], q_sem.at[block]).start()
        return carry

    lax.fori_loop(0, 16, finish, 0)
    for copy in outs:
        copy.wait()

    def drain(block, carry):
        pltpu.make_async_copy(qout.at[block], pq.at[block], q_sem.at[block]).wait()
        return carry

    lax.fori_loop(0, 16, drain, 0)

    def wait_blank(slot, carry):
        @pl.when(idle(slot))
        def _():
            for copy in blank(slot):
                copy.wait()
        return carry

    lax.fori_loop(0, NSLOT, wait_blank, 0)


def scatter_kernel(
    pk, pv, pq,
    out_q, out_k, out_v,
    ownk, ownv, sibk, sibv, relk, relv, fink, finv,
    ownq, relq, finq, fown, frecv, fsum, fsend,
    send, recv, local,
):
    z, y, c, x = place()
    near = neighbours(z, y, c, x)
    greet(list(near.values()))
    started = []

    def remote(index, src, dst, target):
        return pltpu.make_async_remote_copy(
            src_ref=src, dst_ref=dst, send_sem=send.at[index], recv_sem=recv.at[index],
            device_id=target, device_id_type=MESH,
        )

    def go(index, src, dst, target):
        copy = remote(index, src, dst, target)
        copy.start()
        started.append(copy)

    def came(index, dst):
        remote(index, dst, dst, near["sib"]).wait_recv()

    def column(z_at, c_at):
        return pl.ds((z_at * 2 + c_at) * BLK_DEV, BLK_DEV)

    hops = (2, 1, 3, 0)
    parts = ((pk, ownk, sibk), (pv, ownv, sibv))
    locals_k = []
    for j, hop in enumerate(hops):
        for part, (ref, held, other) in enumerate(parts):
            go(2 * j + part, ref.at[column(after(z, hop), 1 - c)], other.at[j], near["sib"])
            copy = pltpu.make_async_copy(
                ref.at[column(after(z, hop), c)], held.at[j], local.at[2 * j + part]
            )
            copy.start()
            locals_k.append(copy)
        if j == 0:
            locals_q = []
            for jq, hop_q in enumerate(hops):
                copy = pltpu.make_async_copy(
                    pq.at[pl.ds(after(y, hop_q) * BLK_DEV, BLK_DEV)], ownq.at[jq], local.at[8 + jq]
                )
                copy.start()
                locals_q.append(copy)
            locals_f = [
                pltpu.make_async_copy(ref.at[FIRST], fown.at[part], local.at[12 + part])
                for part, ref in enumerate((pk, pv))
            ]
            for copy in locals_f:
                copy.start()

    def add(dst, src, blocks):
        def one(block, carry):
            dst[block] = (dst[block].astype(jnp.float32) + src[block].astype(jnp.float32)).astype(
                jnp.bfloat16
            )
            return carry

        lax.fori_loop(blocks[0], blocks[1], one, 0)

    def merge(j, part):
        _, held, other = parts[part]
        locals_k[2 * j + part].wait()
        came(2 * j + part, other.at[j])
        add(held.at[j], other.at[j], (0, BLK_DEV))

    locals_q[0].wait()
    go(8, ownq.at[0, pl.ds(0, 2)], relq.at[0], near["yr"])
    go(9, ownq.at[0, pl.ds(2, 2)], relq.at[1], near["yl"])
    locals_q[1].wait()
    go(10, ownq.at[1, pl.ds(2, 2)], finq.at[0, pl.ds(2, 2)], near["yr"])
    locals_q[2].wait()
    go(11, ownq.at[2, pl.ds(0, 2)], finq.at[1, pl.ds(0, 2)], near["yl"])

    merge(0, 0)
    go(14, ownk.at[0], relk, near["zr"])
    merge(0, 1)
    go(15, ownv.at[0], relv, near["zl"])
    merge(1, 1)
    go(16, ownv.at[1], finv.at[0], near["zr"])
    merge(2, 0)
    go(17, ownk.at[2], fink.at[1], near["zl"])

    for copy in locals_f:
        copy.wait()

    def f_copy(send_at, recv_at, src, dst, target):
        return pltpu.make_async_remote_copy(
            src_ref=src, dst_ref=dst, send_sem=send.at[send_at], recv_sem=recv.at[recv_at],
            device_id=target, device_id_type=MESH,
        )

    to_sib = f_copy(20, 20, fown, frecv.at[0], near["sib"])
    steps = [
        ((c == 0) & ((y == 2) | (y == 1)), f_copy(21, 21, fsend.at[0], frecv.at[1], near["yl"])),
        ((c == 0) & (y == 3), f_copy(22, 22, fsend.at[0], frecv.at[2], near["yr"])),
        ((c == 0) & (y == 0) & ((z == 2) | (z == 1)), f_copy(23, 23, fsend.at[1], frecv.at[3], near["zl"])),
        ((c == 0) & (y == 0) & (z == 3), f_copy(24, 24, fsend.at[1], frecv.at[4], near["zr"])),
    ]
    gets = [
        (c == 0) & ((y == 1) | (y == 0)),
        (c == 0) & (y == 0),
        (c == 0) & (y == 0) & ((z == 1) | (z == 0)),
        (c == 0) & (y == 0) & (z == 0),
    ]

    def f_take(at):
        fsum[...] += frecv[at].astype(jnp.float32)

    @pl.when(c == 1)
    def _():
        to_sib.start()

    @pl.when(c == 0)
    def _():
        to_sib.wait_recv()
        fsum[...] = fown[...].astype(jnp.float32) + frecv[0].astype(jnp.float32)

    for step in range(2):
        @pl.when(gets[step])
        def _(step=step):
            steps[step][1].wait_recv()
            f_take(1 + step)

    @pl.when((c == 0) & (y > 0))
    def _():
        fsend[0] = fsum[...].astype(jnp.bfloat16)

    for step in range(2):
        @pl.when(steps[step][0])
        def _(step=step):
            steps[step][1].start()

    merge(1, 0)
    came(14, relk)
    add(ownk.at[1], relk, (0, BLK_DEV))
    go(18, ownk.at[1], fink.at[0], near["zr"])
    merge(2, 1)
    came(15, relv)
    add(ownv.at[2], relv, (0, BLK_DEV))
    go(19, ownv.at[2], finv.at[1], near["zl"])

    came(8, relq.at[0])
    add(ownq.at[1], relq.at[0], (0, 2))
    go(12, ownq.at[1, pl.ds(0, 2)], finq.at[0, pl.ds(0, 2)], near["yr"])
    came(9, relq.at[1])

    def add_high(block, carry):
        ownq[2, block + 2] = (
            ownq[2, block + 2].astype(jnp.float32) + relq[1, block].astype(jnp.float32)
        ).astype(jnp.bfloat16)
        return carry

    lax.fori_loop(0, 2, add_high, 0)
    go(13, ownq.at[2, pl.ds(2, 2)], finq.at[1, pl.ds(2, 2)], near["yl"])

    for step in (2, 3):
        @pl.when(gets[step])
        def _(step=step):
            steps[step][1].wait_recv()
            f_take(1 + step)

    @pl.when((c == 0) & (y == 0) & (z > 0))
    def _():
        fsend[1] = fsum[...].astype(jnp.bfloat16)

    for step in (2, 3):
        @pl.when(steps[step][0])
        def _(step=step):
            steps[step][1].start()

    locals_q[3].wait()
    came(10, finq.at[0, pl.ds(2, 2)])
    came(11, finq.at[1, pl.ds(0, 2)])
    came(12, finq.at[0, pl.ds(0, 2)])
    came(13, finq.at[1, pl.ds(2, 2)])

    def total(held, parts_in, out):
        def one(block, carry):
            value = held[block].astype(jnp.float32)
            for ref in parts_in:
                value += ref[block].astype(jnp.float32)
            out[block] = value.astype(jnp.bfloat16)
            return carry

        return one

    lax.fori_loop(0, BLK_DEV, total(ownq.at[3], (finq.at[0], finq.at[1]), out_q), 0)

    root = (z == 0) & (y == 0) & (c == 0)
    for part, (held, other, fin, out) in enumerate(
        ((ownk, sibk, fink, out_k), (ownv, sibv, finv, out_v))
    ):
        locals_k[6 + part].wait()
        came(6 + part, other.at[3])
        came((18, 16)[part], fin.at[0])
        came((17, 19)[part], fin.at[1])
        ins = (other.at[3], fin.at[0], fin.at[1])
        lax.fori_loop(1, BLK_DEV, total(held.at[3], ins, out), 0)
        value = held[3, 0].astype(jnp.float32)
        for ref in ins:
            value += ref[0].astype(jnp.float32)

        @pl.when(root)
        def _(value=value, out=out, part=part):
            out[0] = (value + fsum[part]).astype(jnp.bfloat16)

        @pl.when(jnp.logical_not(root))
        def _(value=value, out=out):
            out[0] = value.astype(jnp.bfloat16)

    for copy in started:
        copy.wait_send()

    @pl.when(c == 1)
    def _():
        to_sib.wait_send()

    for condition, copy in steps:
        @pl.when(condition)
        def _(copy=copy):
            copy.wait_send()


def body(query, keys, values, output, d_out, row_logsum, selected):
    bf16, f32 = jnp.bfloat16, jnp.float32
    any_spec = pl.BlockSpec(memory_space=pl.ANY)
    vmem_spec = pl.BlockSpec(memory_space=pltpu.VMEM)
    smem_spec = pl.BlockSpec(memory_space=pltpu.SMEM)
    blocked = (BLK_DEV, BLOCK, WIDTH)
    shape = jax.ShapeDtypeStruct
    dma, vmem, smem = pltpu.SemaphoreType.DMA, pltpu.VMEM, pltpu.SMEM
    kg, vg, qg, gg, sg = pl.pallas_call(
        gather_kernel,
        out_shape=[
            shape((NSLOT, BLOCK, WIDTH), bf16),
            shape((NSLOT, BLOCK, WIDTH), bf16),
            shape((16, BLOCK, WIDTH), bf16),
            shape((16, BLOCK, WIDTH), bf16),
            shape((16, 8, BLOCK), f32),
        ],
        in_specs=[any_spec] * 5 + [vmem_spec],
        out_specs=[any_spec] * 5,
        scratch_shapes=[
            vmem(blocked, bf16),
            vmem(blocked, bf16),
            vmem((BLK_DEV, 8, BLOCK), f32),
            dma((38,)),
            dma((28,)),
            dma((9,)),
        ],
        compiler_params=pltpu.CompilerParams(
            collective_id=0, has_side_effects=True, vmem_limit_bytes=32 * MIB
        ),
        name="gather",
    )(
        keys.reshape(blocked), values.reshape(blocked), query.reshape(blocked),
        d_out, output.reshape(blocked), row_logsum,
    )
    pk, pv, pq = pl.pallas_call(
        pair_kernel,
        out_shape=[
            shape((NSLOT, BLOCK, WIDTH), bf16),
            shape((NSLOT, BLOCK, WIDTH), bf16),
            shape((16, BLOCK, WIDTH), bf16),
        ],
        in_specs=[smem_spec] + [any_spec] * 4 + [vmem_spec],
        out_specs=[any_spec] * 3,
        scratch_shapes=[
            smem((NSLOT * 4,), jnp.int32),
            smem((NSLOT * 4 + 1,), jnp.int32),
            vmem((2, BLOCK, WIDTH), bf16),
            vmem((2, BLOCK, WIDTH), bf16),
            vmem((2, BLOCK, WIDTH), bf16),
            vmem((2, BLOCK, WIDTH), bf16),
            vmem((16, BLOCK, WIDTH), f32),
            vmem((BLOCK, WIDTH), f32),
            vmem((BLOCK, WIDTH), f32),
            vmem((BLOCK, WIDTH), bf16),
            vmem((BLOCK, WIDTH), bf16),
            vmem((16, BLOCK, WIDTH), bf16),
            vmem((BLOCK, WIDTH), bf16),
            dma((2, 4)),
            dma((2,)),
            dma((16,)),
            dma((NSLOT, 2)),
        ],
        compiler_params=pltpu.CompilerParams(vmem_limit_bytes=48 * MIB),
        name="pairs",
    )(selected.reshape(-1), kg, vg, qg, gg, sg)
    out_q, out_k, out_v = pl.pallas_call(
        scatter_kernel,
        out_shape=[shape(blocked, bf16)] * 3,
        in_specs=[any_spec] * 3,
        out_specs=[vmem_spec] * 3,
        scratch_shapes=[
            vmem((4,) + blocked, bf16),
            vmem((4,) + blocked, bf16),
            vmem((4,) + blocked, bf16),
            vmem((4,) + blocked, bf16),
            vmem(blocked, bf16),
            vmem(blocked, bf16),
            vmem((2,) + blocked, bf16),
            vmem((2,) + blocked, bf16),
            vmem((4,) + blocked, bf16),
            vmem((2, 2, BLOCK, WIDTH), bf16),
            vmem((2,) + blocked, bf16),
            vmem((2, BLOCK, WIDTH), bf16),
            vmem((5, 2, BLOCK, WIDTH), bf16),
            vmem((2, BLOCK, WIDTH), f32),
            vmem((2, 2, BLOCK, WIDTH), bf16),
            dma((25,)),
            dma((25,)),
            dma((14,)),
        ],
        compiler_params=pltpu.CompilerParams(
            collective_id=1, has_side_effects=True, vmem_limit_bytes=56 * MIB
        ),
        name="scatter",
    )(pk, pv, pq)
    flat = (BLK_DEV * BLOCK, WIDTH)
    return out_q.reshape(flat), out_k.reshape(flat), out_v.reshape(flat)


def solution(mesh):
    in_specs = (
        P("seq", "head"),
        P("seq", "head"),
        P("seq", "head"),
        P("seq", "head"),
        P(("seq", "head"), None),
        P("head", "seq"),
        P(),
    )
    out_specs = (P("seq", "head"), P("seq", "head"), P("seq", "head"))
    return jax.shard_map(body, mesh=mesh, in_specs=in_specs, out_specs=out_specs, check_vma=False)
```

```python
import functools
import math

import jax
import jax.numpy as jnp
from jax import lax
from jax.experimental import pallas as pl
from jax.experimental.pallas import tpu as pltpu
from jax.sharding import PartitionSpec as P

MESH = pl.DeviceIdType.MESH
BLOCK = 512
HD = 128
WIDTH = 256
BLK_DEV = 4
RING = 4
NSLOT = 33
FIRST = 32
LOG2E = math.log2(math.e)
VMEM = 60 * 1024 * 1024


def place():
    seq = lax.axis_index("seq")
    return lax.div(seq, 8), lax.rem(lax.div(seq, 2), 4), lax.rem(seq, 2), lax.axis_index("head")


def device(z, y, c, x):
    return ((z * 4 + y) * 2 + c, x)


def after(index, step):
    return lax.rem(index + step, RING)


def neighbours(z, y, c, x):
    return {
        "sib": device(z, y, 1 - c, x),
        "zr": device(after(z, 1), y, c, x),
        "zl": device(after(z, 3), y, c, x),
        "yr": device(z, after(y, 1), c, x),
        "yl": device(z, after(y, 3), c, x),
    }


def greet(devices):
    barrier = pltpu.get_barrier_semaphore()
    for target in devices:
        pl.semaphore_signal(barrier, inc=1, device_id=target, device_id_type=MESH)
    pl.semaphore_wait(barrier, len(devices))


NT = (((1,), (1,)), ((), ()))
NN = (((1,), (0,)), ((), ()))
TN = (((0,), (0,)), ((), ()))


def dot(a, b, dims):
    return lax.dot_general(a, b, dims, preferred_element_type=jnp.float32)


def gather_kernel(
    keys, values, query, d_out, output, logsum,
    kg, vg, qg, gg, sg, own_q, own_k, own_v,
    grad, outv, kv, vv, qv, stats, accq, acck, accv, send, recv, local,
):
    z, y, c, x = place()
    near = neighbours(z, y, c, x)
    others = [((z * 4 + y) * 2 + c, after(x, step)) for step in (1, 2, 3)]
    greet(list(near.values()) + others)
    started = []

    def remote(index, src, dst, target):
        return pltpu.make_async_remote_copy(
            src_ref=src, dst_ref=dst, send_sem=send.at[index], recv_sem=recv.at[index],
            device_id=target, device_id_type=MESH,
        )

    def go(index, src, dst, target):
        copy = remote(index, src, dst, target)
        copy.start()
        started.append(copy)
        return copy

    def column(z_at, c_at):
        return pl.ds((z_at * 2 + c_at) * BLK_DEV, BLK_DEV)

    def row(y_at):
        return pl.ds(y_at * BLK_DEV, BLK_DEV)

    zl, zr, zo = after(z, 3), after(z, 1), after(z, 2)
    yl, yr = after(y, 3), after(y, 1)
    top = (z == 0) & (y == 0)
    root = top & (c == 0)

    first_own = [
        pltpu.make_async_copy(keys.at[0], kg.at[FIRST], local.at[0]),
        pltpu.make_async_copy(values.at[0], vg.at[FIRST], local.at[1]),
    ]

    def first_copy(ref, send_at, recv_at, target):
        return pltpu.make_async_remote_copy(
            src_ref=ref.at[FIRST], dst_ref=ref.at[FIRST],
            send_sem=send.at[send_at], recv_sem=recv.at[recv_at],
            device_id=target, device_id_type=MESH,
        )

    first_sends = []
    for core, ref in enumerate((kg, vg)):
        mine = c == core
        first_sends += [
            (mine & (z == 0) & (y <= 1), first_copy(ref, 28, 26, near["yr"])),
            (mine & (z == 0) & (y == 0), first_copy(ref, 29, 26, near["yl"])),
            (mine & (z <= 1), first_copy(ref, 30, 26, near["zr"])),
            (mine & (z == 0), first_copy(ref, 31, 26, near["zl"])),
            (mine & jnp.logical_not(top & (c == 1)), first_copy(ref, 32, 27, near["sib"])),
        ]
    first_start = first_copy(vg, 33, 26, near["sib"])

    def send_first():
        for condition, copy in first_sends:
            @pl.when(condition)
            def _(copy=copy):
                copy.start()

    @pl.when(root)
    def _():
        for copy in first_own:
            copy.start()
        for copy in first_own:
            copy.wait()
        first_start.start()
        send_first()

    @pl.when(top & (c == 1))
    def _():
        first_start.wait_recv()
        send_first()

    for step in (1, 2, 3):
        to = after(x, step)
        go(
            22 + step,
            d_out.at[:, pl.ds(pl.multiple_of(to * WIDTH, WIDTH), WIDTH)],
            grad.at[x],
            others[step - 1],
        )
    to_vmem = [
        pltpu.make_async_copy(
            d_out.at[:, pl.ds(pl.multiple_of(x * WIDTH, WIDTH), WIDTH)], grad.at[x], local.at[2]
        ),
        pltpu.make_async_copy(output, outv, local.at[3]),
        pltpu.make_async_copy(keys, kv, local.at[4]),
        pltpu.make_async_copy(values, vv, local.at[5]),
        pltpu.make_async_copy(query, qv, local.at[6]),
    ]
    kept = [
        pltpu.make_async_copy(keys, kg.at[column(z, c)], local.at[7]),
        pltpu.make_async_copy(values, vg.at[column(z, c)], local.at[8]),
        pltpu.make_async_copy(query, qg.at[row(y)], local.at[9]),
    ]
    for copy in to_vmem + kept:
        copy.start()

    own = column(z, c)
    go(0, keys, kg.at[own], near["zr"])
    go(1, values, vg.at[own], near["zl"])
    go(14, query, qg.at[row(y)], near["yr"])
    go(15, query, qg.at[row(y)], near["yl"])
    go(4, keys, kg.at[own], near["sib"])
    go(5, values, vg.at[own], near["sib"])

    to_vmem[0].wait()
    to_vmem[1].wait()
    for step in (1, 2, 3):
        remote(22 + step, grad.at[x], grad.at[x], others[step - 1]).wait_recv()
    go(16, grad, gg.at[row(y)], near["yl"])
    go(17, grad, gg.at[row(y)], near["yr"])
    go(2, values, vg.at[own], near["zr"])
    go(3, keys, kg.at[own], near["zl"])
    kept.append(pltpu.make_async_copy(grad, gg.at[row(y)], local.at[10]))
    kept[-1].start()
    stats[...] = jnp.zeros_like(stats)

    ones = jnp.ones((8, HD), jnp.bfloat16)
    for block in range(BLK_DEV):
        for head in range(2):
            part = pl.ds(head * HD, HD)
            product = grad[block, :, part].astype(jnp.float32) * outv[block, :, part].astype(jnp.float32)
            high = product.astype(jnp.bfloat16)
            low = (product - high.astype(jnp.float32)).astype(jnp.bfloat16)
            total = dot(ones, high, NT) + dot(ones, low, NT)
            stats[block, pl.ds(2 + head, 1), :] = total[0:1]
            stats[block, pl.ds(head, 1), :] = (
                logsum[pl.ds(head, 1), pl.ds(block * BLOCK, BLOCK)] * LOG2E
            )
    go(18, stats, sg.at[row(y)], near["yr"])
    go(19, stats, sg.at[row(y)], near["yl"])
    kept.append(pltpu.make_async_copy(stats, sg.at[row(y)], local.at[11]))
    kept[-1].start()

    @pl.when(jnp.logical_not(top))
    def _():
        first_copy(kg, 28, 26, near["sib"]).wait_recv()
        send_first()

    for copy in to_vmem[2:]:
        copy.wait()
    scale = 1.0 / math.sqrt(HD)

    def own_block(block, carry):
        for head in range(2):
            part = pl.ds(head * HD, HD)
            k, v, q, g = kv[block, :, part], vv[block, :, part], qv[block, :, part], grad[block, :, part]
            lse = stats[block, pl.ds(head, 1), :]
            delta = stats[block, pl.ds(2 + head, 1), :]
            p = jnp.exp2(dot(k, q, NT) * (scale * LOG2E) - lse)
            key_at = lax.broadcasted_iota(jnp.int32, (BLOCK, BLOCK), 0)
            query_at = lax.broadcasted_iota(jnp.int32, (BLOCK, BLOCK), 1)
            p = jnp.where(key_at <= query_at, p, 0.0)
            ds = (p * (dot(v, g, NT) - delta)).astype(jnp.bfloat16)
            accv[block, :, part] = dot(p.astype(jnp.bfloat16), g, NN)
            acck[block, :, part] = dot(ds, q, NN) * scale
            accq[block, :, part] = dot(ds, k, TN) * scale
        return carry

    lax.fori_loop(0, BLK_DEV, own_block, 0)
    for index, (src, dst) in enumerate(((accq, own_q), (acck, own_k), (accv, own_v))):
        kept.append(pltpu.make_async_copy(src, dst, local.at[12 + index]))
        kept[-1].start()

    def arrived(index, ref, piece, source):
        remote(index, ref.at[piece], ref.at[piece], source).wait_recv()

    def forward(index, ref, piece, target):
        go(index, ref.at[piece], ref.at[piece], target)

    left_k, right_k, far_k = column(zl, c), column(zr, c), column(zo, c)
    arrived(0, kg, left_k, near["zl"])
    forward(6, kg, left_k, near["zr"])
    arrived(1, vg, right_k, near["zr"])
    forward(7, vg, right_k, near["zl"])
    arrived(14, qg, row(yl), near["yl"])
    forward(20, qg, row(yl), near["yr"])
    arrived(18, sg, row(yl), near["yl"])
    forward(22, sg, row(yl), near["yr"])
    arrived(16, gg, row(yr), near["yr"])
    forward(21, gg, row(yr), near["yl"])
    forward(8, kg, left_k, near["sib"])
    forward(9, vg, right_k, near["sib"])
    arrived(2, vg, left_k, near["zl"])
    forward(10, vg, left_k, near["sib"])
    arrived(3, kg, right_k, near["zr"])
    forward(11, kg, right_k, near["sib"])
    arrived(6, kg, far_k, near["zl"])
    forward(12, kg, far_k, near["sib"])
    arrived(7, vg, far_k, near["zr"])
    forward(13, vg, far_k, near["sib"])
    arrived(15, qg, row(yr), near["yr"])
    arrived(17, gg, row(yl), near["yl"])
    arrived(19, sg, row(yr), near["yr"])
    arrived(20, qg, row(after(y, 2)), near["yl"])
    arrived(21, gg, row(after(y, 2)), near["yr"])
    arrived(22, sg, row(after(y, 2)), near["yl"])

    @pl.when(jnp.logical_not(root))
    def _():
        first_copy(kg, 32, 27, near["sib"]).wait_recv()

    for index, ref, z_at in (
        (4, kg, z), (5, vg, z), (8, kg, zl), (9, vg, zr),
        (10, vg, zl), (11, kg, zr), (12, kg, zo), (13, vg, zo),
    ):
        arrived(index, ref, column(z_at, 1 - c), near["sib"])
    for copy in kept:
        copy.wait()
    for copy in started:
        copy.wait_send()

    @pl.when(root)
    def _():
        first_start.wait_send()

    for condition, copy in first_sends:
        @pl.when(condition)
        def _(copy=copy):
            copy.wait_send()


def pair_kernel(
    selected, kg, vg, qg, gg, sg,
    pk, pv, pq,
    table, items, kbuf, vbuf, qbuf, gbuf, dq, dk, dv, kout, vout, qout, zero,
    in_sem, out_sem, q_sem, zero_sem,
):
    z, y, c, _ = place()
    scale = 1.0 / math.sqrt(HD)

    def clear(at, carry):
        table[at] = 0
        return carry

    lax.fori_loop(0, NSLOT * 4, clear, 0)
    for yq in range(4):
        def enter(at, carry, yq=yq):
            block = lax.div(at, 3)
            chosen = selected[(((z * 4 + yq) * 2 + c) * BLK_DEV + block) * 3 + lax.rem(at, 3)]
            owner = lax.div(chosen, BLK_DEV)
            here = (chosen > 0) & (lax.rem(lax.div(owner, 2), 4) == y)
            slot = (lax.div(owner, 8) * 2 + lax.rem(owner, 2)) * BLK_DEV + lax.rem(chosen, BLK_DEV)

            @pl.when(here)
            def _():
                table[slot * 4 + yq] = 1 + yq * BLK_DEV + block
            return carry

        lax.fori_loop(0, BLK_DEV * 3, enter, 0)
    for block in range(BLK_DEV):
        later = ((z * 4 + y) * 2 + c) * BLK_DEV + block > 0
        table[FIRST * 4 + block] = jnp.where(later, 1 + y * BLK_DEV + block, 0)

    def compact(at, count):
        entry = table[at]
        items[count] = at * 128 + entry
        return count + jnp.where(entry > 0, 1, 0)

    count = lax.fori_loop(0, NSLOT * 4, compact, 0)
    items[count] = -1

    zero[...] = jnp.zeros_like(zero)

    def idle(slot):
        return (
            table[slot * 4] + table[slot * 4 + 1] + table[slot * 4 + 2] + table[slot * 4 + 3]
        ) == 0

    def blank(slot):
        return [
            pltpu.make_async_copy(zero, ref.at[slot], zero_sem.at[slot, part])
            for part, ref in enumerate((pk, pv))
        ]

    def start_blank(slot, carry):
        @pl.when(idle(slot))
        def _():
            for copy in blank(slot):
                copy.start()
        return carry

    lax.fori_loop(0, NSLOT, start_blank, 0)

    def decode(item):
        slot = lax.div(item, 512)
        entry = lax.rem(item, 128) - 1
        return slot, entry

    def loads(at):
        slot, block = decode(items[at])
        side = lax.rem(at, 2)
        return [
            pltpu.make_async_copy(kg.at[slot], kbuf.at[side], in_sem.at[side, 0]),
            pltpu.make_async_copy(vg.at[slot], vbuf.at[side], in_sem.at[side, 1]),
            pltpu.make_async_copy(qg.at[block], qbuf.at[side], in_sem.at[side, 2]),
            pltpu.make_async_copy(gg.at[block], gbuf.at[side], in_sem.at[side, 3]),
        ]

    @pl.when(count > 0)
    def _():
        for copy in loads(0):
            copy.start()

    dq[...] = jnp.zeros_like(dq)

    def work(side, block):
        for head in range(2):
            part = pl.ds(head * HD, HD)
            k, v = kbuf[side, :, part], vbuf[side, :, part]
            q, g = qbuf[side, :, part], gbuf[side, :, part]
            lse = sg[block, pl.ds(head, 1), :]
            delta = sg[block, pl.ds(2 + head, 1), :]
            p = jnp.exp2(dot(k, q, NT) * (scale * LOG2E) - lse)
            ds = (p * (dot(v, g, NT) - delta)).astype(jnp.bfloat16)
            dv[:, part] += dot(p.astype(jnp.bfloat16), g, NN)
            dk[:, part] += dot(ds, q, NN)
            dq[block, :, part] += dot(ds, k, TN)

    outs = [
        pltpu.make_async_copy(kout, pk.at[0], out_sem.at[0]),
        pltpu.make_async_copy(vout, pv.at[0], out_sem.at[1]),
    ]

    def item_step(at, carry):
        opened, written = carry
        slot, block = decode(items[at])
        following = items[at + 1]
        side = lax.rem(at, 2)

        @pl.when(following >= 0)
        def _():
            for copy in loads(at + 1):
                copy.start()

        for copy in loads(at):
            copy.wait()

        @pl.when(slot != opened)
        def _():
            dk[...] = jnp.zeros_like(dk)
            dv[...] = jnp.zeros_like(dv)

        work(side, block)
        closing = (following < 0) | (lax.div(following, 512) != slot)

        @pl.when(closing)
        def _():
            @pl.when(written > 0)
            def _():
                for copy in outs:
                    copy.wait()
            kout[...] = (dk[...] * scale).astype(jnp.bfloat16)
            vout[...] = dv[...].astype(jnp.bfloat16)
            pltpu.make_async_copy(kout, pk.at[slot], out_sem.at[0]).start()
            pltpu.make_async_copy(vout, pv.at[slot], out_sem.at[1]).start()

        return slot, written + jnp.where(closing, 1, 0)

    lax.fori_loop(0, count, item_step, (-1, 0))

    def finish(block, carry):
        qout[block] = (dq[block] * scale).astype(jnp.bfloat16)
        pltpu.make_async_copy(qout.at[block], pq.at[block], q_sem.at[block]).start()
        return carry

    lax.fori_loop(0, 16, finish, 0)

    @pl.when(count > 0)
    def _():
        for copy in outs:
            copy.wait()

    def drain(block, carry):
        pltpu.make_async_copy(qout.at[block], pq.at[block], q_sem.at[block]).wait()
        return carry

    lax.fori_loop(0, 16, drain, 0)

    def wait_blank(slot, carry):
        @pl.when(idle(slot))
        def _():
            for copy in blank(slot):
                copy.wait()
        return carry

    lax.fori_loop(0, NSLOT, wait_blank, 0)


def scatter_kernel(
    pk, pv, pq, own_q, own_k, own_v,
    out_q, out_k, out_v,
    ownk, ownv, sibk, sibv, relk, relv, fink, finv,
    ownq, relq, finq, accq, acck, accv, fown, frecv, fsum, fsend,
    send, recv, local,
):
    z, y, c, x = place()
    near = neighbours(z, y, c, x)
    greet(list(near.values()))
    started = []

    def remote(index, src, dst, target):
        return pltpu.make_async_remote_copy(
            src_ref=src, dst_ref=dst, send_sem=send.at[index], recv_sem=recv.at[index],
            device_id=target, device_id_type=MESH,
        )

    def go(index, src, dst, target):
        copy = remote(index, src, dst, target)
        copy.start()
        started.append(copy)

    def came(index, dst):
        remote(index, dst, dst, near["sib"]).wait_recv()

    def column(z_at, c_at):
        return pl.ds((z_at * 2 + c_at) * BLK_DEV, BLK_DEV)

    def local_copy(index, src, dst):
        copy = pltpu.make_async_copy(src, dst, local.at[index])
        copy.start()
        return copy

    hops = (2, 1, 3, 0)
    parts = ((pk, ownk, sibk), (pv, ownv, sibv))
    locals_k = []
    for j, hop in enumerate(hops):
        for part, (ref, held, other) in enumerate(parts):
            go(2 * j + part, ref.at[column(after(z, hop), 1 - c)], other.at[j], near["sib"])
            locals_k.append(local_copy(2 * j + part, ref.at[column(after(z, hop), c)], held.at[j]))
        if j == 0:
            for core, (mine, theirs) in enumerate(((pk, pv), (pv, pk))):
                @pl.when(c == core)
                def _(mine=mine, theirs=theirs):
                    remote(20, theirs.at[FIRST], frecv.at[0], near["sib"]).start()
                    pltpu.make_async_copy(mine.at[FIRST], fown, local.at[8]).start()
    locals_q = [
        local_copy(9 + j, pq.at[pl.ds(after(y, hop) * BLK_DEV, BLK_DEV)], ownq.at[j])
        for j, hop in enumerate(hops)
    ]
    locals_own = [
        local_copy(13 + j, src, dst)
        for j, (src, dst) in enumerate(((own_q, accq), (own_k, acck), (own_v, accv)))
    ]

    def add(dst, src, blocks=BLK_DEV):
        def one(block, carry):
            dst[block] = (dst[block].astype(jnp.float32) + src[block].astype(jnp.float32)).astype(
                jnp.bfloat16
            )
            return carry

        lax.fori_loop(0, blocks, one, 0)

    def merge(j, part):
        _, held, other = parts[part]
        locals_k[2 * j + part].wait()
        came(2 * j + part, other.at[j])
        add(held.at[j], other.at[j])

    merge(0, 0)
    go(14, ownk.at[0], relk, near["zr"])
    merge(0, 1)
    go(15, ownv.at[0], relv, near["zl"])

    def f_copy(index, src, dst, target):
        return remote(index, src, dst, target)

    f_sends = [
        ((y == 2) | (y == 1), f_copy(21, fsend.at[0], frecv.at[1], near["yl"])),
        (y == 3, f_copy(22, fsend.at[0], frecv.at[2], near["yr"])),
        ((y == 0) & ((z == 2) | (z == 1)), f_copy(23, fsend.at[1], frecv.at[3], near["zl"])),
        ((y == 0) & (z == 3), f_copy(24, fsend.at[1], frecv.at[4], near["zr"])),
    ]

    def f_take(at):
        came(20 + at, frecv.at[at])
        fsum[...] += frecv[at].astype(jnp.float32)

    def f_send(at):
        condition, copy = f_sends[at]

        @pl.when(condition)
        def _():
            fsend[at // 2] = fsum[...].astype(jnp.bfloat16)
            copy.start()

    pltpu.make_async_copy(pk.at[FIRST], fown, local.at[8]).wait()
    came(20, frecv.at[0])
    fsum[...] = fown[...].astype(jnp.float32) + frecv[0].astype(jnp.float32)

    @pl.when(y == 1)
    def _():
        f_take(1)

    f_send(0)
    f_send(1)

    locals_q[0].wait()
    go(8, ownq.at[0, pl.ds(0, 2)], relq.at[0], near["yr"])
    go(9, ownq.at[0, pl.ds(2, 2)], relq.at[1], near["yl"])
    merge(1, 1)
    go(16, ownv.at[1], finv.at[0], near["zr"])
    merge(2, 0)
    go(17, ownk.at[2], fink.at[1], near["zl"])
    locals_q[1].wait()
    go(10, ownq.at[1, pl.ds(2, 2)], finq.at[0, pl.ds(2, 2)], near["yr"])
    locals_q[2].wait()
    go(11, ownq.at[2, pl.ds(0, 2)], finq.at[1, pl.ds(0, 2)], near["yl"])

    @pl.when(y == 0)
    def _():
        f_take(1)
        f_take(2)

        @pl.when(z == 1)
        def _():
            f_take(3)

    f_send(2)
    f_send(3)

    merge(1, 0)
    merge(2, 1)
    merge(3, 0)
    merge(3, 1)
    came(8, relq.at[0])
    add(ownq.at[1], relq.at[0], 2)
    go(12, ownq.at[1, pl.ds(0, 2)], finq.at[0, pl.ds(0, 2)], near["yr"])
    came(9, relq.at[1])
    add(ownq.at[2, pl.ds(2, 2)], relq.at[1], 2)
    go(13, ownq.at[2, pl.ds(2, 2)], finq.at[1, pl.ds(2, 2)], near["yl"])
    came(14, relk)
    add(ownk.at[1], relk)
    go(18, ownk.at[1], fink.at[0], near["zr"])
    came(15, relv)
    add(ownv.at[2], relv)
    go(19, ownv.at[2], finv.at[1], near["zl"])

    top = (z == 0) & (y == 0)

    @pl.when(top)
    def _():
        f_take(3)
        f_take(4)

    def total(acc, parts_in, out):
        def one(block, carry):
            value = acc[block]
            for ref in parts_in:
                value += ref[block].astype(jnp.float32)
            out[block] = value.astype(jnp.bfloat16)
            return carry

        lax.fori_loop(0, BLK_DEV, one, 0)

    locals_q[3].wait()
    for copy in locals_own:
        copy.wait()

    @pl.when(top & (c == 1))
    def _():
        fsend[1] = fsum[...].astype(jnp.bfloat16)
        remote(25, fsend.at[1], frecv.at[5], near["sib"]).start()

    @pl.when(top & (c == 0))
    def _():
        came(25, frecv.at[5])
        acck[0] += fsum[...]
        accv[0] += frecv[5].astype(jnp.float32)

    came(10, finq.at[0, pl.ds(2, 2)])
    came(11, finq.at[1, pl.ds(0, 2)])
    came(12, finq.at[0, pl.ds(0, 2)])
    came(13, finq.at[1, pl.ds(2, 2)])
    total(accq, (ownq.at[3], finq.at[0], finq.at[1]), out_q)
    came(17, fink.at[1])
    came(16, finv.at[0])
    came(18, fink.at[0])
    total(acck, (ownk.at[3], fink.at[0], fink.at[1]), out_k)
    came(19, finv.at[1])
    total(accv, (ownv.at[3], finv.at[0], finv.at[1]), out_v)

    for copy in started:
        copy.wait_send()
    remote(20, fown, frecv.at[0], near["sib"]).wait_send()
    for condition, copy in f_sends + [
        (top & (c == 1), remote(25, fsend.at[1], frecv.at[5], near["sib"]))
    ]:
        @pl.when(condition)
        def _(copy=copy):
            copy.wait_send()


def body(query, keys, values, output, d_out, row_logsum, selected):
    bf16, f32 = jnp.bfloat16, jnp.float32
    any_spec = pl.BlockSpec(memory_space=pl.ANY)
    vmem_spec = pl.BlockSpec(memory_space=pltpu.VMEM)
    smem_spec = pl.BlockSpec(memory_space=pltpu.SMEM)
    blocked = (BLK_DEV, BLOCK, WIDTH)
    shape = jax.ShapeDtypeStruct
    dma, vmem, smem = pltpu.SemaphoreType.DMA, pltpu.VMEM, pltpu.SMEM
    kg, vg, qg, gg, sg, own_q, own_k, own_v = pl.pallas_call(
        gather_kernel,
        out_shape=[
            shape((NSLOT, BLOCK, WIDTH), bf16),
            shape((NSLOT, BLOCK, WIDTH), bf16),
            shape((16, BLOCK, WIDTH), bf16),
            shape((16, BLOCK, WIDTH), bf16),
            shape((16, 8, BLOCK), f32),
            shape(blocked, f32),
            shape(blocked, f32),
            shape(blocked, f32),
        ],
        in_specs=[any_spec] * 5 + [vmem_spec],
        out_specs=[any_spec] * 8,
        scratch_shapes=[
            vmem(blocked, bf16),
            vmem(blocked, bf16),
            vmem(blocked, bf16),
            vmem(blocked, bf16),
            vmem(blocked, bf16),
            vmem((BLK_DEV, 8, BLOCK), f32),
            vmem(blocked, f32),
            vmem(blocked, f32),
            vmem(blocked, f32),
            dma((34,)),
            dma((28,)),
            dma((15,)),
        ],
        compiler_params=pltpu.CompilerParams(
            collective_id=0, has_side_effects=True, vmem_limit_bytes=VMEM
        ),
        name="gather",
    )(
        keys.reshape(blocked), values.reshape(blocked), query.reshape(blocked),
        d_out, output.reshape(blocked), row_logsum,
    )
    pk, pv, pq = pl.pallas_call(
        pair_kernel,
        out_shape=[
            shape((NSLOT, BLOCK, WIDTH), bf16),
            shape((NSLOT, BLOCK, WIDTH), bf16),
            shape((16, BLOCK, WIDTH), bf16),
        ],
        in_specs=[smem_spec] + [any_spec] * 4 + [vmem_spec],
        out_specs=[any_spec] * 3,
        scratch_shapes=[
            smem((NSLOT * 4,), jnp.int32),
            smem((NSLOT * 4 + 1,), jnp.int32),
            vmem((2, BLOCK, WIDTH), bf16),
            vmem((2, BLOCK, WIDTH), bf16),
            vmem((2, BLOCK, WIDTH), bf16),
            vmem((2, BLOCK, WIDTH), bf16),
            vmem((16, BLOCK, WIDTH), f32),
            vmem((BLOCK, WIDTH), f32),
            vmem((BLOCK, WIDTH), f32),
            vmem((BLOCK, WIDTH), bf16),
            vmem((BLOCK, WIDTH), bf16),
            vmem((16, BLOCK, WIDTH), bf16),
            vmem((BLOCK, WIDTH), bf16),
            dma((2, 4)),
            dma((2,)),
            dma((16,)),
            dma((NSLOT, 2)),
        ],
        compiler_params=pltpu.CompilerParams(vmem_limit_bytes=VMEM),
        name="pairs",
    )(selected.reshape(-1), kg, vg, qg, gg, sg)
    out_q, out_k, out_v = pl.pallas_call(
        scatter_kernel,
        out_shape=[shape(blocked, bf16)] * 3,
        in_specs=[any_spec] * 6,
        out_specs=[vmem_spec] * 3,
        scratch_shapes=[
            vmem((4,) + blocked, bf16),
            vmem((4,) + blocked, bf16),
            vmem((4,) + blocked, bf16),
            vmem((4,) + blocked, bf16),
            vmem(blocked, bf16),
            vmem(blocked, bf16),
            vmem((2,) + blocked, bf16),
            vmem((2,) + blocked, bf16),
            vmem((4,) + blocked, bf16),
            vmem((2, 2, BLOCK, WIDTH), bf16),
            vmem((2,) + blocked, bf16),
            vmem(blocked, f32),
            vmem(blocked, f32),
            vmem(blocked, f32),
            vmem((BLOCK, WIDTH), bf16),
            vmem((6, BLOCK, WIDTH), bf16),
            vmem((BLOCK, WIDTH), f32),
            vmem((2, BLOCK, WIDTH), bf16),
            dma((26,)),
            dma((26,)),
            dma((16,)),
        ],
        compiler_params=pltpu.CompilerParams(
            collective_id=1, has_side_effects=True, vmem_limit_bytes=VMEM
        ),
        name="scatter",
    )(pk, pv, pq, own_q, own_k, own_v)
    flat = (BLK_DEV * BLOCK, WIDTH)
    return out_q.reshape(flat), out_k.reshape(flat), out_v.reshape(flat)


def solution(mesh):
    in_specs = (
        P("seq", "head"),
        P("seq", "head"),
        P("seq", "head"),
        P("seq", "head"),
        P(("seq", "head"), None),
        P("head", "seq"),
        P(),
    )
    out_specs = (P("seq", "head"), P("seq", "head"), P("seq", "head"))
    return jax.shard_map(body, mesh=mesh, in_specs=in_specs, out_specs=out_specs, check_vma=False)
```

```python
import functools
import math

import jax
import jax.numpy as jnp
from jax import lax
from jax.experimental import pallas as pl
from jax.experimental.pallas import tpu as pltpu
from jax.sharding import PartitionSpec as P

MESH = pl.DeviceIdType.MESH
BLOCK = 512
HD = 128
WIDTH = 256
BLK_DEV = 4
RING = 4
NSLOT = 32
LOG2E = math.log2(math.e)
VMEM = 60 * 1024 * 1024


def place():
    seq = lax.axis_index("seq")
    return lax.div(seq, 8), lax.rem(lax.div(seq, 2), 4), lax.rem(seq, 2), lax.axis_index("head")


def device(z, y, c, x):
    return ((z * 4 + y) * 2 + c, x)


def after(index, step):
    return lax.rem(index + step, RING)


def neighbours(z, y, c, x):
    return {
        "sib": device(z, y, 1 - c, x),
        "zr": device(after(z, 1), y, c, x),
        "zl": device(after(z, 3), y, c, x),
        "yr": device(z, after(y, 1), c, x),
        "yl": device(z, after(y, 3), c, x),
    }


def greet(devices):
    barrier = pltpu.get_barrier_semaphore()
    for target in devices:
        pl.semaphore_signal(barrier, inc=1, device_id=target, device_id_type=MESH)
    pl.semaphore_wait(barrier, len(devices))


NT = (((1,), (1,)), ((), ()))
NN = (((1,), (0,)), ((), ()))
TN = (((0,), (0,)), ((), ()))


def dot(a, b, dims):
    return lax.dot_general(a, b, dims, preferred_element_type=jnp.float32)


def gather_kernel(
    keys, values, query, d_out, output, logsum,
    kg, vg, qg, gg, sg, own_q, own_k, own_v, own_f,
    grad, outv, kv, vv, qv, stats, accq, acck, accv, fblk, accf, fout, send, recv, local,
):
    z, y, c, x = place()
    near = neighbours(z, y, c, x)
    others = [((z * 4 + y) * 2 + c, after(x, step)) for step in (1, 2, 3)]
    greet(list(near.values()) + others)
    started = []

    def remote(index, src, dst, target, chunk=0):
        return pltpu.make_async_remote_copy(
            src_ref=src, dst_ref=dst,
            send_sem=send.at[index, chunk], recv_sem=recv.at[index, chunk],
            device_id=target, device_id_type=MESH,
        )

    def go(index, src, dst, target, chunk=0):
        copy = remote(index, src, dst, target, chunk)
        copy.start()
        started.append(copy)

    def spread(index, src, dst, piece, target):
        for chunk in range(BLK_DEV):
            go(index, src.at[chunk], dst.at[piece + chunk], target, chunk)

    def arrived(index, ref, piece):
        for chunk in range(BLK_DEV):
            at = ref.at[piece + chunk]
            remote(index, at, at, near["sib"], chunk).wait_recv()

    def relay(came, ref, piece, *onward):
        for chunk in range(BLK_DEV):
            at = ref.at[piece + chunk]
            remote(came, at, at, near["sib"], chunk).wait_recv()
            for index, target in onward:
                go(index, at, at, target, chunk)

    def column(z_at, c_at):
        return (z_at * 2 + c_at) * BLK_DEV

    def row(y_at):
        return y_at * BLK_DEV

    def four(start):
        return pl.ds(start, BLK_DEV)

    zl, zr, zo = after(z, 3), after(z, 1), after(z, 2)
    yl, yr = after(y, 3), after(y, 1)
    top = (z == 0) & (y == 0)
    root = top & (c == 0)

    first_own = [
        pltpu.make_async_copy(keys.at[0], fblk.at[0], local.at[0]),
        pltpu.make_async_copy(values.at[0], fblk.at[1], local.at[1]),
    ]

    def first_copy(part, send_at, recv_at, target):
        return pltpu.make_async_remote_copy(
            src_ref=fblk.at[part], dst_ref=fblk.at[part],
            send_sem=send.at[send_at, 0], recv_sem=recv.at[recv_at, 0],
            device_id=target, device_id_type=MESH,
        )

    first_sends = [
        ((z == 0) & (y <= 1), first_copy(c, 28, 26, near["yr"])),
        ((z == 0) & (y == 0), first_copy(c, 29, 26, near["yl"])),
        (z <= 1, first_copy(c, 30, 26, near["zr"])),
        (z == 0, first_copy(c, 31, 26, near["zl"])),
        (jnp.logical_not(top & (c == 1)), first_copy(c, 32, 27, near["sib"])),
    ]
    first_start = first_copy(1, 33, 26, near["sib"])

    def send_first():
        for condition, copy in first_sends:
            @pl.when(condition)
            def _(copy=copy):
                copy.start()

    def pass_first(condition):
        @pl.when(condition)
        def _():
            first_copy(c, 28, 26, near["sib"]).wait_recv()
            send_first()

    @pl.when(root)
    def _():
        for copy in first_own:
            copy.start()
        for copy in first_own:
            copy.wait()
        first_start.start()
        send_first()

    pass_first(top & (c == 1))

    for step in (1, 2, 3):
        to = after(x, step)
        go(
            22 + step,
            d_out.at[:, pl.ds(pl.multiple_of(to * WIDTH, WIDTH), WIDTH)],
            grad.at[x],
            others[step - 1],
        )
    to_vmem = [
        pltpu.make_async_copy(
            d_out.at[:, pl.ds(pl.multiple_of(x * WIDTH, WIDTH), WIDTH)], grad.at[x], local.at[2]
        ),
        pltpu.make_async_copy(output, outv, local.at[3]),
        pltpu.make_async_copy(keys, kv, local.at[4]),
        pltpu.make_async_copy(values, vv, local.at[5]),
        pltpu.make_async_copy(query, qv, local.at[6]),
    ]
    kept = []
    for copy in to_vmem:
        copy.start()

    own = column(z, c)
    spread(0, keys, kg, own, near["zr"])
    spread(1, values, vg, own, near["zl"])
    spread(14, query, qg, row(y), near["yr"])
    spread(15, query, qg, row(y), near["yl"])
    spread(2, values, vg, own, near["zr"])
    spread(3, keys, kg, own, near["zl"])
    spread(4, keys, kg, own, near["sib"])
    spread(5, values, vg, own, near["sib"])

    pass_first((z == 0) & ((y == 1) | (y == 3)))
    to_vmem[0].wait()
    to_vmem[1].wait()
    for step in (1, 2, 3):
        remote(22 + step, grad.at[x], grad.at[x], others[step - 1]).wait_recv()
    spread(16, grad, gg, row(y), near["yl"])
    spread(17, grad, gg, row(y), near["yr"])
    kept.append(pltpu.make_async_copy(grad, gg.at[four(row(y))], local.at[10]))
    kept[-1].start()
    pass_first((z == 0) & (y == 2))
    stats[...] = jnp.zeros_like(stats)

    ones = jnp.ones((8, HD), jnp.bfloat16)
    for block in range(BLK_DEV):
        for head in range(2):
            part = pl.ds(head * HD, HD)
            product = grad[block, :, part].astype(jnp.float32) * outv[block, :, part].astype(jnp.float32)
            high = product.astype(jnp.bfloat16)
            low = (product - high.astype(jnp.float32)).astype(jnp.bfloat16)
            total = dot(ones, high, NT) + dot(ones, low, NT)
            stats[block, pl.ds(2 + head, 1), :] = total[0:1]
            stats[block, pl.ds(head, 1), :] = (
                logsum[pl.ds(head, 1), pl.ds(block * BLOCK, BLOCK)] * LOG2E
            )
    go(18, stats, sg.at[four(row(y))], near["yr"])
    go(19, stats, sg.at[four(row(y))], near["yl"])
    kept.append(pltpu.make_async_copy(stats, sg.at[four(row(y))], local.at[11]))
    kept[-1].start()

    for copy in to_vmem[2:]:
        copy.wait()
    for index, (src, dst) in enumerate(
        ((kv, kg.at[four(own)]), (vv, vg.at[four(own)]), (qv, qg.at[four(row(y))]))
    ):
        kept.append(pltpu.make_async_copy(src, dst, local.at[7 + index]))
        kept[-1].start()
    scale = 1.0 / math.sqrt(HD)

    def own_block(block, carry):
        for head in range(2):
            part = pl.ds(head * HD, HD)
            k, v, q, g = kv[block, :, part], vv[block, :, part], qv[block, :, part], grad[block, :, part]
            lse = stats[block, pl.ds(head, 1), :]
            delta = stats[block, pl.ds(2 + head, 1), :]
            p = jnp.exp2(dot(k, q, NT) * (scale * LOG2E) - lse)
            key_at = lax.broadcasted_iota(jnp.int32, (BLOCK, BLOCK), 0)
            query_at = lax.broadcasted_iota(jnp.int32, (BLOCK, BLOCK), 1)
            p = jnp.where(key_at <= query_at, p, 0.0)
            ds = (p * (dot(v, g, NT) - delta)).astype(jnp.bfloat16)
            accv[block, :, part] = dot(p.astype(jnp.bfloat16), g, NN)
            acck[block, :, part] = dot(ds, q, NN) * scale
            accq[block, :, part] = dot(ds, k, TN) * scale
        return carry

    def first_block(block, carry):
        for head in range(2):
            part = pl.ds(head * HD, HD)
            k, v, q, g = fblk[0, :, part], fblk[1, :, part], qv[block, :, part], grad[block, :, part]
            lse = stats[block, pl.ds(head, 1), :]
            delta = stats[block, pl.ds(2 + head, 1), :]
            p = jnp.exp2(dot(k, q, NT) * (scale * LOG2E) - lse)
            ds = (p * (dot(v, g, NT) - delta)).astype(jnp.bfloat16)
            accf[1, :, part] += dot(p.astype(jnp.bfloat16), g, NN)
            accf[0, :, part] += dot(ds, q, NN) * scale
            accq[block, :, part] += dot(ds, k, TN) * scale
        return carry

    lax.fori_loop(0, BLK_DEV, own_block, 0)
    for index, (src, dst) in enumerate(((acck, own_k), (accv, own_v))):
        kept.append(pltpu.make_async_copy(src, dst, local.at[12 + index]))
        kept[-1].start()
    pass_first((z == 1) | (z == 3))

    left_k, right_k, far_k = column(zl, c), column(zr, c), column(zo, c)
    relay(0, kg, left_k, (6, near["zr"]), (8, near["sib"]))
    relay(1, vg, right_k, (7, near["zl"]), (9, near["sib"]))
    relay(14, qg, row(yl), (20, near["yr"]))
    stats_in = [sg.at[four(row(after(y, step)))] for step in (3, 1, 2)]
    remote(18, stats_in[0], stats_in[0], near["yl"]).wait_recv()
    go(22, stats_in[0], stats_in[0], near["yr"])
    relay(16, gg, row(yr), (21, near["yl"]))
    pass_first(z == 2)

    @pl.when(jnp.logical_not(root))
    def _():
        first_copy(1 - c, 32, 27, near["sib"]).wait_recv()

    accf[...] = jnp.zeros_like(accf)
    lax.fori_loop(jnp.where(root, 1, 0), BLK_DEV, first_block, 0)
    fout[...] = accf[...].astype(jnp.bfloat16)
    for index, (src, dst) in enumerate(((accq, own_q), (fout, own_f))):
        kept.append(pltpu.make_async_copy(src, dst, local.at[14 + index]))
        kept[-1].start()
    relay(2, vg, left_k, (10, near["sib"]))
    relay(3, kg, right_k, (11, near["sib"]))
    relay(6, kg, far_k, (12, near["sib"]))
    relay(7, vg, far_k, (13, near["sib"]))
    arrived(15, qg, row(yr))
    arrived(17, gg, row(yl))
    arrived(20, qg, row(after(y, 2)))
    arrived(21, gg, row(after(y, 2)))
    remote(19, stats_in[1], stats_in[1], near["yr"]).wait_recv()
    remote(22, stats_in[2], stats_in[2], near["yl"]).wait_recv()
    for index, ref, z_at in (
        (4, kg, z), (5, vg, z), (8, kg, zl), (9, vg, zr),
        (10, vg, zl), (11, kg, zr), (12, kg, zo), (13, vg, zo),
    ):
        arrived(index, ref, column(z_at, 1 - c))
    for copy in kept:
        copy.wait()
    for copy in started:
        copy.wait_send()

    @pl.when(root)
    def _():
        first_start.wait_send()

    for condition, copy in first_sends:
        @pl.when(condition)
        def _(copy=copy):
            copy.wait_send()


def pair_kernel(
    selected, kg, vg, qg, gg, sg,
    pk, pv, pq,
    table, items, kbuf, vbuf, qbuf, gbuf, dq, dk, dv, kout, vout, qout, zero,
    in_sem, out_sem, q_sem, zero_sem,
):
    z, y, c, _ = place()
    scale = 1.0 / math.sqrt(HD)

    for at in range(NSLOT * 4):
        table[at] = 0
    for yq in range(4):
        for at in range(BLK_DEV * 3):
            block = at // 3
            chosen = selected[(((z * 4 + yq) * 2 + c) * BLK_DEV + block) * 3 + at % 3]
            owner = lax.div(chosen, BLK_DEV)
            here = (chosen > 0) & (lax.rem(lax.div(owner, 2), 4) == y)
            slot = (lax.div(owner, 8) * 2 + lax.rem(owner, 2)) * BLK_DEV + lax.rem(chosen, BLK_DEV)
            table[jnp.where(here, slot * 4 + yq, NSLOT * 4)] = 1 + yq * BLK_DEV + block
    count = 0
    for at in range(NSLOT * 4):
        entry = table[at]
        items[count] = at * 128 + entry
        count = count + jnp.where(entry > 0, 1, 0)
    items[count] = -1

    zero[...] = jnp.zeros_like(zero)

    def idle(slot):
        return (
            table[slot * 4] + table[slot * 4 + 1] + table[slot * 4 + 2] + table[slot * 4 + 3]
        ) == 0

    def blank(slot):
        return [
            pltpu.make_async_copy(zero, ref.at[slot], zero_sem.at[slot, part])
            for part, ref in enumerate((pk, pv))
        ]

    def start_blank(slot, carry):
        @pl.when(idle(slot))
        def _():
            for copy in blank(slot):
                copy.start()
        return carry

    lax.fori_loop(0, NSLOT, start_blank, 0)

    def decode(item):
        slot = lax.div(item, 512)
        entry = lax.rem(item, 128) - 1
        return slot, entry

    def loads(at):
        slot, block = decode(items[at])
        side = lax.rem(at, 2)
        return [
            pltpu.make_async_copy(kg.at[slot], kbuf.at[side], in_sem.at[side, 0]),
            pltpu.make_async_copy(vg.at[slot], vbuf.at[side], in_sem.at[side, 1]),
            pltpu.make_async_copy(qg.at[block], qbuf.at[side], in_sem.at[side, 2]),
            pltpu.make_async_copy(gg.at[block], gbuf.at[side], in_sem.at[side, 3]),
        ]

    @pl.when(count > 0)
    def _():
        for copy in loads(0):
            copy.start()

    dq[...] = jnp.zeros_like(dq)

    def work(side, block):
        for head in range(2):
            part = pl.ds(head * HD, HD)
            k, v = kbuf[side, :, part], vbuf[side, :, part]
            q, g = qbuf[side, :, part], gbuf[side, :, part]
            lse = sg[block, pl.ds(head, 1), :]
            delta = sg[block, pl.ds(2 + head, 1), :]
            p = jnp.exp2(dot(k, q, NT) * (scale * LOG2E) - lse)
            ds = (p * (dot(v, g, NT) - delta)).astype(jnp.bfloat16)
            dv[:, part] += dot(p.astype(jnp.bfloat16), g, NN)
            dk[:, part] += dot(ds, q, NN)
            dq[block, :, part] += dot(ds, k, TN)

    outs = [
        pltpu.make_async_copy(kout, pk.at[0], out_sem.at[0]),
        pltpu.make_async_copy(vout, pv.at[0], out_sem.at[1]),
    ]

    def item_step(at, carry):
        opened, written = carry
        slot, block = decode(items[at])
        following = items[at + 1]
        side = lax.rem(at, 2)

        @pl.when(following >= 0)
        def _():
            for copy in loads(at + 1):
                copy.start()

        for copy in loads(at):
            copy.wait()

        @pl.when(slot != opened)
        def _():
            dk[...] = jnp.zeros_like(dk)
            dv[...] = jnp.zeros_like(dv)

        work(side, block)
        closing = (following < 0) | (lax.div(following, 512) != slot)

        @pl.when(closing)
        def _():
            @pl.when(written > 0)
            def _():
                for copy in outs:
                    copy.wait()
            kout[...] = (dk[...] * scale).astype(jnp.bfloat16)
            vout[...] = dv[...].astype(jnp.bfloat16)
            pltpu.make_async_copy(kout, pk.at[slot], out_sem.at[0]).start()
            pltpu.make_async_copy(vout, pv.at[slot], out_sem.at[1]).start()

        return slot, written + jnp.where(closing, 1, 0)

    lax.fori_loop(0, count, item_step, (-1, 0))

    def finish(block, carry):
        qout[block] = (dq[block] * scale).astype(jnp.bfloat16)
        pltpu.make_async_copy(qout.at[block], pq.at[block], q_sem.at[block]).start()
        return carry

    lax.fori_loop(0, 16, finish, 0)

    @pl.when(count > 0)
    def _():
        for copy in outs:
            copy.wait()

    def drain(block, carry):
        pltpu.make_async_copy(qout.at[block], pq.at[block], q_sem.at[block]).wait()
        return carry

    lax.fori_loop(0, 16, drain, 0)

    def wait_blank(slot, carry):
        @pl.when(idle(slot))
        def _():
            for copy in blank(slot):
                copy.wait()
        return carry

    lax.fori_loop(0, NSLOT, wait_blank, 0)


def scatter_kernel(
    pk, pv, pq, own_q, own_k, own_v, own_f,
    out_q, out_k, out_v,
    ownk, ownv, sibk, sibv, relk, relv, fink, finv,
    ownq, relq, finq, accq, acck, accv, fown, frecv, fsum, fsend,
    send, recv, local,
):
    z, y, c, x = place()
    near = neighbours(z, y, c, x)
    greet(list(near.values()))
    started = []

    def remote(index, src, dst, target):
        return pltpu.make_async_remote_copy(
            src_ref=src, dst_ref=dst, send_sem=send.at[index], recv_sem=recv.at[index],
            device_id=target, device_id_type=MESH,
        )

    def go(index, src, dst, target):
        copy = remote(index, src, dst, target)
        copy.start()
        started.append(copy)

    def came(index, dst):
        remote(index, dst, dst, near["sib"]).wait_recv()

    def column(z_at, c_at):
        return pl.ds((z_at * 2 + c_at) * BLK_DEV, BLK_DEV)

    def local_copy(index, src, dst):
        copy = pltpu.make_async_copy(src, dst, local.at[index])
        copy.start()
        return copy

    hops = (2, 1, 3, 0)
    parts = ((pk, ownk, sibk), (pv, ownv, sibv))
    locals_k = []
    for j, hop in enumerate(hops):
        for part, (ref, held, other) in enumerate(parts):
            go(2 * j + part, ref.at[column(after(z, hop), 1 - c)], other.at[j], near["sib"])
            locals_k.append(local_copy(2 * j + part, ref.at[column(after(z, hop), c)], held.at[j]))
        if j == 0:
            remote(20, own_f.at[1 - c], frecv.at[0], near["sib"]).start()
            mine_f = local_copy(8, own_f.at[c], fown)
    locals_q = [
        local_copy(9 + j, pq.at[pl.ds(after(y, hop) * BLK_DEV, BLK_DEV)], ownq.at[j])
        for j, hop in enumerate(hops)
    ]
    locals_own = [
        local_copy(13 + j, src, dst)
        for j, (src, dst) in enumerate(((own_q, accq), (own_k, acck), (own_v, accv)))
    ]

    def add(dst, src, blocks=BLK_DEV):
        def one(block, carry):
            dst[block] = (dst[block].astype(jnp.float32) + src[block].astype(jnp.float32)).astype(
                jnp.bfloat16
            )
            return carry

        lax.fori_loop(0, blocks, one, 0)

    def merge(j, part):
        _, held, other = parts[part]
        locals_k[2 * j + part].wait()
        came(2 * j + part, other.at[j])
        add(held.at[j], other.at[j])

    merge(0, 0)
    go(14, ownk.at[0], relk, near["zr"])
    merge(0, 1)
    go(15, ownv.at[0], relv, near["zl"])

    def f_copy(index, src, dst, target):
        return remote(index, src, dst, target)

    f_sends = [
        ((y == 2) | (y == 1), f_copy(21, fsend.at[0], frecv.at[1], near["yl"])),
        (y == 3, f_copy(22, fsend.at[0], frecv.at[2], near["yr"])),
        ((y == 0) & ((z == 2) | (z == 1)), f_copy(23, fsend.at[1], frecv.at[3], near["zl"])),
        ((y == 0) & (z == 3), f_copy(24, fsend.at[1], frecv.at[4], near["zr"])),
    ]

    def f_take(at):
        came(20 + at, frecv.at[at])
        fsum[...] += frecv[at].astype(jnp.float32)

    def f_send(at):
        condition, copy = f_sends[at]

        @pl.when(condition)
        def _():
            fsend[at // 2] = fsum[...].astype(jnp.bfloat16)
            copy.start()

    mine_f.wait()
    came(20, frecv.at[0])
    fsum[...] = fown[...].astype(jnp.float32) + frecv[0].astype(jnp.float32)

    @pl.when(y == 1)
    def _():
        f_take(1)

    f_send(0)
    f_send(1)

    locals_q[0].wait()
    go(8, ownq.at[0, pl.ds(0, 2)], relq.at[0], near["yr"])
    go(9, ownq.at[0, pl.ds(2, 2)], relq.at[1], near["yl"])
    merge(1, 1)
    go(16, ownv.at[1], finv.at[0], near["zr"])
    merge(2, 0)
    go(17, ownk.at[2], fink.at[1], near["zl"])
    locals_q[1].wait()
    go(10, ownq.at[1, pl.ds(2, 2)], finq.at[0, pl.ds(2, 2)], near["yr"])
    locals_q[2].wait()
    go(11, ownq.at[2, pl.ds(0, 2)], finq.at[1, pl.ds(0, 2)], near["yl"])

    @pl.when(y == 0)
    def _():
        f_take(1)
        f_take(2)

        @pl.when(z == 1)
        def _():
            f_take(3)

    f_send(2)
    f_send(3)

    merge(1, 0)
    merge(2, 1)
    merge(3, 0)
    merge(3, 1)
    came(8, relq.at[0])
    add(ownq.at[1], relq.at[0], 2)
    go(12, ownq.at[1, pl.ds(0, 2)], finq.at[0, pl.ds(0, 2)], near["yr"])
    came(9, relq.at[1])
    add(ownq.at[2, pl.ds(2, 2)], relq.at[1], 2)
    go(13, ownq.at[2, pl.ds(2, 2)], finq.at[1, pl.ds(2, 2)], near["yl"])
    came(14, relk)
    add(ownk.at[1], relk)
    go(18, ownk.at[1], fink.at[0], near["zr"])
    came(15, relv)
    add(ownv.at[2], relv)
    go(19, ownv.at[2], finv.at[1], near["zl"])

    top = (z == 0) & (y == 0)

    @pl.when(top)
    def _():
        f_take(3)
        f_take(4)

    def total(acc, parts_in, out):
        def one(block, carry):
            value = acc[block]
            for ref in parts_in:
                value += ref[block].astype(jnp.float32)
            out[block] = value.astype(jnp.bfloat16)
            return carry

        lax.fori_loop(0, BLK_DEV, one, 0)

    locals_q[3].wait()
    for copy in locals_own:
        copy.wait()

    @pl.when(top & (c == 1))
    def _():
        fsend[1] = fsum[...].astype(jnp.bfloat16)
        remote(25, fsend.at[1], frecv.at[5], near["sib"]).start()

    @pl.when(top & (c == 0))
    def _():
        came(25, frecv.at[5])
        acck[0] += fsum[...]
        accv[0] += frecv[5].astype(jnp.float32)

    came(10, finq.at[0, pl.ds(2, 2)])
    came(11, finq.at[1, pl.ds(0, 2)])
    came(12, finq.at[0, pl.ds(0, 2)])
    came(13, finq.at[1, pl.ds(2, 2)])
    total(accq, (ownq.at[3], finq.at[0], finq.at[1]), out_q)
    came(17, fink.at[1])
    came(16, finv.at[0])
    came(18, fink.at[0])
    total(acck, (ownk.at[3], fink.at[0], fink.at[1]), out_k)
    came(19, finv.at[1])
    total(accv, (ownv.at[3], finv.at[0], finv.at[1]), out_v)

    for copy in started:
        copy.wait_send()
    remote(20, fown, frecv.at[0], near["sib"]).wait_send()
    for condition, copy in f_sends + [
        (top & (c == 1), remote(25, fsend.at[1], frecv.at[5], near["sib"]))
    ]:
        @pl.when(condition)
        def _(copy=copy):
            copy.wait_send()


def body(query, keys, values, output, d_out, row_logsum, selected):
    bf16, f32 = jnp.bfloat16, jnp.float32
    any_spec = pl.BlockSpec(memory_space=pl.ANY)
    vmem_spec = pl.BlockSpec(memory_space=pltpu.VMEM)
    smem_spec = pl.BlockSpec(memory_space=pltpu.SMEM)
    blocked = (BLK_DEV, BLOCK, WIDTH)
    shape = jax.ShapeDtypeStruct
    dma, vmem, smem = pltpu.SemaphoreType.DMA, pltpu.VMEM, pltpu.SMEM
    kg, vg, qg, gg, sg, own_q, own_k, own_v, own_f = pl.pallas_call(
        gather_kernel,
        out_shape=[
            shape((NSLOT, BLOCK, WIDTH), bf16),
            shape((NSLOT, BLOCK, WIDTH), bf16),
            shape((16, BLOCK, WIDTH), bf16),
            shape((16, BLOCK, WIDTH), bf16),
            shape((16, 8, BLOCK), f32),
            shape(blocked, f32),
            shape(blocked, f32),
            shape(blocked, f32),
            shape((2, BLOCK, WIDTH), bf16),
        ],
        in_specs=[any_spec] * 5 + [vmem_spec],
        out_specs=[any_spec] * 9,
        scratch_shapes=[
            vmem(blocked, bf16),
            vmem(blocked, bf16),
            vmem(blocked, bf16),
            vmem(blocked, bf16),
            vmem(blocked, bf16),
            vmem((BLK_DEV, 8, BLOCK), f32),
            vmem(blocked, f32),
            vmem(blocked, f32),
            vmem(blocked, f32),
            vmem((2, BLOCK, WIDTH), bf16),
            vmem((2, BLOCK, WIDTH), f32),
            vmem((2, BLOCK, WIDTH), bf16),
            dma((34, BLK_DEV)),
            dma((28, BLK_DEV)),
            dma((16,)),
        ],
        compiler_params=pltpu.CompilerParams(
            collective_id=0, has_side_effects=True, vmem_limit_bytes=VMEM
        ),
        name="gather",
    )(
        keys.reshape(blocked), values.reshape(blocked), query.reshape(blocked),
        d_out, output.reshape(blocked), row_logsum,
    )
    pk, pv, pq = pl.pallas_call(
        pair_kernel,
        out_shape=[
            shape((NSLOT, BLOCK, WIDTH), bf16),
            shape((NSLOT, BLOCK, WIDTH), bf16),
            shape((16, BLOCK, WIDTH), bf16),
        ],
        in_specs=[smem_spec] + [any_spec] * 4 + [vmem_spec],
        out_specs=[any_spec] * 3,
        scratch_shapes=[
            smem((NSLOT * 4 + 1,), jnp.int32),
            smem((NSLOT * 4 + 1,), jnp.int32),
            vmem((2, BLOCK, WIDTH), bf16),
            vmem((2, BLOCK, WIDTH), bf16),
            vmem((2, BLOCK, WIDTH), bf16),
            vmem((2, BLOCK, WIDTH), bf16),
            vmem((16, BLOCK, WIDTH), f32),
            vmem((BLOCK, WIDTH), f32),
            vmem((BLOCK, WIDTH), f32),
            vmem((BLOCK, WIDTH), bf16),
            vmem((BLOCK, WIDTH), bf16),
            vmem((16, BLOCK, WIDTH), bf16),
            vmem((BLOCK, WIDTH), bf16),
            dma((2, 4)),
            dma((2,)),
            dma((16,)),
            dma((NSLOT, 2)),
        ],
        compiler_params=pltpu.CompilerParams(vmem_limit_bytes=VMEM),
        name="pairs",
    )(selected.reshape(-1), kg, vg, qg, gg, sg)
    out_q, out_k, out_v = pl.pallas_call(
        scatter_kernel,
        out_shape=[shape(blocked, bf16)] * 3,
        in_specs=[any_spec] * 7,
        out_specs=[vmem_spec] * 3,
        scratch_shapes=[
            vmem((4,) + blocked, bf16),
            vmem((4,) + blocked, bf16),
            vmem((4,) + blocked, bf16),
            vmem((4,) + blocked, bf16),
            vmem(blocked, bf16),
            vmem(blocked, bf16),
            vmem((2,) + blocked, bf16),
            vmem((2,) + blocked, bf16),
            vmem((4,) + blocked, bf16),
            vmem((2, 2, BLOCK, WIDTH), bf16),
            vmem((2,) + blocked, bf16),
            vmem(blocked, f32),
            vmem(blocked, f32),
            vmem(blocked, f32),
            vmem((BLOCK, WIDTH), bf16),
            vmem((6, BLOCK, WIDTH), bf16),
            vmem((BLOCK, WIDTH), f32),
            vmem((2, BLOCK, WIDTH), bf16),
            dma((26,)),
            dma((26,)),
            dma((16,)),
        ],
        compiler_params=pltpu.CompilerParams(
            collective_id=1, has_side_effects=True, vmem_limit_bytes=VMEM
        ),
        name="scatter",
    )(pk, pv, pq, own_q, own_k, own_v, own_f)
    flat = (BLK_DEV * BLOCK, WIDTH)
    return out_q.reshape(flat), out_k.reshape(flat), out_v.reshape(flat)


def solution(mesh):
    in_specs = (
        P("seq", "head"),
        P("seq", "head"),
        P("seq", "head"),
        P("seq", "head"),
        P(("seq", "head"), None),
        P("head", "seq"),
        P(),
    )
    out_specs = (P("seq", "head"), P("seq", "head"), P("seq", "head"))
    return jax.shard_map(body, mesh=mesh, in_specs=in_specs, out_specs=out_specs, check_vma=False)
```

```python
import functools
import math

import jax
import jax.numpy as jnp
from jax import lax
from jax.experimental import pallas as pl
from jax.experimental.pallas import tpu as pltpu
from jax.sharding import PartitionSpec as P

MESH = pl.DeviceIdType.MESH
BLOCK = 512
HD = 128
WIDTH = 256
BLK_DEV = 4
RING = 4
NSLOT = 32
LOG2E = math.log2(math.e)
VMEM = 60 * 1024 * 1024


def place():
    seq = lax.axis_index("seq")
    return lax.div(seq, 8), lax.rem(lax.div(seq, 2), 4), lax.rem(seq, 2), lax.axis_index("head")


def device(z, y, c, x):
    return ((z * 4 + y) * 2 + c, x)


def after(index, step):
    return lax.rem(index + step, RING)


def neighbours(z, y, c, x):
    return {
        "sib": device(z, y, 1 - c, x),
        "zr": device(after(z, 1), y, c, x),
        "zl": device(after(z, 3), y, c, x),
        "yr": device(z, after(y, 1), c, x),
        "yl": device(z, after(y, 3), c, x),
    }


def greet(devices):
    barrier = pltpu.get_barrier_semaphore()
    for target in devices:
        pl.semaphore_signal(barrier, inc=1, device_id=target, device_id_type=MESH)
    pl.semaphore_wait(barrier, len(devices))


NT = (((1,), (1,)), ((), ()))
NN = (((1,), (0,)), ((), ()))
TN = (((0,), (0,)), ((), ()))


def dot(a, b, dims):
    return lax.dot_general(a, b, dims, preferred_element_type=jnp.float32)


def gather_kernel(
    keys, values, query, d_out, output, logsum,
    kz, vz, qz, gz, sz, qy, gy, ky, vy, sy, own_q, own_k, own_v, own_f,
    grad, outv, kv, vv, qv, stats, accq, acck, accv, fblk, accf, fout,
    send, recv, bulk_send, bulk_recv, local,
):
    z, y, c, x = place()
    near = neighbours(z, y, c, x)
    others = [((z * 4 + y) * 2 + c, after(x, step)) for step in (1, 2, 3)]
    greet(list(near.values()) + others)
    started = []

    def remote(index, src, dst, target):
        return pltpu.make_async_remote_copy(
            src_ref=src, dst_ref=dst, send_sem=send.at[index], recv_sem=recv.at[index],
            device_id=target, device_id_type=MESH,
        )

    def go(index, src, dst, target):
        copy = remote(index, src, dst, target)
        copy.start()
        started.append(copy)

    def bulk(array, kind, chunk, src, dst, target):
        return pltpu.make_async_remote_copy(
            src_ref=src, dst_ref=dst,
            send_sem=bulk_send.at[array * 7 + kind, chunk],
            recv_sem=bulk_recv.at[array * 7 + kind, chunk],
            device_id=target, device_id_type=MESH,
        )

    def spread(array, kind, src, head, dst, piece, target):
        for chunk in range(2):
            copy = bulk(
                array, kind, chunk,
                src.at[pl.ds(2 * chunk, 2), :, pl.ds(head * HD, HD)],
                dst.at[pl.ds(piece + 2 * chunk, 2)],
                target,
            )
            copy.start()
            started.append(copy)

    def relay(array, kind, ref, piece, *onward):
        for chunk in range(2):
            at = ref.at[pl.ds(piece + 2 * chunk, 2)]
            bulk(array, kind, chunk, at, at, near["sib"]).wait_recv()
            for kind_on, target in onward:
                copy = bulk(array, kind_on, chunk, at, at, target)
                copy.start()
                started.append(copy)

    def column(z_at, c_at):
        return (z_at * 2 + c_at) * BLK_DEV

    def row(y_at):
        return y_at * BLK_DEV

    def four(start):
        return pl.ds(start, BLK_DEV)

    zl, zr, zo = after(z, 3), after(z, 1), after(z, 2)
    yl, yr = after(y, 3), after(y, 1)
    top = (z == 0) & (y == 0)
    root = top & (c == 0)

    first_own = [
        pltpu.make_async_copy(keys.at[0], fblk.at[0], local.at[0]),
        pltpu.make_async_copy(values.at[0], fblk.at[1], local.at[1]),
    ]

    def first_copy(part, send_at, recv_at, target):
        return pltpu.make_async_remote_copy(
            src_ref=fblk.at[part], dst_ref=fblk.at[part],
            send_sem=send.at[send_at], recv_sem=recv.at[recv_at],
            device_id=target, device_id_type=MESH,
        )

    first_sends = [
        ((z == 0) & (y <= 1), first_copy(c, 28, 26, near["yr"])),
        ((z == 0) & (y == 0), first_copy(c, 29, 26, near["yl"])),
        (z <= 1, first_copy(c, 30, 26, near["zr"])),
        (z == 0, first_copy(c, 31, 26, near["zl"])),
        (jnp.logical_not(top & (c == 1)), first_copy(c, 32, 27, near["sib"])),
    ]
    first_start = first_copy(1, 33, 26, near["sib"])

    def send_first():
        for condition, copy in first_sends:
            @pl.when(condition)
            def _(copy=copy):
                copy.start()

    def pass_first(condition):
        @pl.when(condition)
        def _():
            first_copy(c, 28, 26, near["sib"]).wait_recv()
            send_first()

    @pl.when(root)
    def _():
        for copy in first_own:
            copy.start()
        for copy in first_own:
            copy.wait()
        first_start.start()
        send_first()

    pass_first(top & (c == 1))

    for step in (1, 2, 3):
        to = after(x, step)
        go(
            22 + step,
            d_out.at[:, pl.ds(pl.multiple_of(to * WIDTH, WIDTH), WIDTH)],
            grad.at[x],
            others[step - 1],
        )
    to_vmem = [
        pltpu.make_async_copy(
            d_out.at[:, pl.ds(pl.multiple_of(x * WIDTH, WIDTH), WIDTH)], grad.at[x], local.at[2]
        ),
        pltpu.make_async_copy(output, outv, local.at[3]),
        pltpu.make_async_copy(keys, kv, local.at[4]),
        pltpu.make_async_copy(values, vv, local.at[5]),
        pltpu.make_async_copy(query, qv, local.at[6]),
    ]
    kept = []
    for copy in to_vmem:
        copy.start()

    own_z, own_y = column(z, c), row(y)
    z_set = ((keys, 0, kz, 0), (values, 0, vz, 1), (query, 1, qz, 0), (grad, 1, gz, 1))
    y_set = ((query, 0, qy, 0), (grad, 0, gy, 1), (keys, 1, ky, 0), (values, 1, vy, 1))
    z_ways, y_ways = (near["zr"], near["zl"]), (near["yr"], near["yl"])

    def spread_all(kind, arrays):
        for array in arrays:
            if array < 4:
                src, head, ref, way = z_set[array]
                spread(array, kind, src, head, ref, own_z, z_ways[(way + kind) % 2])
            else:
                src, head, ref, way = y_set[array - 4]
                spread(array, kind, src, head, ref, own_y, y_ways[(way + kind) % 2])

    spread_all(0, (0, 1, 4, 7, 2, 6))
    spread_all(1, (0, 1, 4, 7, 2, 6))
    for array in (0, 1, 2):
        src, head, ref, _ = z_set[array]
        spread(array, 3, src, head, ref, own_z, near["sib"])

    pass_first((z == 0) & ((y == 1) | (y == 3)))
    to_vmem[0].wait()
    to_vmem[1].wait()
    for step in (1, 2, 3):
        remote(22 + step, grad.at[x], grad.at[x], others[step - 1]).wait_recv()
    spread_all(0, (3, 5))
    spread_all(1, (3, 5))
    spread(3, 3, grad, 1, gz, own_z, near["sib"])
    pass_first((z == 0) & (y == 2))
    stats[...] = jnp.zeros_like(stats)

    ones = jnp.ones((8, HD), jnp.bfloat16)
    for block in range(BLK_DEV):
        for head in range(2):
            part = pl.ds(head * HD, HD)
            product = grad[block, :, part].astype(jnp.float32) * outv[block, :, part].astype(jnp.float32)
            high = product.astype(jnp.bfloat16)
            low = (product - high.astype(jnp.float32)).astype(jnp.bfloat16)
            total = dot(ones, high, NT) + dot(ones, low, NT)
            stats[block, pl.ds(2 + head, 1), :] = total[0:1]
            stats[block, pl.ds(head, 1), :] = (
                logsum[pl.ds(head, 1), pl.ds(block * BLOCK, BLOCK)] * LOG2E
            )
    go(18, stats, sy.at[four(own_y)], near["yr"])
    go(19, stats, sy.at[four(own_y)], near["yl"])
    go(34, stats, sz.at[four(own_z)], near["zr"])
    go(35, stats, sz.at[four(own_z)], near["zl"])
    go(36, stats, sz.at[four(own_z)], near["sib"])

    for copy in to_vmem[2:]:
        copy.wait()
    held = {0: kv, 1: vv, 2: qv, 3: grad}
    keep = [(held[(0, 1, 2, 3)[at]], z_set[at][1], z_set[at][2].at[four(own_z)]) for at in range(4)]
    keep += [(held[(2, 3, 0, 1)[at]], y_set[at][1], y_set[at][2].at[four(own_y)]) for at in range(4)]
    keep += [(stats, None, sz.at[four(own_z)]), (stats, None, sy.at[four(own_y)])]
    for index, (src, head, dst) in enumerate(keep):
        part = src if head is None else src.at[:, :, pl.ds(head * HD, HD)]
        kept.append(pltpu.make_async_copy(part, dst, local.at[16 + index]))
        kept[-1].start()
    scale = 1.0 / math.sqrt(HD)

    def own_block(block, carry):
        for head in range(2):
            part = pl.ds(head * HD, HD)
            k, v, q, g = kv[block, :, part], vv[block, :, part], qv[block, :, part], grad[block, :, part]
            lse = stats[block, pl.ds(head, 1), :]
            delta = stats[block, pl.ds(2 + head, 1), :]
            p = jnp.exp2(dot(k, q, NT) * (scale * LOG2E) - lse)
            key_at = lax.broadcasted_iota(jnp.int32, (BLOCK, BLOCK), 0)
            query_at = lax.broadcasted_iota(jnp.int32, (BLOCK, BLOCK), 1)
            p = jnp.where(key_at <= query_at, p, 0.0)
            ds = (p * (dot(v, g, NT) - delta)).astype(jnp.bfloat16)
            accv[block, :, part] = dot(p.astype(jnp.bfloat16), g, NN)
            acck[block, :, part] = dot(ds, q, NN) * scale
            accq[block, :, part] = dot(ds, k, TN) * scale
        return carry

    def first_block(block, carry):
        for head in range(2):
            part = pl.ds(head * HD, HD)
            k, v, q, g = fblk[0, :, part], fblk[1, :, part], qv[block, :, part], grad[block, :, part]
            lse = stats[block, pl.ds(head, 1), :]
            delta = stats[block, pl.ds(2 + head, 1), :]
            p = jnp.exp2(dot(k, q, NT) * (scale * LOG2E) - lse)
            ds = (p * (dot(v, g, NT) - delta)).astype(jnp.bfloat16)
            accf[1, :, part] += dot(p.astype(jnp.bfloat16), g, NN)
            accf[0, :, part] += dot(ds, q, NN) * scale
            accq[block, :, part] += dot(ds, k, TN) * scale
        return carry

    lax.fori_loop(0, BLK_DEV, own_block, 0)
    for index, (src, dst) in enumerate(((acck, own_k), (accv, own_v))):
        kept.append(pltpu.make_async_copy(src, dst, local.at[12 + index]))
        kept[-1].start()
    pass_first((z == 1) | (z == 3))

    def pieces(array):
        if array < 4:
            _, _, ref, way = z_set[array]
            near_at, far_at = (zl, zr) if way == 0 else (zr, zl)
            return ref, [column(at, c) for at in (near_at, far_at, zo)], z_ways[way]
        _, _, ref, way = y_set[array - 4]
        near_at, far_at = (yl, yr) if way == 0 else (yr, yl)
        return ref, [row(at) for at in (near_at, far_at, after(y, 2))], y_ways[way]

    def onward(array, kind):
        ref, at, way = pieces(array)
        sends = [(2, way)] if kind == 0 else []
        if array < 4:
            sends.append((4 + kind, near["sib"]))
        relay(array, kind, ref, at[kind], *sends)

    for array in (0, 1, 4, 7, 2, 6):
        onward(array, 0)
    sy_in = [sy.at[four(row(after(y, step)))] for step in (3, 1, 2)]
    sz_in = [sz.at[four(column(after(z, step), c))] for step in (3, 1, 2)]

    def stat_in(index, ref):
        remote(index, ref, ref, near["sib"]).wait_recv()

    stat_in(18, sy_in[0])
    go(22, sy_in[0], sy_in[0], near["yr"])
    stat_in(34, sz_in[0])
    go(37, sz_in[0], sz_in[0], near["zr"])
    go(38, sz_in[0], sz_in[0], near["sib"])
    for array in (3, 5):
        onward(array, 0)
    pass_first(z == 2)

    @pl.when(jnp.logical_not(root))
    def _():
        first_copy(1 - c, 32, 27, near["sib"]).wait_recv()

    accf[...] = jnp.zeros_like(accf)
    lax.fori_loop(jnp.where(root, 1, 0), BLK_DEV, first_block, 0)
    fout[...] = accf[...].astype(jnp.bfloat16)
    for index, (src, dst) in enumerate(((accq, own_q), (fout, own_f))):
        kept.append(pltpu.make_async_copy(src, dst, local.at[14 + index]))
        kept[-1].start()
    stat_in(35, sz_in[1])
    go(39, sz_in[1], sz_in[1], near["sib"])
    for kind in (1, 2):
        for array in (0, 1, 4, 7, 2, 6, 3, 5):
            onward(array, kind)
    stat_in(37, sz_in[2])
    go(40, sz_in[2], sz_in[2], near["sib"])
    stat_in(19, sy_in[1])
    stat_in(22, sy_in[2])
    for array in range(4):
        ref, _, _ = pieces(array)
        way = z_set[array][3]
        order = (z, zl, zr, zo) if way == 0 else (z, zr, zl, zo)
        for kind, at in enumerate(order):
            relay(array, 3 + kind, ref, column(at, 1 - c))
    for index, at in ((36, z), (38, zl), (39, zr), (40, zo)):
        stat_in(index, sz.at[four(column(at, 1 - c))])
    for copy in kept:
        copy.wait()
    for copy in started:
        copy.wait_send()

    @pl.when(root)
    def _():
        first_start.wait_send()

    for condition, copy in first_sends:
        @pl.when(condition)
        def _(copy=copy):
            copy.wait_send()


def choose(selected, z, y, c, head):
    row_at = lax.broadcasted_iota(jnp.int32, (32, 1), 0)
    group, core, block = row_at >> 3, (row_at >> 2) & 1, row_at & 3
    if head == 0:
        slab = selected[pl.ds(pl.multiple_of(z * 32, 32), 32), :]
    else:
        slab = jnp.concatenate(
            [selected[pl.ds(pl.multiple_of(at * 32 + y * 8, 8), 8), :] for at in range(4)], axis=0
        )
    lane = lax.broadcasted_iota(jnp.int32, (32, 128), 1)
    found = jnp.zeros((32, 128), jnp.int32)
    for pick in range(3):
        chosen = slab[:, pick : pick + 1]
        z_of, y_of, c_of, b_of = chosen >> 5, (chosen >> 3) & 3, (chosen >> 2) & 1, chosen & 3
        if head == 0:
            here = (chosen > 0) & (y_of == y) & (core == c)
            target = ((z_of * 2 + c_of) * 4 + b_of) * 4 + group
            value = 1 + group * 4 + block
        else:
            here = (chosen > 0) & (z_of == z) & (c_of == c)
            target = (y_of * 4 + b_of) * 8 + group * 2 + core
            value = 1 + (group * 2 + core) * 4 + block
        found += jnp.where(here & (lane == target), value, 0)
    table = jnp.sum(found, axis=0, keepdims=True)
    down = lax.broadcasted_iota(jnp.int32, (128, 128), 0)
    across = lax.broadcasted_iota(jnp.int32, (128, 128), 1)
    spread = jnp.broadcast_to(table, (128, 128))
    rank = jnp.sum(jnp.where((across < down) & (spread > 0), 1, 0), axis=1, keepdims=True)
    entry = jnp.sum(jnp.where(across == down, spread, 0), axis=1, keepdims=True)
    item = jnp.where(entry > 0, down[:, 0:1] * 128 + entry, 0)
    items = jnp.sum(jnp.where(rank == across, item, 0), axis=0, keepdims=True)
    return items, table


def pair_kernel(
    selected, kz, vz, qz, gz, qy, gy, ky, vy, sz, sy,
    pz, py,
    lists_v, lists, kbuf, vbuf, qbuf, gbuf, dq0, dq1, dkv, kvout, qout0, qout1, zero,
    list_sem, in_sem, out_sem, q_sem, zero_sem,
):
    z, y, c, _ = place()
    scale = 1.0 / math.sqrt(HD)
    for head in range(2):
        items, table = choose(selected, z, y, c, head)
        lists_v[pl.ds(2 * head, 1), :] = items
        lists_v[pl.ds(2 * head + 1, 1), :] = table
    listed = pltpu.make_async_copy(lists_v, lists, list_sem)
    listed.start()
    zero[...] = jnp.zeros_like(zero)
    listed.wait()

    class Part:
        pass

    parts = []
    for head in range(2):
        part = Part()
        part.head, part.per, part.slots = head, (4, 8)[head], (32, 16)[head]
        part.k, part.v, part.q, part.g = ((kz, vz, qy, gy), (ky, vy, qz, gz))[head]
        part.stat, part.dq, part.qout = ((sy, dq0, qout0), (sz, dq1, qout1))[head]
        part.out, part.at = ((pz, 0), (py, 1))[head]
        part.dq_out, part.dq_at = ((py, 0), (pz, 2))[head]
        parts.append(part)

    def item_of(part, at):
        item = lists[2 * part.head, at]
        return lax.div(item, 128 * part.per), lax.rem(item, 128) - 1, item

    def loads(part, at):
        slot, block, _ = item_of(part, at)
        side = lax.rem(at, 2)
        pairs = ((part.k, kbuf, slot), (part.v, vbuf, slot), (part.q, qbuf, block), (part.g, gbuf, block))
        return [
            pltpu.make_async_copy(
                src.at[where], buf.at[part.head, side], in_sem.at[part.head, side, index]
            )
            for index, (src, buf, where) in enumerate(pairs)
        ]

    for part in parts:
        @pl.when(lists[2 * part.head, 0] > 0)
        def _(part=part):
            for copy in loads(part, 0):
                copy.start()

    def idle(part, slot):
        total = lists[2 * part.head + 1, slot * part.per]
        for at in range(1, part.per):
            total += lists[2 * part.head + 1, slot * part.per + at]
        return total == 0

    def blank(part, slot):
        return pltpu.make_async_copy(
            zero, part.out.at[slot, pl.ds(part.at, 2)], zero_sem.at[part.head, slot]
        )

    def each_idle(part, act):
        def one(slot, carry):
            @pl.when(idle(part, slot))
            def _():
                act(blank(part, slot))
            return carry

        lax.fori_loop(0, part.slots, one, 0)

    for part in parts:
        each_idle(part, lambda copy: copy.start())
        part.dq[...] = jnp.zeros_like(part.dq)

    out = pltpu.make_async_copy(kvout, pz.at[0, pl.ds(0, 2)], out_sem)
    written = 0
    for part in parts:
        def step(state, part=part):
            at, opened, done = state
            slot, block, _ = item_of(part, at)
            next_slot, _, following = item_of(part, at + 1)
            side = lax.rem(at, 2)

            @pl.when(following > 0)
            def _():
                for copy in loads(part, at + 1):
                    copy.start()

            for copy in loads(part, at):
                copy.wait()

            @pl.when(slot != opened)
            def _():
                dkv[...] = jnp.zeros_like(dkv)

            k, v = kbuf[part.head, side], vbuf[part.head, side]
            q, g = qbuf[part.head, side], gbuf[part.head, side]
            lse = part.stat[block, pl.ds(part.head, 1), :]
            delta = part.stat[block, pl.ds(2 + part.head, 1), :]
            p = jnp.exp2(dot(k, q, NT) * (scale * LOG2E) - lse)
            ds = (p * (dot(v, g, NT) - delta)).astype(jnp.bfloat16)
            dkv[1] += dot(p.astype(jnp.bfloat16), g, NN)
            dkv[0] += dot(ds, q, NN)
            part.dq[block] += dot(ds, k, TN)
            closing = (following == 0) | (next_slot != slot)

            @pl.when(closing)
            def _():
                @pl.when(done > 0)
                def _():
                    out.wait()
                kvout[0] = (dkv[0] * scale).astype(jnp.bfloat16)
                kvout[1] = dkv[1].astype(jnp.bfloat16)
                pltpu.make_async_copy(kvout, part.out.at[slot, pl.ds(part.at, 2)], out_sem).start()

            return at + 1, slot, done + jnp.where(closing, 1, 0)

        _, _, written = lax.while_loop(
            lambda state, part=part: lists[2 * part.head, state[0]] > 0,
            step,
            (jnp.int32(0), jnp.int32(-1), jnp.int32(written)),
        )

        def flush(block, part=part):
            return pltpu.make_async_copy(
                part.qout.at[block], part.dq_out.at[block, part.dq_at], q_sem.at[part.head, block]
            )

        def finish(block, carry, part=part, flush=flush):
            part.qout[block] = (part.dq[block] * scale).astype(jnp.bfloat16)
            flush(block).start()
            return carry

        part.flush = flush
        part.blocks = (16, 32)[part.head]
        lax.fori_loop(0, part.blocks, finish, 0)

    @pl.when(written > 0)
    def _():
        out.wait()

    for part in parts:
        def drain(block, carry, part=part):
            part.flush(block).wait()
            return carry

        lax.fori_loop(0, part.blocks, drain, 0)
        each_idle(part, lambda copy: copy.wait())


def scatter_kernel(
    pz, py, own_q, own_k, own_v, own_f,
    out_q, out_k, out_v,
    ownz, sibz, relz, finz, owny, rely, finy, accq, acck, accv,
    fown, frecv, fsum, fsend,
    send, recv, ring_send, ring_recv, local,
):
    z, y, c, x = place()
    near = neighbours(z, y, c, x)
    greet(list(near.values()))
    started = []

    def remote(index, src, dst, target):
        return pltpu.make_async_remote_copy(
            src_ref=src, dst_ref=dst, send_sem=send.at[index], recv_sem=recv.at[index],
            device_id=target, device_id_type=MESH,
        )

    def go(index, src, dst, target):
        copy = remote(index, src, dst, target)
        copy.start()
        started.append(copy)

    def came(index, dst):
        remote(index, dst, dst, near["sib"]).wait_recv()

    def ring_copy(index, src, dst, target):
        return pltpu.make_async_remote_copy(
            src_ref=src, dst_ref=dst, send_sem=ring_send.at[index], recv_sem=ring_recv.at[index],
            device_id=target, device_id_type=MESH,
        )

    def ring_go(index, src, dst, target):
        copy = ring_copy(index, src, dst, target)
        copy.start()
        started.append(copy)

    def ring_came(index, dst):
        ring_copy(index, dst, dst, near["sib"]).wait_recv()

    def column(z_at, c_at):
        return pl.ds((z_at * 2 + c_at) * BLK_DEV, BLK_DEV)

    def local_copy(index, src, dst):
        copy = pltpu.make_async_copy(src, dst, local.at[index])
        copy.start()
        return copy

    hops = (2, 1, 3, 0)
    locals_z, locals_y = [], []
    for j, hop in enumerate(hops):
        go(j, pz.at[column(after(z, hop), 1 - c)], sibz.at[j], near["sib"])
        locals_z.append(local_copy(j, pz.at[column(after(z, hop), c)], ownz.at[j]))
        locals_y.append(
            local_copy(4 + j, py.at[pl.ds(after(y, hop) * BLK_DEV, BLK_DEV)], owny.at[j])
        )
        if j == 0:
            remote(20, own_f.at[1 - c], frecv.at[0], near["sib"]).start()
            mine_f = local_copy(8, own_f.at[c], fown)
    locals_own = [
        local_copy(9 + j, src, dst)
        for j, (src, dst) in enumerate(((own_q, accq), (own_k, acck), (own_v, accv)))
    ]

    def add(dst, src):
        for part in range(3):
            dst[part] = (dst[part].astype(jnp.float32) + src[part].astype(jnp.float32)).astype(
                jnp.bfloat16
            )

    def merge(j):
        locals_z[j].wait()
        came(j, sibz.at[j])

        def one(block, carry):
            add(ownz.at[j, block], sibz.at[j, block])
            return carry

        lax.fori_loop(0, BLK_DEV, one, 0)

    rings = ((0, ownz, relz, finz, near["zr"], near["zl"]), (12, owny, rely, finy, near["yr"], near["yl"]))

    def ring_far(base, own, rel, fin, right, left):
        for block in range(2):
            ring_go(base + block, own.at[0, block], rel.at[0, block], right)
            ring_go(base + 2 + block, own.at[0, 2 + block], rel.at[1, block], left)

    def ring_right(base, own, rel, fin, right, left):
        for block in range(2):
            ring_go(base + 4 + block, own.at[1, 2 + block], fin.at[0, 2 + block], right)

    def ring_left(base, own, rel, fin, right, left):
        for block in range(2):
            ring_go(base + 6 + block, own.at[2, block], fin.at[1, block], left)

    def ring_relay(base, own, rel, fin, right, left):
        for block in range(2):
            ring_came(base + block, rel.at[0, block])
            add(own.at[1, block], rel.at[0, block])
            ring_go(base + 8 + block, own.at[1, block], fin.at[0, block], right)
            ring_came(base + 2 + block, rel.at[1, block])
            add(own.at[2, 2 + block], rel.at[1, block])
            ring_go(base + 10 + block, own.at[2, 2 + block], fin.at[1, 2 + block], left)

    def ring_end(base, own, rel, fin, right, left):
        for block in range(2):
            ring_came(base + 4 + block, fin.at[0, 2 + block])
            ring_came(base + 6 + block, fin.at[1, block])
            ring_came(base + 8 + block, fin.at[0, block])
            ring_came(base + 10 + block, fin.at[1, 2 + block])

    locals_y[0].wait()
    ring_far(*rings[1])
    merge(0)
    ring_far(*rings[0])

    f_sends = [
        ((y == 2) | (y == 1), remote(21, fsend.at[0], frecv.at[1], near["yl"])),
        (y == 3, remote(22, fsend.at[0], frecv.at[2], near["yr"])),
        ((y == 0) & ((z == 2) | (z == 1)), remote(23, fsend.at[1], frecv.at[3], near["zl"])),
        ((y == 0) & (z == 3), remote(24, fsend.at[1], frecv.at[4], near["zr"])),
    ]

    def f_take(at):
        came(20 + at, frecv.at[at])
        fsum[...] += frecv[at].astype(jnp.float32)

    def f_send(at):
        condition, copy = f_sends[at]

        @pl.when(condition)
        def _():
            fsend[at // 2] = fsum[...].astype(jnp.bfloat16)
            copy.start()

    mine_f.wait()
    came(20, frecv.at[0])
    fsum[...] = fown[...].astype(jnp.float32) + frecv[0].astype(jnp.float32)

    @pl.when(y == 1)
    def _():
        f_take(1)

    f_send(0)
    f_send(1)

    locals_y[1].wait()
    ring_right(*rings[1])
    locals_y[2].wait()
    ring_left(*rings[1])
    merge(1)
    ring_right(*rings[0])
    merge(2)
    ring_left(*rings[0])

    @pl.when(y == 0)
    def _():
        f_take(1)
        f_take(2)

        @pl.when(z == 1)
        def _():
            f_take(3)

    f_send(2)
    f_send(3)

    merge(3)
    ring_relay(*rings[1])
    ring_relay(*rings[0])
    top = (z == 0) & (y == 0)

    @pl.when(top)
    def _():
        f_take(3)
        f_take(4)

    locals_y[3].wait()
    for copy in locals_own:
        copy.wait()

    @pl.when(top & (c == 1))
    def _():
        fsend[1] = fsum[...].astype(jnp.bfloat16)
        remote(25, fsend.at[1], frecv.at[5], near["sib"]).start()

    @pl.when(top & (c == 0))
    def _():
        came(25, frecv.at[5])
        acck[0] += fsum[...]
        accv[0] += frecv[5].astype(jnp.float32)

    def total(own, fin, places):
        def one(block, carry):
            for part, (acc, out, head) in enumerate(places):
                lanes = pl.ds(head * HD, HD)
                value = acc[block, :, lanes]
                for ref in (own.at[3], fin.at[0], fin.at[1]):
                    value += ref[block, part].astype(jnp.float32)
                out[block, :, lanes] = value.astype(jnp.bfloat16)
            return carry

        lax.fori_loop(0, BLK_DEV, one, 0)

    ring_end(*rings[1])
    total(owny, finy, ((accq, out_q, 0), (acck, out_k, 1), (accv, out_v, 1)))
    ring_end(*rings[0])
    total(ownz, finz, ((acck, out_k, 0), (accv, out_v, 0), (accq, out_q, 1)))

    for copy in started:
        copy.wait_send()
    remote(20, fown, frecv.at[0], near["sib"]).wait_send()
    for condition, copy in f_sends + [
        (top & (c == 1), remote(25, fsend.at[1], frecv.at[5], near["sib"]))
    ]:
        @pl.when(condition)
        def _(copy=copy):
            copy.wait_send()


def body(query, keys, values, output, d_out, row_logsum, selected):
    bf16, f32 = jnp.bfloat16, jnp.float32
    any_spec = pl.BlockSpec(memory_space=pl.ANY)
    vmem_spec = pl.BlockSpec(memory_space=pltpu.VMEM)
    smem_spec = pl.BlockSpec(memory_space=pltpu.SMEM)
    blocked = (BLK_DEV, BLOCK, WIDTH)
    shape = jax.ShapeDtypeStruct
    dma, vmem, smem = pltpu.SemaphoreType.DMA, pltpu.VMEM, pltpu.SMEM
    zs, ys = shape((32, BLOCK, HD), bf16), shape((16, BLOCK, HD), bf16)
    kz, vz, qz, gz, sz, qy, gy, ky, vy, sy, own_q, own_k, own_v, own_f = pl.pallas_call(
        gather_kernel,
        out_shape=[zs] * 4
        + [shape((32, 8, BLOCK), f32)]
        + [ys] * 4
        + [shape((16, 8, BLOCK), f32)]
        + [shape(blocked, f32)] * 3
        + [shape((2, BLOCK, WIDTH), bf16)],
        in_specs=[any_spec] * 5 + [vmem_spec],
        out_specs=[any_spec] * 14,
        scratch_shapes=[vmem(blocked, bf16)] * 5
        + [vmem((BLK_DEV, 8, BLOCK), f32)]
        + [vmem(blocked, f32)] * 3
        + [
            vmem((2, BLOCK, WIDTH), bf16),
            vmem((2, BLOCK, WIDTH), f32),
            vmem((2, BLOCK, WIDTH), bf16),
            dma((41,)),
            dma((41,)),
            dma((56, 2)),
            dma((56, 2)),
            dma((26,)),
        ],
        compiler_params=pltpu.CompilerParams(
            collective_id=0, has_side_effects=True, vmem_limit_bytes=VMEM
        ),
        name="gather",
    )(
        keys.reshape(blocked), values.reshape(blocked), query.reshape(blocked),
        d_out, output.reshape(blocked), row_logsum,
    )
    pz, py = pl.pallas_call(
        pair_kernel,
        out_shape=[shape((32, 3, BLOCK, HD), bf16), shape((16, 3, BLOCK, HD), bf16)],
        in_specs=[vmem_spec] + [any_spec] * 8 + [vmem_spec] * 2,
        out_specs=[any_spec] * 2,
        scratch_shapes=[
            vmem((8, 128), jnp.int32),
            smem((8, 128), jnp.int32),
            vmem((2, 2, BLOCK, HD), bf16),
            vmem((2, 2, BLOCK, HD), bf16),
            vmem((2, 2, BLOCK, HD), bf16),
            vmem((2, 2, BLOCK, HD), bf16),
            vmem((16, BLOCK, HD), f32),
            vmem((32, BLOCK, HD), f32),
            vmem((2, BLOCK, HD), f32),
            vmem((2, BLOCK, HD), bf16),
            vmem((16, BLOCK, HD), bf16),
            vmem((32, BLOCK, HD), bf16),
            vmem((2, BLOCK, HD), bf16),
            dma,
            dma((2, 2, 4)),
            dma,
            dma((2, 32)),
            dma((2, 32)),
        ],
        compiler_params=pltpu.CompilerParams(vmem_limit_bytes=VMEM),
        name="pairs",
    )(selected, kz, vz, qz, gz, qy, gy, ky, vy, sz, sy)
    piece = (BLK_DEV, 3, BLOCK, HD)
    out_q, out_k, out_v = pl.pallas_call(
        scatter_kernel,
        out_shape=[shape(blocked, bf16)] * 3,
        in_specs=[any_spec] * 6,
        out_specs=[vmem_spec] * 3,
        scratch_shapes=[
            vmem((4,) + piece, bf16),
            vmem((4,) + piece, bf16),
            vmem((2, 2, 3, BLOCK, HD), bf16),
            vmem((2,) + piece, bf16),
            vmem((4,) + piece, bf16),
            vmem((2, 2, 3, BLOCK, HD), bf16),
            vmem((2,) + piece, bf16),
            vmem(blocked, f32),
            vmem(blocked, f32),
            vmem(blocked, f32),
            vmem((BLOCK, WIDTH), bf16),
            vmem((6, BLOCK, WIDTH), bf16),
            vmem((BLOCK, WIDTH), f32),
            vmem((2, BLOCK, WIDTH), bf16),
            dma((26,)),
            dma((26,)),
            dma((24,)),
            dma((24,)),
            dma((12,)),
        ],
        compiler_params=pltpu.CompilerParams(
            collective_id=1, has_side_effects=True, vmem_limit_bytes=VMEM
        ),
        name="scatter",
    )(pz, py, own_q, own_k, own_v, own_f)
    flat = (BLK_DEV * BLOCK, WIDTH)
    return out_q.reshape(flat), out_k.reshape(flat), out_v.reshape(flat)


def solution(mesh):
    in_specs = (
        P("seq", "head"),
        P("seq", "head"),
        P("seq", "head"),
        P("seq", "head"),
        P(("seq", "head"), None),
        P("head", "seq"),
        P(),
    )
    out_specs = (P("seq", "head"), P("seq", "head"), P("seq", "head"))
    return jax.shard_map(body, mesh=mesh, in_specs=in_specs, out_specs=out_specs, check_vma=False)
```

```python
import functools
import math

import jax
import jax.numpy as jnp
from jax import lax
from jax.experimental import pallas as pl
from jax.experimental.pallas import tpu as pltpu
from jax.sharding import PartitionSpec as P

MESH = pl.DeviceIdType.MESH
BLOCK = 512
HD = 128
WIDTH = 256
BLK_DEV = 4
RING = 4
NSLOT = 32
LOG2E = math.log2(math.e)
VMEM = 60 * 1024 * 1024


def place():
    seq = lax.axis_index("seq")
    return lax.div(seq, 8), lax.rem(lax.div(seq, 2), 4), lax.rem(seq, 2), lax.axis_index("head")


def device(z, y, c, x):
    return ((z * 4 + y) * 2 + c, x)


def after(index, step):
    return lax.rem(index + step, RING)


def neighbours(z, y, c, x):
    return {
        "sib": device(z, y, 1 - c, x),
        "zr": device(after(z, 1), y, c, x),
        "zl": device(after(z, 3), y, c, x),
        "yr": device(z, after(y, 1), c, x),
        "yl": device(z, after(y, 3), c, x),
    }


def greet(devices):
    barrier = pltpu.get_barrier_semaphore()
    for target in devices:
        pl.semaphore_signal(barrier, inc=1, device_id=target, device_id_type=MESH)
    pl.semaphore_wait(barrier, len(devices))


NT = (((1,), (1,)), ((), ()))
NN = (((1,), (0,)), ((), ()))
TN = (((0,), (0,)), ((), ()))


def dot(a, b, dims):
    return lax.dot_general(a, b, dims, preferred_element_type=jnp.float32)


def gather_kernel(
    keys, values, query, d_out, output, logsum,
    kz, vz, qz, gz, sz, qy, gy, ky, vy, sy, own_q, own_k, own_v, own_f,
    grad, outv, kv, vv, qv, stats, accq, acck, accv, fblk, accf, fout,
    send, recv, bulk_send, bulk_recv, local,
):
    z, y, c, x = place()
    near = neighbours(z, y, c, x)
    others = [((z * 4 + y) * 2 + c, after(x, step)) for step in (1, 2, 3)]
    greet(list(near.values()) + others)
    started = []

    def remote(index, src, dst, target):
        return pltpu.make_async_remote_copy(
            src_ref=src, dst_ref=dst, send_sem=send.at[index], recv_sem=recv.at[index],
            device_id=target, device_id_type=MESH,
        )

    def go(index, src, dst, target):
        copy = remote(index, src, dst, target)
        copy.start()
        started.append(copy)

    def bulk(array, kind, chunk, src, dst, target):
        return pltpu.make_async_remote_copy(
            src_ref=src, dst_ref=dst,
            send_sem=bulk_send.at[array * 7 + kind, chunk],
            recv_sem=bulk_recv.at[array * 7 + kind, chunk],
            device_id=target, device_id_type=MESH,
        )

    started_if = []

    def start_if(condition, copies):
        @pl.when(condition)
        def _():
            for copy in copies:
                copy.start()

        started_if.append((condition, copies))

    def spread(array, kind, src, head, dst, piece, target, condition):
        start_if(condition, [
            bulk(
                array, kind, chunk,
                src.at[pl.ds(2 * chunk, 2), :, pl.ds(head * HD, HD)],
                dst.at[pl.ds(piece + 2 * chunk, 2)],
                target,
            )
            for chunk in range(2)
        ])

    def relay(array, kind, ref, piece, condition, *onward):
        for chunk in range(2):
            at = ref.at[pl.ds(piece + 2 * chunk, 2)]

            @pl.when(condition)
            def _(at=at, chunk=chunk):
                bulk(array, kind, chunk, at, at, near["sib"]).wait_recv()

            for kind_on, target, condition_on in onward:
                start_if(condition_on, [bulk(array, kind_on, chunk, at, at, target)])

    def column(z_at, c_at):
        return (z_at * 2 + c_at) * BLK_DEV

    def row(y_at):
        return y_at * BLK_DEV

    def four(start):
        return pl.ds(start, BLK_DEV)

    zl, zr, zo = after(z, 3), after(z, 1), after(z, 2)
    yl, yr = after(y, 3), after(y, 1)
    top = (z == 0) & (y == 0)
    root = top & (c == 0)

    first_own = [
        pltpu.make_async_copy(keys.at[0], fblk.at[0], local.at[0]),
        pltpu.make_async_copy(values.at[0], fblk.at[1], local.at[1]),
    ]

    def first_copy(part, send_at, recv_at, target):
        return pltpu.make_async_remote_copy(
            src_ref=fblk.at[part], dst_ref=fblk.at[part],
            send_sem=send.at[send_at], recv_sem=recv.at[recv_at],
            device_id=target, device_id_type=MESH,
        )

    first_sends = [
        ((z == 0) & (y <= 1), first_copy(c, 28, 26, near["yr"])),
        ((z == 0) & (y == 0), first_copy(c, 29, 26, near["yl"])),
        (z <= 1, first_copy(c, 30, 26, near["zr"])),
        (z == 0, first_copy(c, 31, 26, near["zl"])),
        (jnp.logical_not(top & (c == 1)), first_copy(c, 32, 27, near["sib"])),
    ]
    first_start = first_copy(1, 33, 26, near["sib"])

    def send_first():
        for condition, copy in first_sends:
            @pl.when(condition)
            def _(copy=copy):
                copy.start()

    def pass_first(condition):
        @pl.when(condition)
        def _():
            first_copy(c, 28, 26, near["sib"]).wait_recv()
            send_first()

    @pl.when(root)
    def _():
        for copy in first_own:
            copy.start()
        for copy in first_own:
            copy.wait()
        first_start.start()
        send_first()

    pass_first(top & (c == 1))

    for step in (1, 2, 3):
        to = after(x, step)
        go(
            22 + step,
            d_out.at[:, pl.ds(pl.multiple_of(to * WIDTH, WIDTH), WIDTH)],
            grad.at[x],
            others[step - 1],
        )
    to_vmem = [
        pltpu.make_async_copy(
            d_out.at[:, pl.ds(pl.multiple_of(x * WIDTH, WIDTH), WIDTH)], grad.at[x], local.at[2]
        ),
        pltpu.make_async_copy(output, outv, local.at[3]),
        pltpu.make_async_copy(keys, kv, local.at[4]),
        pltpu.make_async_copy(values, vv, local.at[5]),
        pltpu.make_async_copy(query, qv, local.at[6]),
    ]
    kept = []
    for copy in to_vmem:
        copy.start()

    own_z, own_y = column(z, c), row(y)
    z_set = ((keys, 0, kz, 0), (values, 0, vz, 1), (query, 1, qz, 0), (grad, 1, gz, 1))
    y_set = ((query, 0, qy, 0), (grad, 0, gy, 1), (keys, 1, ky, 0), (values, 1, vy, 1))
    z_ways, y_ways = (near["zr"], near["zl"]), (near["yr"], near["yl"])

    def wanted(array, src, dst):
        if array < 2:
            return dst > src
        if array < 4:
            return dst < src
        if array < 6:
            return (dst < src) | (z > 0)
        return (dst > src) | (z < 3)

    def sent(array, kind, src):
        way = (z_set + y_set)[array][3]
        step = (1, 3)[way]
        if kind == 0:
            return wanted(array, src, after(src, step)) | wanted(array, src, after(src, 2))
        if kind == 1:
            return wanted(array, src, after(src, 4 - step))
        return wanted(array, src, after(src, 2))

    def spread_all(kind, arrays):
        for array in arrays:
            src, head, ref, way = (z_set + y_set)[array]
            piece, at, ways = (own_z, z, z_ways) if array < 4 else (own_y, y, y_ways)
            spread(
                array, kind, src, head, ref, piece, ways[(way + kind) % 2], sent(array, kind, at)
            )

    spread_all(0, (0, 1, 4, 7, 2, 6))
    spread_all(1, (0, 1, 4, 7, 2, 6))
    for array in (0, 1, 2):
        src, head, ref, _ = z_set[array]
        spread(array, 3, src, head, ref, own_z, near["sib"], z >= 0)

    pass_first((z == 0) & ((y == 1) | (y == 3)))
    to_vmem[0].wait()
    to_vmem[1].wait()
    for step in (1, 2, 3):
        remote(22 + step, grad.at[x], grad.at[x], others[step - 1]).wait_recv()
    spread_all(0, (3, 5))
    spread_all(1, (3, 5))
    spread(3, 3, grad, 1, gz, own_z, near["sib"], z >= 0)
    pass_first((z == 0) & (y == 2))
    stats[...] = jnp.zeros_like(stats)

    ones = jnp.ones((8, HD), jnp.bfloat16)
    for block in range(BLK_DEV):
        for head in range(2):
            part = pl.ds(head * HD, HD)
            product = grad[block, :, part].astype(jnp.float32) * outv[block, :, part].astype(jnp.float32)
            high = product.astype(jnp.bfloat16)
            low = (product - high.astype(jnp.float32)).astype(jnp.bfloat16)
            total = dot(ones, high, NT) + dot(ones, low, NT)
            stats[block, pl.ds(2 + head, 1), :] = total[0:1]
            stats[block, pl.ds(head, 1), :] = (
                logsum[pl.ds(head, 1), pl.ds(block * BLOCK, BLOCK)] * LOG2E
            )
    go(18, stats, sy.at[four(own_y)], near["yr"])
    go(19, stats, sy.at[four(own_y)], near["yl"])
    go(34, stats, sz.at[four(own_z)], near["zr"])
    go(35, stats, sz.at[four(own_z)], near["zl"])
    go(36, stats, sz.at[four(own_z)], near["sib"])

    for copy in to_vmem[2:]:
        copy.wait()
    held = {0: kv, 1: vv, 2: qv, 3: grad}
    keep = [(held[(0, 1, 2, 3)[at]], z_set[at][1], z_set[at][2].at[four(own_z)]) for at in range(4)]
    keep += [(held[(2, 3, 0, 1)[at]], y_set[at][1], y_set[at][2].at[four(own_y)]) for at in range(4)]
    keep += [(stats, None, sz.at[four(own_z)]), (stats, None, sy.at[four(own_y)])]
    for index, (src, head, dst) in enumerate(keep):
        part = src if head is None else src.at[:, :, pl.ds(head * HD, HD)]
        kept.append(pltpu.make_async_copy(part, dst, local.at[16 + index]))
        kept[-1].start()
    scale = 1.0 / math.sqrt(HD)

    def own_block(block, carry):
        for head in range(2):
            part = pl.ds(head * HD, HD)
            k, v, q, g = kv[block, :, part], vv[block, :, part], qv[block, :, part], grad[block, :, part]
            lse = stats[block, pl.ds(head, 1), :]
            delta = stats[block, pl.ds(2 + head, 1), :]
            p = jnp.exp2(dot(k, q, NT) * (scale * LOG2E) - lse)
            key_at = lax.broadcasted_iota(jnp.int32, (BLOCK, BLOCK), 0)
            query_at = lax.broadcasted_iota(jnp.int32, (BLOCK, BLOCK), 1)
            p = jnp.where(key_at <= query_at, p, 0.0)
            ds = (p * (dot(v, g, NT) - delta)).astype(jnp.bfloat16)
            accv[block, :, part] = dot(p.astype(jnp.bfloat16), g, NN)
            acck[block, :, part] = dot(ds, q, NN) * scale
            accq[block, :, part] = dot(ds, k, TN) * scale
        return carry

    def first_block(block, carry):
        for head in range(2):
            part = pl.ds(head * HD, HD)
            k, v, q, g = fblk[0, :, part], fblk[1, :, part], qv[block, :, part], grad[block, :, part]
            lse = stats[block, pl.ds(head, 1), :]
            delta = stats[block, pl.ds(2 + head, 1), :]
            p = jnp.exp2(dot(k, q, NT) * (scale * LOG2E) - lse)
            ds = (p * (dot(v, g, NT) - delta)).astype(jnp.bfloat16)
            accf[1, :, part] += dot(p.astype(jnp.bfloat16), g, NN)
            accf[0, :, part] += dot(ds, q, NN) * scale
            accq[block, :, part] += dot(ds, k, TN) * scale
        return carry

    lax.fori_loop(0, BLK_DEV, own_block, 0)
    for index, (src, dst) in enumerate(((acck, own_k), (accv, own_v))):
        kept.append(pltpu.make_async_copy(src, dst, local.at[12 + index]))
        kept[-1].start()
    pass_first((z == 1) | (z == 3))

    def pieces(array):
        _, _, ref, way = (z_set + y_set)[array]
        if array < 4:
            at = (zl, zr, zo) if way == 0 else (zr, zl, zo)
            return ref, at, [column(one, c) for one in at], z_ways[way]
        at = (yl, yr, after(y, 2)) if way == 0 else (yr, yl, after(y, 2))
        return ref, at, [row(one) for one in at], y_ways[way]

    def onward(array, kind):
        ref, at, piece, way = pieces(array)
        came = sent(array, kind, at[kind])
        sends = [(2, way, sent(array, 2, at[0]))] if kind == 0 else []
        if array < 4:
            sends.append((4 + kind, near["sib"], came))
        relay(array, kind, ref, piece[kind], came, *sends)

    for array in (0, 1, 4, 7, 2, 6):
        onward(array, 0)
    sy_in = [sy.at[four(row(after(y, step)))] for step in (3, 1, 2)]
    sz_in = [sz.at[four(column(after(z, step), c))] for step in (3, 1, 2)]

    def stat_in(index, ref):
        remote(index, ref, ref, near["sib"]).wait_recv()

    stat_in(18, sy_in[0])
    go(22, sy_in[0], sy_in[0], near["yr"])
    stat_in(34, sz_in[0])
    go(37, sz_in[0], sz_in[0], near["zr"])
    go(38, sz_in[0], sz_in[0], near["sib"])
    for array in (3, 5):
        onward(array, 0)
    pass_first(z == 2)

    @pl.when(jnp.logical_not(root))
    def _():
        first_copy(1 - c, 32, 27, near["sib"]).wait_recv()

    accf[...] = jnp.zeros_like(accf)
    lax.fori_loop(jnp.where(root, 1, 0), BLK_DEV, first_block, 0)
    fout[...] = accf[...].astype(jnp.bfloat16)
    for index, (src, dst) in enumerate(((accq, own_q), (fout, own_f))):
        kept.append(pltpu.make_async_copy(src, dst, local.at[14 + index]))
        kept[-1].start()
    stat_in(35, sz_in[1])
    go(39, sz_in[1], sz_in[1], near["sib"])
    for kind in (1, 2):
        for array in (0, 1, 4, 7, 2, 6, 3, 5):
            onward(array, kind)
    stat_in(37, sz_in[2])
    go(40, sz_in[2], sz_in[2], near["sib"])
    stat_in(19, sy_in[1])
    stat_in(22, sy_in[2])
    for array in range(4):
        ref, at, _, _ = pieces(array)
        relay(array, 3, ref, column(z, 1 - c), z >= 0)
        for kind in range(3):
            relay(array, 4 + kind, ref, column(at[kind], 1 - c), sent(array, kind, at[kind]))
    for index, at in ((36, z), (38, zl), (39, zr), (40, zo)):
        stat_in(index, sz.at[four(column(at, 1 - c))])
    for copy in kept:
        copy.wait()
    for condition, copies in started_if:
        @pl.when(condition)
        def _(copies=copies):
            for copy in copies:
                copy.wait_send()

    for copy in started:
        copy.wait_send()

    @pl.when(root)
    def _():
        first_start.wait_send()

    for condition, copy in first_sends:
        @pl.when(condition)
        def _(copy=copy):
            copy.wait_send()


def choose(selected, z, y, c, head):
    row_at = lax.broadcasted_iota(jnp.int32, (32, 1), 0)
    group, core, block = row_at >> 3, (row_at >> 2) & 1, row_at & 3
    if head == 0:
        slab = selected[pl.ds(pl.multiple_of(z * 32, 32), 32), :]
    else:
        slab = jnp.concatenate(
            [selected[pl.ds(pl.multiple_of(at * 32 + y * 8, 8), 8), :] for at in range(4)], axis=0
        )
    lane = lax.broadcasted_iota(jnp.int32, (32, 128), 1)
    found = jnp.zeros((32, 128), jnp.int32)
    for pick in range(3):
        chosen = slab[:, pick : pick + 1]
        z_of, y_of, c_of, b_of = chosen >> 5, (chosen >> 3) & 3, (chosen >> 2) & 1, chosen & 3
        if head == 0:
            here = (chosen > 0) & (y_of == y) & (core == c)
            target = ((z_of * 2 + c_of) * 4 + b_of) * 4 + group
            value = 1 + group * 4 + block
        else:
            here = (chosen > 0) & (z_of == z) & (c_of == c)
            target = (y_of * 4 + b_of) * 8 + group * 2 + core
            value = 1 + (group * 2 + core) * 4 + block
        found += jnp.where(here & (lane == target), value, 0)
    table = jnp.sum(found, axis=0, keepdims=True)
    down = lax.broadcasted_iota(jnp.int32, (128, 128), 0)
    across = lax.broadcasted_iota(jnp.int32, (128, 128), 1)
    spread = jnp.broadcast_to(table, (128, 128))
    rank = jnp.sum(jnp.where((across < down) & (spread > 0), 1, 0), axis=1, keepdims=True)
    entry = jnp.sum(jnp.where(across == down, spread, 0), axis=1, keepdims=True)
    item = jnp.where(entry > 0, down[:, 0:1] * 128 + entry, 0)
    items = jnp.sum(jnp.where(rank == across, item, 0), axis=0, keepdims=True)
    return items, table


def pair_kernel(
    selected, kz, vz, qz, gz, qy, gy, ky, vy, sz, sy,
    pz, py,
    lists_v, lists, kbuf, vbuf, qbuf, gbuf, dq0, dq1, dkv, kvout, qout0, qout1, zero,
    list_sem, in_sem, out_sem, q_sem, zero_sem,
):
    z, y, c, _ = place()
    scale = 1.0 / math.sqrt(HD)
    for head in range(2):
        items, table = choose(selected, z, y, c, head)
        lists_v[pl.ds(2 * head, 1), :] = items
        lists_v[pl.ds(2 * head + 1, 1), :] = table
    listed = pltpu.make_async_copy(lists_v, lists, list_sem)
    listed.start()
    zero[...] = jnp.zeros_like(zero)
    listed.wait()

    class Part:
        pass

    parts = []
    for head in range(2):
        part = Part()
        part.head, part.per, part.slots = head, (4, 8)[head], (32, 16)[head]
        part.k, part.v, part.q, part.g = ((kz, vz, qy, gy), (ky, vy, qz, gz))[head]
        part.stat, part.dq, part.qout = ((sy, dq0, qout0), (sz, dq1, qout1))[head]
        part.out, part.at = ((pz, 0), (py, 1))[head]
        part.dq_out, part.dq_at = ((py, 0), (pz, 2))[head]
        parts.append(part)

    def item_of(part, at):
        item = lists[2 * part.head, at]
        return lax.div(item, 128 * part.per), lax.rem(item, 128) - 1, item

    def loads(part, at):
        slot, block, _ = item_of(part, at)
        side = lax.rem(at, 2)
        pairs = ((part.k, kbuf, slot), (part.v, vbuf, slot), (part.q, qbuf, block), (part.g, gbuf, block))
        return [
            pltpu.make_async_copy(
                src.at[where], buf.at[part.head, side], in_sem.at[part.head, side, index]
            )
            for index, (src, buf, where) in enumerate(pairs)
        ]

    for part in parts:
        @pl.when(lists[2 * part.head, 0] > 0)
        def _(part=part):
            for copy in loads(part, 0):
                copy.start()

    def idle(part, slot):
        total = lists[2 * part.head + 1, slot * part.per]
        for at in range(1, part.per):
            total += lists[2 * part.head + 1, slot * part.per + at]
        return total == 0

    def blank(part, slot):
        return pltpu.make_async_copy(
            zero, part.out.at[slot, pl.ds(part.at, 2)], zero_sem.at[part.head, slot]
        )

    def each_idle(part, act):
        def one(slot, carry):
            @pl.when(idle(part, slot))
            def _():
                act(blank(part, slot))
            return carry

        lax.fori_loop(0, part.slots, one, 0)

    for part in parts:
        each_idle(part, lambda copy: copy.start())
        part.dq[...] = jnp.zeros_like(part.dq)

    out = pltpu.make_async_copy(kvout, pz.at[0, pl.ds(0, 2)], out_sem)
    written = 0
    for part in parts:
        def step(state, part=part):
            at, opened, done = state
            slot, block, _ = item_of(part, at)
            next_slot, _, following = item_of(part, at + 1)
            side = lax.rem(at, 2)

            @pl.when(following > 0)
            def _():
                for copy in loads(part, at + 1):
                    copy.start()

            for copy in loads(part, at):
                copy.wait()

            @pl.when(slot != opened)
            def _():
                dkv[...] = jnp.zeros_like(dkv)

            k, v = kbuf[part.head, side], vbuf[part.head, side]
            q, g = qbuf[part.head, side], gbuf[part.head, side]
            lse = part.stat[block, pl.ds(part.head, 1), :]
            delta = part.stat[block, pl.ds(2 + part.head, 1), :]
            p = jnp.exp2(dot(k, q, NT) * (scale * LOG2E) - lse)
            ds = (p * (dot(v, g, NT) - delta)).astype(jnp.bfloat16)
            dkv[1] += dot(p.astype(jnp.bfloat16), g, NN)
            dkv[0] += dot(ds, q, NN)
            part.dq[block] += dot(ds, k, TN)
            closing = (following == 0) | (next_slot != slot)

            @pl.when(closing)
            def _():
                @pl.when(done > 0)
                def _():
                    out.wait()
                kvout[0] = (dkv[0] * scale).astype(jnp.bfloat16)
                kvout[1] = dkv[1].astype(jnp.bfloat16)
                pltpu.make_async_copy(kvout, part.out.at[slot, pl.ds(part.at, 2)], out_sem).start()

            return at + 1, slot, done + jnp.where(closing, 1, 0)

        _, _, written = lax.while_loop(
            lambda state, part=part: lists[2 * part.head, state[0]] > 0,
            step,
            (jnp.int32(0), jnp.int32(-1), jnp.int32(written)),
        )

        def flush(block, part=part):
            return pltpu.make_async_copy(
                part.qout.at[block], part.dq_out.at[block, part.dq_at], q_sem.at[part.head, block]
            )

        def finish(block, carry, part=part, flush=flush):
            part.qout[block] = (part.dq[block] * scale).astype(jnp.bfloat16)
            flush(block).start()
            return carry

        part.flush = flush
        part.blocks = (16, 32)[part.head]
        lax.fori_loop(0, part.blocks, finish, 0)

    @pl.when(written > 0)
    def _():
        out.wait()

    for part in parts:
        def drain(block, carry, part=part):
            part.flush(block).wait()
            return carry

        lax.fori_loop(0, part.blocks, drain, 0)
        each_idle(part, lambda copy: copy.wait())


def scatter_kernel(
    pz, py, own_q, own_k, own_v, own_f,
    out_q, out_k, out_v,
    ownz, sibz, relz, finz, owny, rely, finy, accq, acck, accv,
    fown, frecv, fsum, fsend,
    send, recv, ring_send, ring_recv, local,
):
    z, y, c, x = place()
    near = neighbours(z, y, c, x)
    greet(list(near.values()))
    started = []

    def remote(index, src, dst, target):
        return pltpu.make_async_remote_copy(
            src_ref=src, dst_ref=dst, send_sem=send.at[index], recv_sem=recv.at[index],
            device_id=target, device_id_type=MESH,
        )

    def go(index, src, dst, target):
        copy = remote(index, src, dst, target)
        copy.start()
        started.append(copy)

    def came(index, dst):
        remote(index, dst, dst, near["sib"]).wait_recv()

    def ring_copy(index, src, dst, target):
        return pltpu.make_async_remote_copy(
            src_ref=src, dst_ref=dst, send_sem=ring_send.at[index], recv_sem=ring_recv.at[index],
            device_id=target, device_id_type=MESH,
        )

    def ring_go(index, src, dst, target):
        copy = ring_copy(index, src, dst, target)
        copy.start()
        started.append(copy)

    def ring_came(index, dst):
        ring_copy(index, dst, dst, near["sib"]).wait_recv()

    def column(z_at, c_at):
        return pl.ds((z_at * 2 + c_at) * BLK_DEV, BLK_DEV)

    def local_copy(index, src, dst):
        copy = pltpu.make_async_copy(src, dst, local.at[index])
        copy.start()
        return copy

    hops = (2, 1, 3, 0)
    locals_z, locals_y = [], []
    for j, hop in enumerate(hops):
        go(j, pz.at[column(after(z, hop), 1 - c)], sibz.at[j], near["sib"])
        locals_z.append(local_copy(j, pz.at[column(after(z, hop), c)], ownz.at[j]))
        locals_y.append(
            local_copy(4 + j, py.at[pl.ds(after(y, hop) * BLK_DEV, BLK_DEV)], owny.at[j])
        )
        if j == 0:
            remote(20, own_f.at[1 - c], frecv.at[0], near["sib"]).start()
            mine_f = local_copy(8, own_f.at[c], fown)
    locals_own = [
        local_copy(9 + j, src, dst)
        for j, (src, dst) in enumerate(((own_q, accq), (own_k, acck), (own_v, accv)))
    ]

    def add(dst, src):
        for part in range(3):
            dst[part] = (dst[part].astype(jnp.float32) + src[part].astype(jnp.float32)).astype(
                jnp.bfloat16
            )

    def merge(j):
        locals_z[j].wait()
        came(j, sibz.at[j])

        def one(block, carry):
            add(ownz.at[j, block], sibz.at[j, block])
            return carry

        lax.fori_loop(0, BLK_DEV, one, 0)

    rings = ((0, ownz, relz, finz, near["zr"], near["zl"]), (12, owny, rely, finy, near["yr"], near["yl"]))

    def ring_far(base, own, rel, fin, right, left):
        for block in range(2):
            ring_go(base + block, own.at[0, block], rel.at[0, block], right)
            ring_go(base + 2 + block, own.at[0, 2 + block], rel.at[1, block], left)

    def ring_right(base, own, rel, fin, right, left):
        for block in range(2):
            ring_go(base + 4 + block, own.at[1, 2 + block], fin.at[0, 2 + block], right)

    def ring_left(base, own, rel, fin, right, left):
        for block in range(2):
            ring_go(base + 6 + block, own.at[2, block], fin.at[1, block], left)

    def ring_relay(base, own, rel, fin, right, left):
        for block in range(2):
            ring_came(base + block, rel.at[0, block])
            add(own.at[1, block], rel.at[0, block])
            ring_go(base + 8 + block, own.at[1, block], fin.at[0, block], right)
            ring_came(base + 2 + block, rel.at[1, block])
            add(own.at[2, 2 + block], rel.at[1, block])
            ring_go(base + 10 + block, own.at[2, 2 + block], fin.at[1, 2 + block], left)

    def ring_end(base, own, rel, fin, right, left):
        for block in range(2):
            ring_came(base + 4 + block, fin.at[0, 2 + block])
            ring_came(base + 6 + block, fin.at[1, block])
            ring_came(base + 8 + block, fin.at[0, block])
            ring_came(base + 10 + block, fin.at[1, 2 + block])

    locals_y[0].wait()
    ring_far(*rings[1])
    merge(0)
    ring_far(*rings[0])

    f_sends = [
        ((y == 2) | (y == 1), remote(21, fsend.at[0], frecv.at[1], near["yl"])),
        (y == 3, remote(22, fsend.at[0], frecv.at[2], near["yr"])),
        ((y == 0) & ((z == 2) | (z == 1)), remote(23, fsend.at[1], frecv.at[3], near["zl"])),
        ((y == 0) & (z == 3), remote(24, fsend.at[1], frecv.at[4], near["zr"])),
    ]

    def f_take(at):
        came(20 + at, frecv.at[at])
        fsum[...] += frecv[at].astype(jnp.float32)

    def f_send(at):
        condition, copy = f_sends[at]

        @pl.when(condition)
        def _():
            fsend[at // 2] = fsum[...].astype(jnp.bfloat16)
            copy.start()

    mine_f.wait()
    came(20, frecv.at[0])
    fsum[...] = fown[...].astype(jnp.float32) + frecv[0].astype(jnp.float32)

    @pl.when(y == 1)
    def _():
        f_take(1)

    f_send(0)
    f_send(1)

    locals_y[1].wait()
    ring_right(*rings[1])
    locals_y[2].wait()
    ring_left(*rings[1])
    merge(1)
    ring_right(*rings[0])
    merge(2)
    ring_left(*rings[0])

    @pl.when(y == 0)
    def _():
        f_take(1)
        f_take(2)

        @pl.when(z == 1)
        def _():
            f_take(3)

    f_send(2)
    f_send(3)

    merge(3)
    ring_relay(*rings[1])
    ring_relay(*rings[0])
    top = (z == 0) & (y == 0)

    @pl.when(top)
    def _():
        f_take(3)
        f_take(4)

    locals_y[3].wait()
    for copy in locals_own:
        copy.wait()

    @pl.when(top & (c == 1))
    def _():
        fsend[1] = fsum[...].astype(jnp.bfloat16)
        remote(25, fsend.at[1], frecv.at[5], near["sib"]).start()

    @pl.when(top & (c == 0))
    def _():
        came(25, frecv.at[5])
        acck[0] += fsum[...]
        accv[0] += frecv[5].astype(jnp.float32)

    def total(own, fin, places):
        def one(block, carry):
            for part, (acc, out, head) in enumerate(places):
                lanes = pl.ds(head * HD, HD)
                value = acc[block, :, lanes]
                for ref in (own.at[3], fin.at[0], fin.at[1]):
                    value += ref[block, part].astype(jnp.float32)
                out[block, :, lanes] = value.astype(jnp.bfloat16)
            return carry

        lax.fori_loop(0, BLK_DEV, one, 0)

    ring_end(*rings[1])
    total(owny, finy, ((accq, out_q, 0), (acck, out_k, 1), (accv, out_v, 1)))
    ring_end(*rings[0])
    total(ownz, finz, ((acck, out_k, 0), (accv, out_v, 0), (accq, out_q, 1)))

    for copy in started:
        copy.wait_send()
    remote(20, fown, frecv.at[0], near["sib"]).wait_send()
    for condition, copy in f_sends + [
        (top & (c == 1), remote(25, fsend.at[1], frecv.at[5], near["sib"]))
    ]:
        @pl.when(condition)
        def _(copy=copy):
            copy.wait_send()


def keep_kernel(in_q, in_k, in_v, out_q, out_k, out_v, held, in_sem, out_sem):
    ins, outs = [], []
    for part, (src, dst) in enumerate(((in_q, out_q), (in_k, out_k), (in_v, out_v))):
        for half in range(2):
            piece = pl.ds(2 * half, 2)
            ins.append(
                pltpu.make_async_copy(src.at[piece], held.at[part, piece], in_sem.at[part, half])
            )
            outs.append(
                pltpu.make_async_copy(held.at[part, piece], dst.at[piece], out_sem.at[part, half])
            )
    for copy in ins:
        copy.start()
    for copy, out in zip(ins, outs):
        copy.wait()
        out.start()
    for out in outs:
        out.wait()


def body(query, keys, values, output, d_out, row_logsum, selected):
    bf16, f32 = jnp.bfloat16, jnp.float32
    any_spec = pl.BlockSpec(memory_space=pl.ANY)
    vmem_spec = pl.BlockSpec(memory_space=pltpu.VMEM)
    smem_spec = pl.BlockSpec(memory_space=pltpu.SMEM)
    blocked = (BLK_DEV, BLOCK, WIDTH)
    shape = jax.ShapeDtypeStruct
    dma, vmem, smem = pltpu.SemaphoreType.DMA, pltpu.VMEM, pltpu.SMEM
    zs, ys = shape((32, BLOCK, HD), bf16), shape((16, BLOCK, HD), bf16)
    kz, vz, qz, gz, sz, qy, gy, ky, vy, sy, own_q, own_k, own_v, own_f = pl.pallas_call(
        gather_kernel,
        out_shape=[zs] * 4
        + [shape((32, 8, BLOCK), f32)]
        + [ys] * 4
        + [shape((16, 8, BLOCK), f32)]
        + [shape(blocked, f32)] * 3
        + [shape((2, BLOCK, WIDTH), bf16)],
        in_specs=[any_spec] * 5 + [vmem_spec],
        out_specs=[any_spec] * 14,
        scratch_shapes=[vmem(blocked, bf16)] * 5
        + [vmem((BLK_DEV, 8, BLOCK), f32)]
        + [vmem(blocked, f32)] * 3
        + [
            vmem((2, BLOCK, WIDTH), bf16),
            vmem((2, BLOCK, WIDTH), f32),
            vmem((2, BLOCK, WIDTH), bf16),
            dma((41,)),
            dma((41,)),
            dma((56, 2)),
            dma((56, 2)),
            dma((26,)),
        ],
        compiler_params=pltpu.CompilerParams(
            collective_id=0, has_side_effects=True, vmem_limit_bytes=VMEM
        ),
        name="gather",
    )(
        keys.reshape(blocked), values.reshape(blocked), query.reshape(blocked),
        d_out, output.reshape(blocked), row_logsum,
    )
    pz, py = pl.pallas_call(
        pair_kernel,
        out_shape=[shape((32, 3, BLOCK, HD), bf16), shape((16, 3, BLOCK, HD), bf16)],
        in_specs=[vmem_spec] + [any_spec] * 8 + [vmem_spec] * 2,
        out_specs=[any_spec] * 2,
        scratch_shapes=[
            vmem((8, 128), jnp.int32),
            smem((8, 128), jnp.int32),
            vmem((2, 2, BLOCK, HD), bf16),
            vmem((2, 2, BLOCK, HD), bf16),
            vmem((2, 2, BLOCK, HD), bf16),
            vmem((2, 2, BLOCK, HD), bf16),
            vmem((16, BLOCK, HD), f32),
            vmem((32, BLOCK, HD), f32),
            vmem((2, BLOCK, HD), f32),
            vmem((2, BLOCK, HD), bf16),
            vmem((16, BLOCK, HD), bf16),
            vmem((32, BLOCK, HD), bf16),
            vmem((2, BLOCK, HD), bf16),
            dma,
            dma((2, 2, 4)),
            dma,
            dma((2, 32)),
            dma((2, 32)),
        ],
        compiler_params=pltpu.CompilerParams(vmem_limit_bytes=VMEM),
        name="pairs",
    )(selected, kz, vz, qz, gz, qy, gy, ky, vy, sz, sy)
    piece = (BLK_DEV, 3, BLOCK, HD)
    out_q, out_k, out_v = pl.pallas_call(
        scatter_kernel,
        out_shape=[shape(blocked, bf16)] * 3,
        in_specs=[any_spec] * 6,
        out_specs=[vmem_spec] * 3,
        scratch_shapes=[
            vmem((4,) + piece, bf16),
            vmem((4,) + piece, bf16),
            vmem((2, 2, 3, BLOCK, HD), bf16),
            vmem((2,) + piece, bf16),
            vmem((4,) + piece, bf16),
            vmem((2, 2, 3, BLOCK, HD), bf16),
            vmem((2,) + piece, bf16),
            vmem(blocked, f32),
            vmem(blocked, f32),
            vmem(blocked, f32),
            vmem((BLOCK, WIDTH), bf16),
            vmem((6, BLOCK, WIDTH), bf16),
            vmem((BLOCK, WIDTH), f32),
            vmem((2, BLOCK, WIDTH), bf16),
            dma((26,)),
            dma((26,)),
            dma((24,)),
            dma((24,)),
            dma((12,)),
        ],
        compiler_params=pltpu.CompilerParams(
            collective_id=1, has_side_effects=True, vmem_limit_bytes=VMEM
        ),
        name="scatter",
    )(pz, py, own_q, own_k, own_v, own_f)
    out_q, out_k, out_v = pl.pallas_call(
        keep_kernel,
        out_shape=[shape(blocked, bf16)] * 3,
        in_specs=[any_spec] * 3,
        out_specs=[any_spec] * 3,
        scratch_shapes=[vmem((3,) + blocked, bf16), dma((3, 2)), dma((3, 2))],
        compiler_params=pltpu.CompilerParams(vmem_limit_bytes=VMEM),
        name="keep",
    )(out_q, out_k, out_v)
    flat = (BLK_DEV * BLOCK, WIDTH)
    return out_q.reshape(flat), out_k.reshape(flat), out_v.reshape(flat)


def solution(mesh):
    in_specs = (
        P("seq", "head"),
        P("seq", "head"),
        P("seq", "head"),
        P("seq", "head"),
        P(("seq", "head"), None),
        P("head", "seq"),
        P(),
    )
    out_specs = (P("seq", "head"), P("seq", "head"), P("seq", "head"))
    return jax.shard_map(body, mesh=mesh, in_specs=in_specs, out_specs=out_specs, check_vma=False)
```

```python
import functools
import math

import jax
import jax.numpy as jnp
from jax import lax
from jax.experimental import pallas as pl
from jax.experimental.pallas import tpu as pltpu
from jax.sharding import PartitionSpec as P

MESH = pl.DeviceIdType.MESH
BLOCK = 512
HD = 128
WIDTH = 256
BLK_DEV = 4
RING = 4
NSLOT = 32
LOG2E = math.log2(math.e)
VMEM = 60 * 1024 * 1024


def place():
    seq = lax.axis_index("seq")
    return lax.div(seq, 8), lax.rem(lax.div(seq, 2), 4), lax.rem(seq, 2), lax.axis_index("head")


def device(z, y, c, x):
    return ((z * 4 + y) * 2 + c, x)


def after(index, step):
    return lax.rem(index + step, RING)


def neighbours(z, y, c, x):
    return {
        "sib": device(z, y, 1 - c, x),
        "zr": device(after(z, 1), y, c, x),
        "zl": device(after(z, 3), y, c, x),
        "yr": device(z, after(y, 1), c, x),
        "yl": device(z, after(y, 3), c, x),
    }


def greet(devices):
    barrier = pltpu.get_barrier_semaphore()
    for target in devices:
        pl.semaphore_signal(barrier, inc=1, device_id=target, device_id_type=MESH)
    pl.semaphore_wait(barrier, len(devices))


NT = (((1,), (1,)), ((), ()))
NN = (((1,), (0,)), ((), ()))
TN = (((0,), (0,)), ((), ()))


def dot(a, b, dims):
    return lax.dot_general(a, b, dims, preferred_element_type=jnp.float32)


def gather_kernel(
    keys, values, query, d_out, output, logsum,
    kz, vz, qz, gz, sz, qy, gy, ky, vy, sy, own_q, own_k, own_v, own_f,
    grad, outv, kv, vv, qv, stats, accq, acck, accv, fblk, accf, fout,
    send, recv, bulk_send, bulk_recv, local,
):
    z, y, c, x = place()
    near = neighbours(z, y, c, x)
    others = [((z * 4 + y) * 2 + c, after(x, step)) for step in (1, 2, 3)]
    greet(list(near.values()) + others)
    started = []

    def remote(index, src, dst, target):
        return pltpu.make_async_remote_copy(
            src_ref=src, dst_ref=dst, send_sem=send.at[index], recv_sem=recv.at[index],
            device_id=target, device_id_type=MESH,
        )

    def go(index, src, dst, target):
        copy = remote(index, src, dst, target)
        copy.start()
        started.append(copy)

    def bulk(array, kind, chunk, src, dst, target):
        return pltpu.make_async_remote_copy(
            src_ref=src, dst_ref=dst,
            send_sem=bulk_send.at[array * 7 + kind, chunk],
            recv_sem=bulk_recv.at[array * 7 + kind, chunk],
            device_id=target, device_id_type=MESH,
        )

    started_if = []

    def start_if(condition, copies):
        @pl.when(condition)
        def _():
            for copy in copies:
                copy.start()

        started_if.append((condition, copies))

    def spread(array, kind, src, head, dst, piece, target, condition):
        start_if(condition, [
            bulk(
                array, kind, chunk,
                src.at[pl.ds(2 * chunk, 2), :, pl.ds(head * HD, HD)],
                dst.at[pl.ds(piece + 2 * chunk, 2)],
                target,
            )
            for chunk in range(2)
        ])

    def relay(array, kind, ref, piece, condition, *onward):
        for chunk in range(2):
            at = ref.at[pl.ds(piece + 2 * chunk, 2)]

            @pl.when(condition)
            def _(at=at, chunk=chunk):
                bulk(array, kind, chunk, at, at, near["sib"]).wait_recv()

            for kind_on, target, condition_on in onward:
                start_if(condition_on, [bulk(array, kind_on, chunk, at, at, target)])

    def column(z_at, c_at):
        return (z_at * 2 + c_at) * BLK_DEV

    def row(y_at):
        return y_at * BLK_DEV

    def four(start):
        return pl.ds(start, BLK_DEV)

    zl, zr, zo = after(z, 3), after(z, 1), after(z, 2)
    yl, yr = after(y, 3), after(y, 1)
    top = (z == 0) & (y == 0)
    root = top & (c == 0)

    first_own = [
        pltpu.make_async_copy(keys.at[0], fblk.at[0], local.at[0]),
        pltpu.make_async_copy(values.at[0], fblk.at[1], local.at[1]),
    ]

    def first_copy(part, send_at, recv_at, target):
        return pltpu.make_async_remote_copy(
            src_ref=fblk.at[part], dst_ref=fblk.at[part],
            send_sem=send.at[send_at], recv_sem=recv.at[recv_at],
            device_id=target, device_id_type=MESH,
        )

    first_sends = [
        ((z == 0) & (y <= 1), first_copy(c, 28, 26, near["yr"])),
        ((z == 0) & (y == 0), first_copy(c, 29, 26, near["yl"])),
        (z <= 1, first_copy(c, 30, 26, near["zr"])),
        (z == 0, first_copy(c, 31, 26, near["zl"])),
        (jnp.logical_not(top & (c == 1)), first_copy(c, 32, 27, near["sib"])),
    ]
    first_start = first_copy(1, 33, 26, near["sib"])

    def send_first():
        for condition, copy in first_sends:
            @pl.when(condition)
            def _(copy=copy):
                copy.start()

    def pass_first(condition):
        @pl.when(condition)
        def _():
            first_copy(c, 28, 26, near["sib"]).wait_recv()
            send_first()

    @pl.when(root)
    def _():
        for copy in first_own:
            copy.start()
        for copy in first_own:
            copy.wait()
        first_start.start()
        send_first()

    pass_first(top & (c == 1))

    for step in (1, 2, 3):
        to = after(x, step)
        go(
            22 + step,
            d_out.at[:, pl.ds(pl.multiple_of(to * WIDTH, WIDTH), WIDTH)],
            grad.at[x],
            others[step - 1],
        )
    to_vmem = [
        pltpu.make_async_copy(
            d_out.at[:, pl.ds(pl.multiple_of(x * WIDTH, WIDTH), WIDTH)], grad.at[x], local.at[2]
        ),
        pltpu.make_async_copy(output, outv, local.at[3]),
        pltpu.make_async_copy(keys, kv, local.at[4]),
        pltpu.make_async_copy(values, vv, local.at[5]),
        pltpu.make_async_copy(query, qv, local.at[6]),
    ]
    kept = []
    for copy in to_vmem:
        copy.start()

    own_z, own_y = column(z, c), row(y)
    z_set = ((keys, 0, kz, 0), (values, 0, vz, 1), (query, 1, qz, 0), (grad, 1, gz, 1))
    y_set = ((query, 0, qy, 0), (grad, 0, gy, 1), (keys, 1, ky, 0), (values, 1, vy, 1))
    z_ways, y_ways = (near["zr"], near["zl"]), (near["yr"], near["yl"])

    def wanted(array, src, dst):
        if array < 2:
            return dst > src
        if array < 4:
            return dst < src
        if array < 6:
            return (dst < src) | (z > 0)
        return (dst > src) | (z < 3)

    def sent(array, kind, src):
        way = (z_set + y_set)[array][3]
        step = (1, 3)[way]
        if kind == 0:
            return wanted(array, src, after(src, step)) | wanted(array, src, after(src, 2))
        if kind == 1:
            return wanted(array, src, after(src, 4 - step))
        return wanted(array, src, after(src, 2))

    def spread_all(kind, arrays):
        for array in arrays:
            src, head, ref, way = (z_set + y_set)[array]
            piece, at, ways = (own_z, z, z_ways) if array < 4 else (own_y, y, y_ways)
            spread(
                array, kind, src, head, ref, piece, ways[(way + kind) % 2], sent(array, kind, at)
            )

    spread_all(0, (0, 1, 4, 7, 2, 6))
    spread_all(1, (0, 1, 4, 7, 2, 6))
    for array in (0, 1, 2):
        src, head, ref, _ = z_set[array]
        spread(array, 3, src, head, ref, own_z, near["sib"], z >= 0)

    pass_first((z == 0) & ((y == 1) | (y == 3)))
    to_vmem[0].wait()
    to_vmem[1].wait()
    for step in (1, 2, 3):
        remote(22 + step, grad.at[x], grad.at[x], others[step - 1]).wait_recv()
    spread_all(0, (3, 5))
    spread_all(1, (3, 5))
    spread(3, 3, grad, 1, gz, own_z, near["sib"], z >= 0)
    pass_first((z == 0) & (y == 2))
    stats[...] = jnp.zeros_like(stats)

    ones = jnp.ones((8, HD), jnp.bfloat16)
    for block in range(BLK_DEV):
        for head in range(2):
            part = pl.ds(head * HD, HD)
            product = grad[block, :, part].astype(jnp.float32) * outv[block, :, part].astype(jnp.float32)
            high = product.astype(jnp.bfloat16)
            low = (product - high.astype(jnp.float32)).astype(jnp.bfloat16)
            total = dot(ones, high, NT) + dot(ones, low, NT)
            stats[block, pl.ds(2 + head, 1), :] = total[0:1]
            stats[block, pl.ds(head, 1), :] = (
                logsum[pl.ds(head, 1), pl.ds(block * BLOCK, BLOCK)] * LOG2E
            )
    go(18, stats, sy.at[four(own_y)], near["yr"])
    go(19, stats, sy.at[four(own_y)], near["yl"])
    go(34, stats, sz.at[four(own_z)], near["zr"])
    go(35, stats, sz.at[four(own_z)], near["zl"])
    go(36, stats, sz.at[four(own_z)], near["sib"])

    for copy in to_vmem[2:]:
        copy.wait()
    held = {0: kv, 1: vv, 2: qv, 3: grad}
    keep = [(held[(0, 1, 2, 3)[at]], z_set[at][1], z_set[at][2].at[four(own_z)]) for at in range(4)]
    keep += [(held[(2, 3, 0, 1)[at]], y_set[at][1], y_set[at][2].at[four(own_y)]) for at in range(4)]
    keep += [(stats, None, sz.at[four(own_z)]), (stats, None, sy.at[four(own_y)])]
    for index, (src, head, dst) in enumerate(keep):
        part = src if head is None else src.at[:, :, pl.ds(head * HD, HD)]
        kept.append(pltpu.make_async_copy(part, dst, local.at[16 + index]))
        kept[-1].start()
    scale = 1.0 / math.sqrt(HD)

    def own_block(block, carry):
        for head in range(2):
            part = pl.ds(head * HD, HD)
            k, v, q, g = kv[block, :, part], vv[block, :, part], qv[block, :, part], grad[block, :, part]
            lse = stats[block, pl.ds(head, 1), :]
            delta = stats[block, pl.ds(2 + head, 1), :]
            p = jnp.exp2(dot(k, q, NT) * (scale * LOG2E) - lse)
            key_at = lax.broadcasted_iota(jnp.int32, (BLOCK, BLOCK), 0)
            query_at = lax.broadcasted_iota(jnp.int32, (BLOCK, BLOCK), 1)
            p = jnp.where(key_at <= query_at, p, 0.0)
            ds = (p * (dot(v, g, NT) - delta)).astype(jnp.bfloat16)
            accv[block, :, part] = dot(p.astype(jnp.bfloat16), g, NN)
            acck[block, :, part] = dot(ds, q, NN) * scale
            accq[block, :, part] = dot(ds, k, TN) * scale
        return carry

    def first_block(block, carry):
        for head in range(2):
            part = pl.ds(head * HD, HD)
            k, v, q, g = fblk[0, :, part], fblk[1, :, part], qv[block, :, part], grad[block, :, part]
            lse = stats[block, pl.ds(head, 1), :]
            delta = stats[block, pl.ds(2 + head, 1), :]
            p = jnp.exp2(dot(k, q, NT) * (scale * LOG2E) - lse)
            ds = (p * (dot(v, g, NT) - delta)).astype(jnp.bfloat16)
            accf[1, :, part] += dot(p.astype(jnp.bfloat16), g, NN)
            accf[0, :, part] += dot(ds, q, NN) * scale
            accq[block, :, part] += dot(ds, k, TN) * scale
        return carry

    lax.fori_loop(0, BLK_DEV, own_block, 0)
    for index, (src, dst) in enumerate(((acck, own_k), (accv, own_v))):
        kept.append(pltpu.make_async_copy(src, dst, local.at[12 + index]))
        kept[-1].start()
    pass_first((z == 1) | (z == 3))

    def pieces(array):
        _, _, ref, way = (z_set + y_set)[array]
        if array < 4:
            at = (zl, zr, zo) if way == 0 else (zr, zl, zo)
            return ref, at, [column(one, c) for one in at], z_ways[way]
        at = (yl, yr, after(y, 2)) if way == 0 else (yr, yl, after(y, 2))
        return ref, at, [row(one) for one in at], y_ways[way]

    def onward(array, kind):
        ref, at, piece, way = pieces(array)
        came = sent(array, kind, at[kind])
        sends = [(2, way, sent(array, 2, at[0]))] if kind == 0 else []
        if array < 4:
            sends.append((4 + kind, near["sib"], came))
        relay(array, kind, ref, piece[kind], came, *sends)

    for array in (0, 1, 4, 7, 2, 6):
        onward(array, 0)
    sy_in = [sy.at[four(row(after(y, step)))] for step in (3, 1, 2)]
    sz_in = [sz.at[four(column(after(z, step), c))] for step in (3, 1, 2)]

    def stat_in(index, ref):
        remote(index, ref, ref, near["sib"]).wait_recv()

    stat_in(18, sy_in[0])
    go(22, sy_in[0], sy_in[0], near["yr"])
    stat_in(34, sz_in[0])
    go(37, sz_in[0], sz_in[0], near["zr"])
    go(38, sz_in[0], sz_in[0], near["sib"])
    for array in (3, 5):
        onward(array, 0)
    pass_first(z == 2)

    @pl.when(jnp.logical_not(root))
    def _():
        first_copy(1 - c, 32, 27, near["sib"]).wait_recv()

    accf[...] = jnp.zeros_like(accf)
    lax.fori_loop(jnp.where(root, 1, 0), BLK_DEV, first_block, 0)
    fout[...] = accf[...].astype(jnp.bfloat16)
    for index, (src, dst) in enumerate(((accq, own_q), (fout, own_f))):
        kept.append(pltpu.make_async_copy(src, dst, local.at[14 + index]))
        kept[-1].start()
    stat_in(35, sz_in[1])
    go(39, sz_in[1], sz_in[1], near["sib"])
    for kind in (1, 2):
        for array in (0, 1, 4, 7, 2, 6, 3, 5):
            onward(array, kind)
    stat_in(37, sz_in[2])
    go(40, sz_in[2], sz_in[2], near["sib"])
    stat_in(19, sy_in[1])
    stat_in(22, sy_in[2])
    for array in range(4):
        ref, at, _, _ = pieces(array)
        relay(array, 3, ref, column(z, 1 - c), z >= 0)
        for kind in range(3):
            relay(array, 4 + kind, ref, column(at[kind], 1 - c), sent(array, kind, at[kind]))
    for index, at in ((36, z), (38, zl), (39, zr), (40, zo)):
        stat_in(index, sz.at[four(column(at, 1 - c))])
    for copy in kept:
        copy.wait()
    for condition, copies in started_if:
        @pl.when(condition)
        def _(copies=copies):
            for copy in copies:
                copy.wait_send()

    for copy in started:
        copy.wait_send()

    @pl.when(root)
    def _():
        first_start.wait_send()

    for condition, copy in first_sends:
        @pl.when(condition)
        def _(copy=copy):
            copy.wait_send()


def choose(selected, z, y, c, head):
    row_at = lax.broadcasted_iota(jnp.int32, (32, 1), 0)
    group, core, block = row_at >> 3, (row_at >> 2) & 1, row_at & 3
    if head == 0:
        slab = selected[pl.ds(pl.multiple_of(z * 32, 32), 32), :]
    else:
        slab = jnp.concatenate(
            [selected[pl.ds(pl.multiple_of(at * 32 + y * 8, 8), 8), :] for at in range(4)], axis=0
        )
    lane = lax.broadcasted_iota(jnp.int32, (32, 128), 1)
    found = jnp.zeros((32, 128), jnp.int32)
    for pick in range(3):
        chosen = slab[:, pick : pick + 1]
        z_of, y_of, c_of, b_of = chosen >> 5, (chosen >> 3) & 3, (chosen >> 2) & 1, chosen & 3
        if head == 0:
            here = (chosen > 0) & (y_of == y) & (core == c)
            target = ((z_of * 2 + c_of) * 4 + b_of) * 4 + group
            value = 1 + group * 4 + block
        else:
            here = (chosen > 0) & (z_of == z) & (c_of == c)
            target = (y_of * 4 + b_of) * 8 + group * 2 + core
            value = 1 + (group * 2 + core) * 4 + block
        found += jnp.where(here & (lane == target), value, 0)
    table = jnp.sum(found, axis=0, keepdims=True)
    down = lax.broadcasted_iota(jnp.int32, (128, 128), 0)
    across = lax.broadcasted_iota(jnp.int32, (128, 128), 1)
    spread = jnp.broadcast_to(table, (128, 128))
    rank = jnp.sum(jnp.where((across < down) & (spread > 0), 1, 0), axis=1, keepdims=True)
    entry = jnp.sum(jnp.where(across == down, spread, 0), axis=1, keepdims=True)
    item = jnp.where(entry > 0, down[:, 0:1] * 128 + entry, 0)
    items = jnp.sum(jnp.where(rank == across, item, 0), axis=0, keepdims=True)
    return items, table


def pair_kernel(
    selected, kz, vz, qz, gz, qy, gy, ky, vy, sz, sy,
    pz, py,
    lists_v, lists, kbuf, vbuf, qbuf, gbuf, dq0, dq1, dkv, kvout, qout0, qout1, zero,
    list_sem, in_sem, out_sem, q_sem, zero_sem,
):
    z, y, c, _ = place()
    scale = 1.0 / math.sqrt(HD)
    for head in range(2):
        items, table = choose(selected, z, y, c, head)
        lists_v[pl.ds(2 * head, 1), :] = items
        lists_v[pl.ds(2 * head + 1, 1), :] = table
    listed = pltpu.make_async_copy(lists_v, lists, list_sem)
    listed.start()
    zero[...] = jnp.zeros_like(zero)
    dq0[...] = jnp.zeros_like(dq0)
    dq1[...] = jnp.zeros_like(dq1)
    listed.wait()

    class Part:
        pass

    parts = []
    for head in range(2):
        part = Part()
        part.head, part.per, part.slots = head, (4, 8)[head], (32, 16)[head]
        part.k, part.v, part.q, part.g = ((kz, vz, qy, gy), (ky, vy, qz, gz))[head]
        part.stat, part.dq, part.qout = ((sy, dq0, qout0), (sz, dq1, qout1))[head]
        part.out, part.at = ((pz, 0), (py, 1))[head]
        part.dq_out, part.dq_at = ((py, 0), (pz, 2))[head]
        parts.append(part)

    def item_of(part, at):
        item = lists[2 * part.head, at]
        return lax.div(item, 128 * part.per), lax.rem(item, 128) - 1, item

    def loads(part, at):
        slot, block, _ = item_of(part, at)
        side = lax.rem(at, 2)
        pairs = ((part.k, kbuf, slot), (part.v, vbuf, slot), (part.q, qbuf, block), (part.g, gbuf, block))
        return [
            pltpu.make_async_copy(
                src.at[where], buf.at[part.head, side], in_sem.at[part.head, side, index]
            )
            for index, (src, buf, where) in enumerate(pairs)
        ]

    for part in parts:
        @pl.when(lists[2 * part.head, 0] > 0)
        def _(part=part):
            for copy in loads(part, 0):
                copy.start()

    def idle(part, slot):
        total = lists[2 * part.head + 1, slot * part.per]
        for at in range(1, part.per):
            total += lists[2 * part.head + 1, slot * part.per + at]
        return total == 0

    def blank(part, slot):
        return pltpu.make_async_copy(
            zero, part.out.at[slot, pl.ds(part.at, 2)], zero_sem.at[part.head, slot]
        )

    def each_idle(part, act):
        def one(slot, carry):
            @pl.when(idle(part, slot))
            def _():
                act(blank(part, slot))
            return carry

        lax.fori_loop(0, part.slots, one, 0)

    for part in parts:
        each_idle(part, lambda copy: copy.start())

    def put(part, slot):
        return pltpu.make_async_copy(
            kvout.at[part.head], part.out.at[slot, pl.ds(part.at, 2)], out_sem.at[part.head]
        )

    def enter(part, at, opened):
        slot, _, _ = item_of(part, at)
        _, _, following = item_of(part, at + 1)

        @pl.when(following > 0)
        def _():
            for copy in loads(part, at + 1):
                copy.start()

        for copy in loads(part, at):
            copy.wait()

        @pl.when(slot != opened)
        def _():
            dkv[part.head] = jnp.zeros(dkv.shape[1:], dkv.dtype)

    def work(part, at):
        _, block, _ = item_of(part, at)
        side = lax.rem(at, 2)
        k, v = kbuf[part.head, side], vbuf[part.head, side]
        q, g = qbuf[part.head, side], gbuf[part.head, side]
        lse = part.stat[block, pl.ds(part.head, 1), :]
        delta = part.stat[block, pl.ds(2 + part.head, 1), :]
        p = jnp.exp2(dot(k, q, NT) * (scale * LOG2E) - lse)
        ds = (p * (dot(v, g, NT) - delta)).astype(jnp.bfloat16)
        dkv[part.head, 1] += dot(p.astype(jnp.bfloat16), g, NN)
        dkv[part.head, 0] += dot(ds, q, NN)
        part.dq[block] += dot(ds, k, TN)

    def leave(part, at, done):
        slot, _, _ = item_of(part, at)
        next_slot, _, following = item_of(part, at + 1)
        closing = (following == 0) | (next_slot != slot)

        @pl.when(closing)
        def _():
            @pl.when(done > 0)
            def _():
                put(part, 0).wait()
            kvout[part.head, 0] = (dkv[part.head, 0] * scale).astype(jnp.bfloat16)
            kvout[part.head, 1] = dkv[part.head, 1].astype(jnp.bfloat16)
            put(part, slot).start()

        return slot, done + jnp.where(closing, 1, 0)

    def both(state):
        at, opened0, done0, opened1, done1 = state
        enter(parts[0], at, opened0)
        enter(parts[1], at, opened1)
        work(parts[0], at)
        work(parts[1], at)
        return (at + 1,) + leave(parts[0], at, done0) + leave(parts[1], at, done1)

    none, nil = jnp.int32(-1), jnp.int32(0)
    at_both, *rest = lax.while_loop(
        lambda state: (lists[0, state[0]] > 0) & (lists[2, state[0]] > 0),
        both,
        (nil, none, nil, none, nil),
    )
    ends = []
    for part in parts:
        def one(state, part=part):
            at, opened, done = state
            enter(part, at, opened)
            work(part, at)
            return (at + 1,) + leave(part, at, done)

        _, _, done = lax.while_loop(
            lambda state, part=part: lists[2 * part.head, state[0]] > 0,
            one,
            (at_both, rest[2 * part.head], rest[2 * part.head + 1]),
        )
        ends.append(done)

        def flush(block, part=part):
            return pltpu.make_async_copy(
                part.qout.at[block], part.dq_out.at[block, part.dq_at], q_sem.at[part.head, block]
            )

        def finish(block, carry, part=part, flush=flush):
            part.qout[block] = (part.dq[block] * scale).astype(jnp.bfloat16)
            flush(block).start()
            return carry

        part.flush = flush
        part.blocks = (16, 32)[part.head]
        lax.fori_loop(0, part.blocks, finish, 0)

    for part in parts:
        @pl.when(ends[part.head] > 0)
        def _(part=part):
            put(part, 0).wait()

    for part in parts:
        def drain(block, carry, part=part):
            part.flush(block).wait()
            return carry

        lax.fori_loop(0, part.blocks, drain, 0)
        each_idle(part, lambda copy: copy.wait())


def scatter_kernel(
    pz, py, own_q, own_k, own_v, own_f,
    out_q, out_k, out_v,
    ownz, sibz, relz, finz, owny, rely, finy, accq, acck, accv,
    fown, frecv, fsum, fsend,
    send, recv, ring_send, ring_recv, local,
):
    z, y, c, x = place()
    near = neighbours(z, y, c, x)
    relz[...] = jnp.zeros_like(relz)
    finz[...] = jnp.zeros_like(finz)
    greet(list(near.values()))
    started = []
    started_if = []

    def remote(index, src, dst, target):
        return pltpu.make_async_remote_copy(
            src_ref=src, dst_ref=dst, send_sem=send.at[index], recv_sem=recv.at[index],
            device_id=target, device_id_type=MESH,
        )

    def go(index, src, dst, target):
        copy = remote(index, src, dst, target)
        copy.start()
        started.append(copy)

    def came(index, dst):
        remote(index, dst, dst, near["sib"]).wait_recv()

    def ring_copies(index, src, dst, target, groups):
        copies = []
        for at, (condition, first, size) in enumerate(groups):
            part = pl.ds(first, size)
            copies.append((condition, pltpu.make_async_remote_copy(
                src_ref=src.at[part], dst_ref=dst.at[part],
                send_sem=ring_send.at[index, at], recv_sem=ring_recv.at[index, at],
                device_id=target, device_id_type=MESH,
            )))
        return copies

    def ring_go(index, src, dst, target, groups):
        for condition, copy in ring_copies(index, src, dst, target, groups):
            @pl.when(condition)
            def _(copy=copy):
                copy.start()

            started_if.append((condition, copy))

    def ring_came(index, dst, groups):
        for condition, copy in ring_copies(index, dst, dst, near["sib"], groups):
            @pl.when(condition)
            def _(copy=copy):
                copy.wait_recv()

    def whole(_):
        return [(z >= 0, 0, 3)]

    def split(low, high):
        return [(low, 0, 2), (high, 2, 1)]

    y_kinds = {kind: whole for kind in ("far", "right", "left", "on_right", "on_left")}
    z_kinds = {
        "far": lambda at: split(at >= 2, at < 2),
        "right": lambda at: split(at == 3, at < 3),
        "left": lambda at: split(at > 0, at == 0),
        "on_right": lambda at: split((at == 0) | (at == 3), at < 3),
        "on_left": lambda at: split(at > 0, (at == 0) | (at == 3)),
    }

    def column(z_at, c_at):
        return pl.ds((z_at * 2 + c_at) * BLK_DEV, BLK_DEV)

    def local_copy(index, src, dst):
        copy = pltpu.make_async_copy(src, dst, local.at[index])
        copy.start()
        return copy

    hops = (2, 1, 3, 0)
    locals_z, locals_y = [], []
    for j, hop in enumerate(hops):
        go(j, pz.at[column(after(z, hop), 1 - c)], sibz.at[j], near["sib"])
        locals_z.append(local_copy(j, pz.at[column(after(z, hop), c)], ownz.at[j]))
        locals_y.append(
            local_copy(4 + j, py.at[pl.ds(after(y, hop) * BLK_DEV, BLK_DEV)], owny.at[j])
        )
        if j == 0:
            remote(20, own_f.at[1 - c], frecv.at[0], near["sib"]).start()
            mine_f = local_copy(8, own_f.at[c], fown)
    locals_own = [
        local_copy(9 + j, src, dst)
        for j, (src, dst) in enumerate(((own_q, accq), (own_k, acck), (own_v, accv)))
    ]

    def add(dst, src):
        for part in range(3):
            dst[part] = (dst[part].astype(jnp.float32) + src[part].astype(jnp.float32)).astype(
                jnp.bfloat16
            )

    def merge(j):
        locals_z[j].wait()
        came(j, sibz.at[j])

        def one(block, carry):
            add(ownz.at[j, block], sibz.at[j, block])
            return carry

        lax.fori_loop(0, BLK_DEV, one, 0)

    rings = (
        (0, ownz, relz, finz, near["zr"], near["zl"], z, z_kinds),
        (12, owny, rely, finy, near["yr"], near["yl"], y, y_kinds),
    )

    def ring_far(base, own, rel, fin, right, left, me, kinds):
        groups = kinds["far"](me)
        for block in range(2):
            ring_go(base + block, own.at[0, block], rel.at[0, block], right, groups)
            ring_go(base + 2 + block, own.at[0, 2 + block], rel.at[1, block], left, groups)

    def ring_right(base, own, rel, fin, right, left, me, kinds):
        for block in range(2, 4):
            ring_go(base + 2 + block, own.at[1, block], fin.at[0, block], right, kinds["right"](me))

    def ring_left(base, own, rel, fin, right, left, me, kinds):
        for block in range(2):
            ring_go(base + 6 + block, own.at[2, block], fin.at[1, block], left, kinds["left"](me))

    def ring_relay(base, own, rel, fin, right, left, me, kinds):
        before, behind = after(me, 3), after(me, 1)
        for block in range(2):
            ring_came(base + block, rel.at[0, block], kinds["far"](before))
            add(own.at[1, block], rel.at[0, block])
            ring_go(
                base + 8 + block, own.at[1, block], fin.at[0, block], right, kinds["on_right"](me)
            )
            ring_came(base + 2 + block, rel.at[1, block], kinds["far"](behind))
            add(own.at[2, 2 + block], rel.at[1, block])
            ring_go(
                base + 10 + block, own.at[2, 2 + block], fin.at[1, 2 + block], left,
                kinds["on_left"](me),
            )

    def ring_end(base, own, rel, fin, right, left, me, kinds):
        before, behind = after(me, 3), after(me, 1)
        for block in range(2):
            ring_came(base + 4 + block, fin.at[0, 2 + block], kinds["right"](before))
            ring_came(base + 6 + block, fin.at[1, block], kinds["left"](behind))
            ring_came(base + 8 + block, fin.at[0, block], kinds["on_right"](before))
            ring_came(base + 10 + block, fin.at[1, 2 + block], kinds["on_left"](behind))

    locals_y[0].wait()
    ring_far(*rings[1])
    merge(0)
    ring_far(*rings[0])

    f_sends = [
        ((y == 2) | (y == 1), remote(21, fsend.at[0], frecv.at[1], near["yl"])),
        (y == 3, remote(22, fsend.at[0], frecv.at[2], near["yr"])),
        ((y == 0) & ((z == 2) | (z == 1)), remote(23, fsend.at[1], frecv.at[3], near["zl"])),
        ((y == 0) & (z == 3), remote(24, fsend.at[1], frecv.at[4], near["zr"])),
    ]

    def f_take(at):
        came(20 + at, frecv.at[at])
        fsum[...] += frecv[at].astype(jnp.float32)

    def f_send(at):
        condition, copy = f_sends[at]

        @pl.when(condition)
        def _():
            fsend[at // 2] = fsum[...].astype(jnp.bfloat16)
            copy.start()

    mine_f.wait()
    came(20, frecv.at[0])
    fsum[...] = fown[...].astype(jnp.float32) + frecv[0].astype(jnp.float32)

    @pl.when(y == 1)
    def _():
        f_take(1)

    f_send(0)
    f_send(1)

    locals_y[1].wait()
    ring_right(*rings[1])
    locals_y[2].wait()
    ring_left(*rings[1])
    merge(1)
    ring_right(*rings[0])
    merge(2)
    ring_left(*rings[0])

    @pl.when(y == 0)
    def _():
        f_take(1)
        f_take(2)

        @pl.when(z == 1)
        def _():
            f_take(3)

    f_send(2)
    f_send(3)

    merge(3)
    ring_relay(*rings[0])
    ring_relay(*rings[1])
    top = (z == 0) & (y == 0)

    @pl.when(top)
    def _():
        f_take(3)
        f_take(4)

    locals_y[3].wait()
    for copy in locals_own:
        copy.wait()

    @pl.when(top & (c == 1))
    def _():
        fsend[1] = fsum[...].astype(jnp.bfloat16)
        remote(25, fsend.at[1], frecv.at[5], near["sib"]).start()

    @pl.when(top & (c == 0))
    def _():
        came(25, frecv.at[5])
        acck[0] += fsum[...]
        accv[0] += frecv[5].astype(jnp.float32)

    def total(own, fin, places):
        def one(block, carry):
            for part, (acc, out, head) in enumerate(places):
                lanes = pl.ds(head * HD, HD)
                value = acc[block, :, lanes]
                for ref in (own.at[3], fin.at[0], fin.at[1]):
                    value += ref[block, part].astype(jnp.float32)
                out[block, :, lanes] = value.astype(jnp.bfloat16)
            return carry

        lax.fori_loop(0, BLK_DEV, one, 0)

    ring_end(*rings[0])
    total(ownz, finz, ((acck, out_k, 0), (accv, out_v, 0), (accq, out_q, 1)))
    ring_end(*rings[1])
    total(owny, finy, ((accq, out_q, 0), (acck, out_k, 1), (accv, out_v, 1)))

    for condition, copy in started_if:
        @pl.when(condition)
        def _(copy=copy):
            copy.wait_send()

    for copy in started:
        copy.wait_send()
    remote(20, fown, frecv.at[0], near["sib"]).wait_send()
    for condition, copy in f_sends + [
        (top & (c == 1), remote(25, fsend.at[1], frecv.at[5], near["sib"]))
    ]:
        @pl.when(condition)
        def _(copy=copy):
            copy.wait_send()


def keep_kernel(in_q, in_k, in_v, out_q, out_k, out_v, held, in_sem, out_sem):
    ins, outs = [], []
    for part, (src, dst) in enumerate(((in_q, out_q), (in_k, out_k), (in_v, out_v))):
        for half in range(2):
            piece = pl.ds(2 * half, 2)
            ins.append(
                pltpu.make_async_copy(src.at[piece], held.at[part, piece], in_sem.at[part, half])
            )
            outs.append(
                pltpu.make_async_copy(held.at[part, piece], dst.at[piece], out_sem.at[part, half])
            )
    for copy in ins:
        copy.start()
    for copy, out in zip(ins, outs):
        copy.wait()
        out.start()
    for out in outs:
        out.wait()


def body(query, keys, values, output, d_out, row_logsum, selected):
    bf16, f32 = jnp.bfloat16, jnp.float32
    any_spec = pl.BlockSpec(memory_space=pl.ANY)
    vmem_spec = pl.BlockSpec(memory_space=pltpu.VMEM)
    smem_spec = pl.BlockSpec(memory_space=pltpu.SMEM)
    blocked = (BLK_DEV, BLOCK, WIDTH)
    shape = jax.ShapeDtypeStruct
    dma, vmem, smem = pltpu.SemaphoreType.DMA, pltpu.VMEM, pltpu.SMEM
    zs, ys = shape((32, BLOCK, HD), bf16), shape((16, BLOCK, HD), bf16)
    kz, vz, qz, gz, sz, qy, gy, ky, vy, sy, own_q, own_k, own_v, own_f = pl.pallas_call(
        gather_kernel,
        out_shape=[zs] * 4
        + [shape((32, 8, BLOCK), f32)]
        + [ys] * 4
        + [shape((16, 8, BLOCK), f32)]
        + [shape(blocked, f32)] * 3
        + [shape((2, BLOCK, WIDTH), bf16)],
        in_specs=[any_spec] * 5 + [vmem_spec],
        out_specs=[any_spec] * 14,
        scratch_shapes=[vmem(blocked, bf16)] * 5
        + [vmem((BLK_DEV, 8, BLOCK), f32)]
        + [vmem(blocked, f32)] * 3
        + [
            vmem((2, BLOCK, WIDTH), bf16),
            vmem((2, BLOCK, WIDTH), f32),
            vmem((2, BLOCK, WIDTH), bf16),
            dma((41,)),
            dma((41,)),
            dma((56, 2)),
            dma((56, 2)),
            dma((26,)),
        ],
        compiler_params=pltpu.CompilerParams(
            collective_id=0, has_side_effects=True, vmem_limit_bytes=VMEM
        ),
        name="gather",
    )(
        keys.reshape(blocked), values.reshape(blocked), query.reshape(blocked),
        d_out, output.reshape(blocked), row_logsum,
    )
    pz, py = pl.pallas_call(
        pair_kernel,
        out_shape=[shape((32, 3, BLOCK, HD), bf16), shape((16, 3, BLOCK, HD), bf16)],
        in_specs=[vmem_spec] + [any_spec] * 8 + [vmem_spec] * 2,
        out_specs=[any_spec] * 2,
        scratch_shapes=[
            vmem((8, 128), jnp.int32),
            smem((8, 128), jnp.int32),
            vmem((2, 2, BLOCK, HD), bf16),
            vmem((2, 2, BLOCK, HD), bf16),
            vmem((2, 2, BLOCK, HD), bf16),
            vmem((2, 2, BLOCK, HD), bf16),
            vmem((16, BLOCK, HD), f32),
            vmem((32, BLOCK, HD), f32),
            vmem((2, 2, BLOCK, HD), f32),
            vmem((2, 2, BLOCK, HD), bf16),
            vmem((16, BLOCK, HD), bf16),
            vmem((32, BLOCK, HD), bf16),
            vmem((2, BLOCK, HD), bf16),
            dma,
            dma((2, 2, 4)),
            dma((2,)),
            dma((2, 32)),
            dma((2, 32)),
        ],
        compiler_params=pltpu.CompilerParams(vmem_limit_bytes=VMEM),
        name="pairs",
    )(selected, kz, vz, qz, gz, qy, gy, ky, vy, sz, sy)
    piece = (BLK_DEV, 3, BLOCK, HD)
    out_q, out_k, out_v = pl.pallas_call(
        scatter_kernel,
        out_shape=[shape(blocked, bf16)] * 3,
        in_specs=[any_spec] * 6,
        out_specs=[vmem_spec] * 3,
        scratch_shapes=[
            vmem((4,) + piece, bf16),
            vmem((4,) + piece, bf16),
            vmem((2, 2, 3, BLOCK, HD), bf16),
            vmem((2,) + piece, bf16),
            vmem((4,) + piece, bf16),
            vmem((2, 2, 3, BLOCK, HD), bf16),
            vmem((2,) + piece, bf16),
            vmem(blocked, f32),
            vmem(blocked, f32),
            vmem(blocked, f32),
            vmem((BLOCK, WIDTH), bf16),
            vmem((6, BLOCK, WIDTH), bf16),
            vmem((BLOCK, WIDTH), f32),
            vmem((2, BLOCK, WIDTH), bf16),
            dma((26,)),
            dma((26,)),
            dma((24, 2)),
            dma((24, 2)),
            dma((12,)),
        ],
        compiler_params=pltpu.CompilerParams(
            collective_id=1, has_side_effects=True, vmem_limit_bytes=VMEM
        ),
        name="scatter",
    )(pz, py, own_q, own_k, own_v, own_f)
    out_q, out_k, out_v = pl.pallas_call(
        keep_kernel,
        out_shape=[shape(blocked, bf16)] * 3,
        in_specs=[any_spec] * 3,
        out_specs=[any_spec] * 3,
        scratch_shapes=[vmem((3,) + blocked, bf16), dma((3, 2)), dma((3, 2))],
        compiler_params=pltpu.CompilerParams(vmem_limit_bytes=VMEM),
        name="keep",
    )(out_q, out_k, out_v)
    flat = (BLK_DEV * BLOCK, WIDTH)
    return out_q.reshape(flat), out_k.reshape(flat), out_v.reshape(flat)


def solution(mesh):
    in_specs = (
        P("seq", "head"),
        P("seq", "head"),
        P("seq", "head"),
        P("seq", "head"),
        P(("seq", "head"), None),
        P("head", "seq"),
        P(),
    )
    out_specs = (P("seq", "head"), P("seq", "head"), P("seq", "head"))
    return jax.shard_map(body, mesh=mesh, in_specs=in_specs, out_specs=out_specs, check_vma=False)
```

```python
import functools
import math

import jax
import jax.numpy as jnp
from jax import lax
from jax.experimental import pallas as pl
from jax.experimental.pallas import tpu as pltpu
from jax.sharding import PartitionSpec as P

MESH = pl.DeviceIdType.MESH
BLOCK = 512
HD = 128
WIDTH = 256
BLK_DEV = 4
RING = 4
NSLOT = 32
LOG2E = math.log2(math.e)
VMEM = 60 * 1024 * 1024


def place():
    seq = lax.axis_index("seq")
    return lax.div(seq, 8), lax.rem(lax.div(seq, 2), 4), lax.rem(seq, 2), lax.axis_index("head")


def device(z, y, c, x):
    return ((z * 4 + y) * 2 + c, x)


def after(index, step):
    return lax.rem(index + step, RING)


def neighbours(z, y, c, x):
    return {
        "sib": device(z, y, 1 - c, x),
        "zr": device(after(z, 1), y, c, x),
        "zl": device(after(z, 3), y, c, x),
        "yr": device(z, after(y, 1), c, x),
        "yl": device(z, after(y, 3), c, x),
    }


def greet(devices):
    barrier = pltpu.get_barrier_semaphore()
    for target in devices:
        pl.semaphore_signal(barrier, inc=1, device_id=target, device_id_type=MESH)
    pl.semaphore_wait(barrier, len(devices))


NT = (((1,), (1,)), ((), ()))
NN = (((1,), (0,)), ((), ()))
TN = (((0,), (0,)), ((), ()))


def dot(a, b, dims):
    return lax.dot_general(a, b, dims, preferred_element_type=jnp.float32)


def gather_kernel(
    keys, values, query, d_out, output, logsum,
    kz, vz, qz, gz, sz, qy, gy, ky, vy, sy, own_q, own_k, own_v, own_f,
    grad, outv, kv, vv, qv, stats, accq, acck, accv, fblk, accf, fout,
    send, recv, bulk_send, bulk_recv, local,
):
    z, y, c, x = place()
    near = neighbours(z, y, c, x)
    others = [((z * 4 + y) * 2 + c, after(x, step)) for step in (1, 2, 3)]
    greet(list(near.values()) + others)
    started = []

    def remote(index, src, dst, target):
        return pltpu.make_async_remote_copy(
            src_ref=src, dst_ref=dst, send_sem=send.at[index], recv_sem=recv.at[index],
            device_id=target, device_id_type=MESH,
        )

    def go(index, src, dst, target):
        copy = remote(index, src, dst, target)
        copy.start()
        started.append(copy)

    def bulk(array, kind, chunk, src, dst, target):
        return pltpu.make_async_remote_copy(
            src_ref=src, dst_ref=dst,
            send_sem=bulk_send.at[array * 7 + kind, chunk],
            recv_sem=bulk_recv.at[array * 7 + kind, chunk],
            device_id=target, device_id_type=MESH,
        )

    started_if = []

    def start_if(condition, copies):
        @pl.when(condition)
        def _():
            for copy in copies:
                copy.start()

        started_if.append((condition, copies))

    def spread(array, kind, src, head, dst, piece, target, condition):
        start_if(condition, [
            bulk(
                array, kind, chunk,
                src.at[pl.ds(2 * chunk, 2), :, pl.ds(head * HD, HD)],
                dst.at[pl.ds(piece + 2 * chunk, 2)],
                target,
            )
            for chunk in range(2)
        ])

    def relay(array, kind, ref, piece, condition, *onward):
        for chunk in range(2):
            at = ref.at[pl.ds(piece + 2 * chunk, 2)]

            @pl.when(condition)
            def _(at=at, chunk=chunk):
                bulk(array, kind, chunk, at, at, near["sib"]).wait_recv()

            for kind_on, target, condition_on in onward:
                start_if(condition_on, [bulk(array, kind_on, chunk, at, at, target)])

    def column(z_at, c_at):
        return (z_at * 2 + c_at) * BLK_DEV

    def row(y_at):
        return y_at * BLK_DEV

    def four(start):
        return pl.ds(start, BLK_DEV)

    zl, zr, zo = after(z, 3), after(z, 1), after(z, 2)
    yl, yr = after(y, 3), after(y, 1)
    top = (z == 0) & (y == 0)
    root = top & (c == 0)

    first_own = [
        pltpu.make_async_copy(keys.at[0], fblk.at[0], local.at[0]),
        pltpu.make_async_copy(values.at[0], fblk.at[1], local.at[1]),
    ]

    def first_copy(part, send_at, recv_at, target):
        return pltpu.make_async_remote_copy(
            src_ref=fblk.at[part], dst_ref=fblk.at[part],
            send_sem=send.at[send_at], recv_sem=recv.at[recv_at],
            device_id=target, device_id_type=MESH,
        )

    first_sends = [
        ((z == 0) & (y <= 1), first_copy(c, 28, 26, near["yr"])),
        ((z == 0) & (y == 0), first_copy(c, 29, 26, near["yl"])),
        (z <= 1, first_copy(c, 30, 26, near["zr"])),
        (z == 0, first_copy(c, 31, 26, near["zl"])),
        (jnp.logical_not(top & (c == 1)), first_copy(c, 32, 27, near["sib"])),
    ]
    first_start = first_copy(1, 33, 26, near["sib"])

    def send_first():
        for condition, copy in first_sends:
            @pl.when(condition)
            def _(copy=copy):
                copy.start()

    def pass_first(condition):
        @pl.when(condition)
        def _():
            first_copy(c, 28, 26, near["sib"]).wait_recv()
            send_first()

    @pl.when(root)
    def _():
        for copy in first_own:
            copy.start()
        for copy in first_own:
            copy.wait()
        first_start.start()
        send_first()

    pass_first(top & (c == 1))

    for step in (1, 2, 3):
        to = after(x, step)
        go(
            22 + step,
            d_out.at[:, pl.ds(pl.multiple_of(to * WIDTH, WIDTH), WIDTH)],
            grad.at[x],
            others[step - 1],
        )
    to_vmem = [
        pltpu.make_async_copy(
            d_out.at[:, pl.ds(pl.multiple_of(x * WIDTH, WIDTH), WIDTH)], grad.at[x], local.at[2]
        ),
        pltpu.make_async_copy(output, outv, local.at[3]),
        pltpu.make_async_copy(keys, kv, local.at[4]),
        pltpu.make_async_copy(values, vv, local.at[5]),
        pltpu.make_async_copy(query, qv, local.at[6]),
    ]
    kept = []
    for copy in to_vmem:
        copy.start()

    own_z, own_y = column(z, c), row(y)
    z_set = ((keys, 0, kz, 0), (values, 0, vz, 1), (query, 1, qz, 0), (grad, 1, gz, 1))
    y_set = ((query, 0, qy, 0), (grad, 0, gy, 1), (keys, 1, ky, 0), (values, 1, vy, 1))
    z_ways, y_ways = (near["zr"], near["zl"]), (near["yr"], near["yl"])

    def wanted(array, src, dst):
        if array < 2:
            return dst > src
        if array < 4:
            return dst < src
        if array < 6:
            return (dst < src) | (z > 0)
        return (dst > src) | (z < 3)

    def sent(array, kind, src):
        way = (z_set + y_set)[array][3]
        step = (1, 3)[way]
        if kind == 0:
            return wanted(array, src, after(src, step)) | wanted(array, src, after(src, 2))
        if kind == 1:
            return wanted(array, src, after(src, 4 - step))
        return wanted(array, src, after(src, 2))

    def spread_all(kind, arrays):
        for array in arrays:
            src, head, ref, way = (z_set + y_set)[array]
            piece, at, ways = (own_z, z, z_ways) if array < 4 else (own_y, y, y_ways)
            spread(
                array, kind, src, head, ref, piece, ways[(way + kind) % 2], sent(array, kind, at)
            )

    spread_all(0, (0, 1, 4, 7, 2, 6))
    spread_all(1, (0, 1, 4, 7, 2, 6))
    for array in (0, 1, 2):
        src, head, ref, _ = z_set[array]
        spread(array, 3, src, head, ref, own_z, near["sib"], z >= 0)

    pass_first((z == 0) & ((y == 1) | (y == 3)))
    to_vmem[0].wait()
    to_vmem[1].wait()
    for step in (1, 2, 3):
        remote(22 + step, grad.at[x], grad.at[x], others[step - 1]).wait_recv()
    spread_all(0, (3, 5))
    spread_all(1, (3, 5))
    spread(3, 3, grad, 1, gz, own_z, near["sib"], z >= 0)
    pass_first((z == 0) & (y == 2))
    stats[...] = jnp.zeros_like(stats)

    ones = jnp.ones((8, HD), jnp.bfloat16)
    for block in range(BLK_DEV):
        for head in range(2):
            part = pl.ds(head * HD, HD)
            product = grad[block, :, part].astype(jnp.float32) * outv[block, :, part].astype(jnp.float32)
            high = product.astype(jnp.bfloat16)
            low = (product - high.astype(jnp.float32)).astype(jnp.bfloat16)
            total = dot(ones, high, NT) + dot(ones, low, NT)
            stats[block, pl.ds(2 + head, 1), :] = total[0:1]
            stats[block, pl.ds(head, 1), :] = (
                logsum[pl.ds(head, 1), pl.ds(block * BLOCK, BLOCK)] * LOG2E
            )
    go(18, stats, sy.at[four(own_y)], near["yr"])
    go(19, stats, sy.at[four(own_y)], near["yl"])
    go(34, stats, sz.at[four(own_z)], near["zr"])
    go(35, stats, sz.at[four(own_z)], near["zl"])
    go(36, stats, sz.at[four(own_z)], near["sib"])

    for copy in to_vmem[2:]:
        copy.wait()
    held = {0: kv, 1: vv, 2: qv, 3: grad}
    keep = [(held[(0, 1, 2, 3)[at]], z_set[at][1], z_set[at][2].at[four(own_z)]) for at in range(4)]
    keep += [(held[(2, 3, 0, 1)[at]], y_set[at][1], y_set[at][2].at[four(own_y)]) for at in range(4)]
    keep += [(stats, None, sz.at[four(own_z)]), (stats, None, sy.at[four(own_y)])]
    for index, (src, head, dst) in enumerate(keep):
        part = src if head is None else src.at[:, :, pl.ds(head * HD, HD)]
        kept.append(pltpu.make_async_copy(part, dst, local.at[16 + index]))
        kept[-1].start()
    scale = 1.0 / math.sqrt(HD)

    def own_block(block, carry):
        for head in range(2):
            part = pl.ds(head * HD, HD)
            k, v, q, g = kv[block, :, part], vv[block, :, part], qv[block, :, part], grad[block, :, part]
            lse = stats[block, pl.ds(head, 1), :]
            delta = stats[block, pl.ds(2 + head, 1), :]
            p = jnp.exp2(dot(k, q, NT) * (scale * LOG2E) - lse)
            key_at = lax.broadcasted_iota(jnp.int32, (BLOCK, BLOCK), 0)
            query_at = lax.broadcasted_iota(jnp.int32, (BLOCK, BLOCK), 1)
            p = jnp.where(key_at <= query_at, p, 0.0)
            ds = (p * (dot(v, g, NT) - delta)).astype(jnp.bfloat16)
            accv[block, :, part] = dot(p.astype(jnp.bfloat16), g, NN)
            acck[block, :, part] = dot(ds, q, NN) * scale
            accq[block, :, part] = dot(ds, k, TN) * scale
        return carry

    def first_block(block, carry):
        for head in range(2):
            part = pl.ds(head * HD, HD)
            k, v, q, g = fblk[0, :, part], fblk[1, :, part], qv[block, :, part], grad[block, :, part]
            lse = stats[block, pl.ds(head, 1), :]
            delta = stats[block, pl.ds(2 + head, 1), :]
            p = jnp.exp2(dot(k, q, NT) * (scale * LOG2E) - lse)
            ds = (p * (dot(v, g, NT) - delta)).astype(jnp.bfloat16)
            accf[1, :, part] += dot(p.astype(jnp.bfloat16), g, NN)
            accf[0, :, part] += dot(ds, q, NN) * scale
            accq[block, :, part] += dot(ds, k, TN) * scale
        return carry

    lax.fori_loop(0, BLK_DEV, own_block, 0)
    for index, (src, dst) in enumerate(((acck, own_k), (accv, own_v))):
        kept.append(pltpu.make_async_copy(src, dst, local.at[12 + index]))
        kept[-1].start()
    pass_first((z == 1) | (z == 3))

    def pieces(array):
        _, _, ref, way = (z_set + y_set)[array]
        if array < 4:
            at = (zl, zr, zo) if way == 0 else (zr, zl, zo)
            return ref, at, [column(one, c) for one in at], z_ways[way]
        at = (yl, yr, after(y, 2)) if way == 0 else (yr, yl, after(y, 2))
        return ref, at, [row(one) for one in at], y_ways[way]

    def onward(array, kind):
        ref, at, piece, way = pieces(array)
        came = sent(array, kind, at[kind])
        sends = [(2, way, sent(array, 2, at[0]))] if kind == 0 else []
        if array < 4:
            sends.append((4 + kind, near["sib"], came))
        relay(array, kind, ref, piece[kind], came, *sends)

    for array in (0, 1, 4, 7, 2, 6):
        onward(array, 0)
    sy_in = [sy.at[four(row(after(y, step)))] for step in (3, 1, 2)]
    sz_in = [sz.at[four(column(after(z, step), c))] for step in (3, 1, 2)]

    def stat_in(index, ref):
        remote(index, ref, ref, near["sib"]).wait_recv()

    stat_in(18, sy_in[0])
    go(22, sy_in[0], sy_in[0], near["yr"])
    stat_in(34, sz_in[0])
    go(37, sz_in[0], sz_in[0], near["zr"])
    go(38, sz_in[0], sz_in[0], near["sib"])
    for array in (3, 5):
        onward(array, 0)
    pass_first(z == 2)

    @pl.when(jnp.logical_not(root))
    def _():
        first_copy(1 - c, 32, 27, near["sib"]).wait_recv()

    accf[...] = jnp.zeros_like(accf)
    lax.fori_loop(jnp.where(root, 1, 0), BLK_DEV, first_block, 0)
    fout[...] = accf[...].astype(jnp.bfloat16)
    for index, (src, dst) in enumerate(((accq, own_q), (fout, own_f))):
        kept.append(pltpu.make_async_copy(src, dst, local.at[14 + index]))
        kept[-1].start()
    stat_in(35, sz_in[1])
    go(39, sz_in[1], sz_in[1], near["sib"])
    for kind in (1, 2):
        for array in (0, 1, 4, 7, 2, 6, 3, 5):
            onward(array, kind)
    stat_in(37, sz_in[2])
    go(40, sz_in[2], sz_in[2], near["sib"])
    stat_in(19, sy_in[1])
    stat_in(22, sy_in[2])
    for array in range(4):
        ref, at, _, _ = pieces(array)
        relay(array, 3, ref, column(z, 1 - c), z >= 0)
        for kind in range(3):
            relay(array, 4 + kind, ref, column(at[kind], 1 - c), sent(array, kind, at[kind]))
    for index, at in ((36, z), (38, zl), (39, zr), (40, zo)):
        stat_in(index, sz.at[four(column(at, 1 - c))])
    for copy in kept:
        copy.wait()
    for condition, copies in started_if:
        @pl.when(condition)
        def _(copies=copies):
            for copy in copies:
                copy.wait_send()

    for copy in started:
        copy.wait_send()

    @pl.when(root)
    def _():
        first_start.wait_send()

    for condition, copy in first_sends:
        @pl.when(condition)
        def _(copy=copy):
            copy.wait_send()


def choose(selected, z, y, c, head):
    row_at = lax.broadcasted_iota(jnp.int32, (32, 1), 0)
    group, core, block = row_at >> 3, (row_at >> 2) & 1, row_at & 3
    if head == 0:
        token_block = row_at + z * 32
    else:
        token_block = group * 32 + y * 8 + (row_at & 7)
    lane = lax.broadcasted_iota(jnp.int32, (32, 128), 1)
    found = jnp.zeros((32, 128), jnp.int32)
    for pick in range(3):
        row = selected[pl.ds(pick, 1), :]
        chosen = jnp.sum(jnp.where(lane == token_block, row, 0), axis=1, keepdims=True)
        z_of, y_of, c_of, b_of = chosen >> 5, (chosen >> 3) & 3, (chosen >> 2) & 1, chosen & 3
        if head == 0:
            here = (chosen > 0) & (y_of == y) & (core == c)
            target = ((z_of * 2 + c_of) * 4 + b_of) * 4 + group
            value = 1 + group * 4 + block
        else:
            here = (chosen > 0) & (z_of == z) & (c_of == c)
            target = (y_of * 4 + b_of) * 8 + group * 2 + core
            value = 1 + (group * 2 + core) * 4 + block
        found += jnp.where(here & (lane == target), value, 0)
    table = jnp.sum(found, axis=0, keepdims=True)
    down = lax.broadcasted_iota(jnp.int32, (128, 128), 0)
    across = lax.broadcasted_iota(jnp.int32, (128, 128), 1)
    spread = jnp.broadcast_to(table, (128, 128))
    rank = jnp.sum(jnp.where((across < down) & (spread > 0), 1, 0), axis=1, keepdims=True)
    entry = jnp.sum(jnp.where(across == down, spread, 0), axis=1, keepdims=True)
    item = jnp.where(entry > 0, down[:, 0:1] * 128 + entry, 0)
    items = jnp.sum(jnp.where(rank == across, item, 0), axis=0, keepdims=True)
    return items, table


def pair_kernel(
    selected, kz, vz, qz, gz, qy, gy, ky, vy, sz, sy,
    pz, py,
    lists_v, lists, kbuf, vbuf, qbuf, gbuf, dq0, dq1, dkv, kvout, qout0, qout1, zero,
    list_sem, in_sem, out_sem, q_sem, zero_sem,
):
    z, y, c, _ = place()
    scale = 1.0 / math.sqrt(HD)
    for head in range(2):
        items, table = choose(selected, z, y, c, head)
        lists_v[pl.ds(2 * head, 1), :] = items
        lists_v[pl.ds(2 * head + 1, 1), :] = table
    listed = pltpu.make_async_copy(lists_v, lists, list_sem)
    listed.start()
    zero[...] = jnp.zeros_like(zero)
    dq0[...] = jnp.zeros_like(dq0)
    dq1[...] = jnp.zeros_like(dq1)
    listed.wait()

    class Part:
        pass

    parts = []
    for head in range(2):
        part = Part()
        part.head, part.per, part.slots = head, (4, 8)[head], (32, 16)[head]
        part.k, part.v, part.q, part.g = ((kz, vz, qy, gy), (ky, vy, qz, gz))[head]
        part.stat, part.dq, part.qout = ((sy, dq0, qout0), (sz, dq1, qout1))[head]
        part.out, part.at = ((pz, 0), (py, 1))[head]
        part.dq_out, part.dq_at = ((py, 0), (pz, 2))[head]
        parts.append(part)

    def item_of(part, at):
        item = lists[2 * part.head, at]
        return lax.div(item, 128 * part.per), lax.rem(item, 128) - 1, item

    def loads(part, at):
        slot, block, _ = item_of(part, at)
        side = lax.rem(at, 2)
        pairs = ((part.k, kbuf, slot), (part.v, vbuf, slot), (part.q, qbuf, block), (part.g, gbuf, block))
        return [
            pltpu.make_async_copy(
                src.at[where], buf.at[part.head, side], in_sem.at[part.head, side, index]
            )
            for index, (src, buf, where) in enumerate(pairs)
        ]

    for part in parts:
        @pl.when(lists[2 * part.head, 0] > 0)
        def _(part=part):
            for copy in loads(part, 0):
                copy.start()

    def idle(part, slot):
        total = lists[2 * part.head + 1, slot * part.per]
        for at in range(1, part.per):
            total += lists[2 * part.head + 1, slot * part.per + at]
        return total == 0

    def blank(part, slot):
        return pltpu.make_async_copy(
            zero, part.out.at[slot, pl.ds(part.at, 2)], zero_sem.at[part.head, slot]
        )

    def each_idle(part, act):
        def one(slot, carry):
            @pl.when(idle(part, slot))
            def _():
                act(blank(part, slot))
            return carry

        lax.fori_loop(0, part.slots, one, 0)

    for part in parts:
        each_idle(part, lambda copy: copy.start())

    def put(part, slot):
        return pltpu.make_async_copy(
            kvout.at[part.head], part.out.at[slot, pl.ds(part.at, 2)], out_sem.at[part.head]
        )

    def enter(part, at, opened):
        slot, _, _ = item_of(part, at)
        _, _, following = item_of(part, at + 1)

        @pl.when(following > 0)
        def _():
            for copy in loads(part, at + 1):
                copy.start()

        for copy in loads(part, at):
            copy.wait()

        @pl.when(slot != opened)
        def _():
            dkv[part.head] = jnp.zeros(dkv.shape[1:], dkv.dtype)

    def work(part, at):
        _, block, _ = item_of(part, at)
        side = lax.rem(at, 2)
        k, v = kbuf[part.head, side], vbuf[part.head, side]
        q, g = qbuf[part.head, side], gbuf[part.head, side]
        lse = part.stat[block, pl.ds(part.head, 1), :]
        delta = part.stat[block, pl.ds(2 + part.head, 1), :]
        p = jnp.exp2(dot(k, q, NT) * (scale * LOG2E) - lse)
        ds = (p * (dot(v, g, NT) - delta)).astype(jnp.bfloat16)
        dkv[part.head, 1] += dot(p.astype(jnp.bfloat16), g, NN)
        dkv[part.head, 0] += dot(ds, q, NN)
        part.dq[block] += dot(ds, k, TN)

    def leave(part, at, done):
        slot, _, _ = item_of(part, at)
        next_slot, _, following = item_of(part, at + 1)
        closing = (following == 0) | (next_slot != slot)

        @pl.when(closing)
        def _():
            @pl.when(done > 0)
            def _():
                put(part, 0).wait()
            kvout[part.head, 0] = (dkv[part.head, 0] * scale).astype(jnp.bfloat16)
            kvout[part.head, 1] = dkv[part.head, 1].astype(jnp.bfloat16)
            put(part, slot).start()

        return slot, done + jnp.where(closing, 1, 0)

    def both(state):
        at, opened0, done0, opened1, done1 = state
        enter(parts[0], at, opened0)
        enter(parts[1], at, opened1)
        work(parts[0], at)
        work(parts[1], at)
        return (at + 1,) + leave(parts[0], at, done0) + leave(parts[1], at, done1)

    none, nil = jnp.int32(-1), jnp.int32(0)
    at_both, *rest = lax.while_loop(
        lambda state: (lists[0, state[0]] > 0) & (lists[2, state[0]] > 0),
        both,
        (nil, none, nil, none, nil),
    )
    ends = []
    for part in parts:
        def one(state, part=part):
            at, opened, done = state
            enter(part, at, opened)
            work(part, at)
            return (at + 1,) + leave(part, at, done)

        _, _, done = lax.while_loop(
            lambda state, part=part: lists[2 * part.head, state[0]] > 0,
            one,
            (at_both, rest[2 * part.head], rest[2 * part.head + 1]),
        )
        ends.append(done)

        def flush(block, part=part):
            return pltpu.make_async_copy(
                part.qout.at[block], part.dq_out.at[block, part.dq_at], q_sem.at[part.head, block]
            )

        def finish(block, carry, part=part, flush=flush):
            part.qout[block] = (part.dq[block] * scale).astype(jnp.bfloat16)
            flush(block).start()
            return carry

        part.flush = flush
        part.blocks = (16, 32)[part.head]
        lax.fori_loop(0, part.blocks, finish, 0)

    for part in parts:
        @pl.when(ends[part.head] > 0)
        def _(part=part):
            put(part, 0).wait()

    for part in parts:
        def drain(block, carry, part=part):
            part.flush(block).wait()
            return carry

        lax.fori_loop(0, part.blocks, drain, 0)
        each_idle(part, lambda copy: copy.wait())


def scatter_kernel(
    pz, py, own_q, own_k, own_v, own_f,
    out_q, out_k, out_v,
    ownz, sibz, relz, finz, owny, rely, finy, accq, acck, accv,
    fown, frecv, fsum, fsend,
    send, recv, ring_send, ring_recv, local,
):
    z, y, c, x = place()
    near = neighbours(z, y, c, x)
    relz[...] = jnp.zeros_like(relz)
    finz[...] = jnp.zeros_like(finz)
    greet(list(near.values()))
    started = []
    started_if = []

    def remote(index, src, dst, target):
        return pltpu.make_async_remote_copy(
            src_ref=src, dst_ref=dst, send_sem=send.at[index], recv_sem=recv.at[index],
            device_id=target, device_id_type=MESH,
        )

    def go(index, src, dst, target):
        copy = remote(index, src, dst, target)
        copy.start()
        started.append(copy)

    def came(index, dst):
        remote(index, dst, dst, near["sib"]).wait_recv()

    def ring_copies(index, src, dst, target, groups):
        copies = []
        for at, (condition, first, size) in enumerate(groups):
            part = pl.ds(first, size)
            copies.append((condition, pltpu.make_async_remote_copy(
                src_ref=src.at[part], dst_ref=dst.at[part],
                send_sem=ring_send.at[index, at], recv_sem=ring_recv.at[index, at],
                device_id=target, device_id_type=MESH,
            )))
        return copies

    def ring_go(index, src, dst, target, groups):
        for condition, copy in ring_copies(index, src, dst, target, groups):
            @pl.when(condition)
            def _(copy=copy):
                copy.start()

            started_if.append((condition, copy))

    def ring_came(index, dst, groups):
        for condition, copy in ring_copies(index, dst, dst, near["sib"], groups):
            @pl.when(condition)
            def _(copy=copy):
                copy.wait_recv()

    def whole(_):
        return [(z >= 0, 0, 3)]

    def split(low, high):
        return [(low, 0, 2), (high, 2, 1)]

    y_kinds = {kind: whole for kind in ("far", "right", "left", "on_right", "on_left")}
    z_kinds = {
        "far": lambda at: split(at >= 2, at < 2),
        "right": lambda at: split(at == 3, at < 3),
        "left": lambda at: split(at > 0, at == 0),
        "on_right": lambda at: split((at == 0) | (at == 3), at < 3),
        "on_left": lambda at: split(at > 0, (at == 0) | (at == 3)),
    }

    def column(z_at, c_at):
        return pl.ds((z_at * 2 + c_at) * BLK_DEV, BLK_DEV)

    def local_copy(index, src, dst):
        copy = pltpu.make_async_copy(src, dst, local.at[index])
        copy.start()
        return copy

    hops = (2, 1, 3, 0)
    locals_z, locals_y = [], []
    for j, hop in enumerate(hops):
        go(j, pz.at[column(after(z, hop), 1 - c)], sibz.at[j], near["sib"])
        locals_z.append(local_copy(j, pz.at[column(after(z, hop), c)], ownz.at[j]))
        locals_y.append(
            local_copy(4 + j, py.at[pl.ds(after(y, hop) * BLK_DEV, BLK_DEV)], owny.at[j])
        )
        if j == 0:
            remote(20, own_f.at[1 - c], frecv.at[0], near["sib"]).start()
            mine_f = local_copy(8, own_f.at[c], fown)
    locals_own = [
        local_copy(9 + j, src, dst)
        for j, (src, dst) in enumerate(((own_q, accq), (own_k, acck), (own_v, accv)))
    ]

    def add(dst, src):
        for part in range(3):
            dst[part] = (dst[part].astype(jnp.float32) + src[part].astype(jnp.float32)).astype(
                jnp.bfloat16
            )

    def merge(j):
        locals_z[j].wait()
        came(j, sibz.at[j])

        def one(block, carry):
            add(ownz.at[j, block], sibz.at[j, block])
            return carry

        lax.fori_loop(0, BLK_DEV, one, 0)

    rings = (
        (0, ownz, relz, finz, near["zr"], near["zl"], z, z_kinds),
        (12, owny, rely, finy, near["yr"], near["yl"], y, y_kinds),
    )

    def source(base, own, j, block):
        return own.at[j, block] if base == 0 else py.at[after(y, hops[j]) * BLK_DEV + block]


    def ring_far(base, own, rel, fin, right, left, me, kinds):
        groups = kinds["far"](me)
        for block in range(2):
            ring_go(base + block, source(base, own, 0, block), rel.at[0, block], right, groups)
            ring_go(base + 2 + block, source(base, own, 0, 2 + block), rel.at[1, block], left, groups)

    def ring_right(base, own, rel, fin, right, left, me, kinds):
        for block in range(2, 4):
            ring_go(
                base + 2 + block, source(base, own, 1, block), fin.at[0, block], right,
                kinds["right"](me),
            )

    def ring_left(base, own, rel, fin, right, left, me, kinds):
        for block in range(2):
            ring_go(
                base + 6 + block, source(base, own, 2, block), fin.at[1, block], left,
                kinds["left"](me),
            )

    def ring_relay(base, own, rel, fin, right, left, me, kinds):
        before, behind = after(me, 3), after(me, 1)
        for block in range(2):
            ring_came(base + block, rel.at[0, block], kinds["far"](before))
            add(own.at[1, block], rel.at[0, block])
            ring_go(
                base + 8 + block, own.at[1, block], fin.at[0, block], right, kinds["on_right"](me)
            )
            ring_came(base + 2 + block, rel.at[1, block], kinds["far"](behind))
            add(own.at[2, 2 + block], rel.at[1, block])
            ring_go(
                base + 10 + block, own.at[2, 2 + block], fin.at[1, 2 + block], left,
                kinds["on_left"](me),
            )

    def ring_end(base, own, rel, fin, right, left, me, kinds):
        before, behind = after(me, 3), after(me, 1)
        for block in range(2):
            ring_came(base + 4 + block, fin.at[0, 2 + block], kinds["right"](before))
            ring_came(base + 6 + block, fin.at[1, block], kinds["left"](behind))
            ring_came(base + 8 + block, fin.at[0, block], kinds["on_right"](before))
            ring_came(base + 10 + block, fin.at[1, 2 + block], kinds["on_left"](behind))

    ring_far(*rings[1])
    merge(0)
    ring_far(*rings[0])

    f_sends = [
        ((y == 2) | (y == 1), remote(21, fsend.at[0], frecv.at[1], near["yl"])),
        (y == 3, remote(22, fsend.at[0], frecv.at[2], near["yr"])),
        ((y == 0) & ((z == 2) | (z == 1)), remote(23, fsend.at[1], frecv.at[3], near["zl"])),
        ((y == 0) & (z == 3), remote(24, fsend.at[1], frecv.at[4], near["zr"])),
    ]

    def f_take(at):
        came(20 + at, frecv.at[at])
        fsum[...] += frecv[at].astype(jnp.float32)

    def f_send(at):
        condition, copy = f_sends[at]

        @pl.when(condition)
        def _():
            fsend[at // 2] = fsum[...].astype(jnp.bfloat16)
            copy.start()

    mine_f.wait()
    came(20, frecv.at[0])
    fsum[...] = fown[...].astype(jnp.float32) + frecv[0].astype(jnp.float32)

    @pl.when(y == 1)
    def _():
        f_take(1)

    f_send(0)
    f_send(1)

    ring_right(*rings[1])
    ring_left(*rings[1])
    merge(1)
    ring_right(*rings[0])
    merge(2)
    ring_left(*rings[0])

    @pl.when(y == 0)
    def _():
        f_take(1)
        f_take(2)

        @pl.when(z == 1)
        def _():
            f_take(3)

    f_send(2)
    f_send(3)

    merge(3)
    for copy in locals_y:
        copy.wait()
    ring_relay(*rings[0])
    ring_relay(*rings[1])
    top = (z == 0) & (y == 0)

    @pl.when(top)
    def _():
        f_take(3)
        f_take(4)

    for copy in locals_own:
        copy.wait()

    @pl.when(top & (c == 1))
    def _():
        fsend[1] = fsum[...].astype(jnp.bfloat16)
        remote(25, fsend.at[1], frecv.at[5], near["sib"]).start()

    @pl.when(top & (c == 0))
    def _():
        came(25, frecv.at[5])
        acck[0] += fsum[...]
        accv[0] += frecv[5].astype(jnp.float32)

    def total(own, fin, places):
        def one(block, carry):
            for part, (acc, out, head) in enumerate(places):
                lanes = pl.ds(head * HD, HD)
                value = acc[block, :, lanes]
                for ref in (own.at[3], fin.at[0], fin.at[1]):
                    value += ref[block, part].astype(jnp.float32)
                out[block, :, lanes] = value.astype(jnp.bfloat16)
            return carry

        lax.fori_loop(0, BLK_DEV, one, 0)

    ring_end(*rings[0])
    total(ownz, finz, ((acck, out_k, 0), (accv, out_v, 0), (accq, out_q, 1)))
    ring_end(*rings[1])
    total(owny, finy, ((accq, out_q, 0), (acck, out_k, 1), (accv, out_v, 1)))

    for condition, copy in started_if:
        @pl.when(condition)
        def _(copy=copy):
            copy.wait_send()

    for copy in started:
        copy.wait_send()
    remote(20, fown, frecv.at[0], near["sib"]).wait_send()
    for condition, copy in f_sends + [
        (top & (c == 1), remote(25, fsend.at[1], frecv.at[5], near["sib"]))
    ]:
        @pl.when(condition)
        def _(copy=copy):
            copy.wait_send()


def keep_kernel(in_q, in_k, in_v, out_q, out_k, out_v, held, in_sem, out_sem):
    ins, outs = [], []
    for part, (src, dst) in enumerate(((in_q, out_q), (in_k, out_k), (in_v, out_v))):
        for half in range(2):
            piece = pl.ds(2 * half, 2)
            ins.append(
                pltpu.make_async_copy(src.at[piece], held.at[part, piece], in_sem.at[part, half])
            )
            outs.append(
                pltpu.make_async_copy(held.at[part, piece], dst.at[piece], out_sem.at[part, half])
            )
    for copy in ins:
        copy.start()
    for copy, out in zip(ins, outs):
        copy.wait()
        out.start()
    for out in outs:
        out.wait()


def body(query, keys, values, output, d_out, row_logsum, selected):
    bf16, f32 = jnp.bfloat16, jnp.float32
    any_spec = pl.BlockSpec(memory_space=pl.ANY)
    vmem_spec = pl.BlockSpec(memory_space=pltpu.VMEM)
    smem_spec = pl.BlockSpec(memory_space=pltpu.SMEM)
    blocked = (BLK_DEV, BLOCK, WIDTH)
    shape = jax.ShapeDtypeStruct
    dma, vmem, smem = pltpu.SemaphoreType.DMA, pltpu.VMEM, pltpu.SMEM
    zs, ys = shape((32, BLOCK, HD), bf16), shape((16, BLOCK, HD), bf16)
    kz, vz, qz, gz, sz, qy, gy, ky, vy, sy, own_q, own_k, own_v, own_f = pl.pallas_call(
        gather_kernel,
        out_shape=[zs] * 4
        + [shape((32, 8, BLOCK), f32)]
        + [ys] * 4
        + [shape((16, 8, BLOCK), f32)]
        + [shape(blocked, f32)] * 3
        + [shape((2, BLOCK, WIDTH), bf16)],
        in_specs=[any_spec] * 5 + [vmem_spec],
        out_specs=[any_spec] * 14,
        scratch_shapes=[vmem(blocked, bf16)] * 5
        + [vmem((BLK_DEV, 8, BLOCK), f32)]
        + [vmem(blocked, f32)] * 3
        + [
            vmem((2, BLOCK, WIDTH), bf16),
            vmem((2, BLOCK, WIDTH), f32),
            vmem((2, BLOCK, WIDTH), bf16),
            dma((41,)),
            dma((41,)),
            dma((56, 2)),
            dma((56, 2)),
            dma((26,)),
        ],
        compiler_params=pltpu.CompilerParams(
            collective_id=0, has_side_effects=True, vmem_limit_bytes=VMEM
        ),
        name="gather",
    )(
        keys.reshape(blocked), values.reshape(blocked), query.reshape(blocked),
        d_out, output.reshape(blocked), row_logsum,
    )
    pz, py = pl.pallas_call(
        pair_kernel,
        out_shape=[shape((32, 3, BLOCK, HD), bf16), shape((16, 3, BLOCK, HD), bf16)],
        in_specs=[vmem_spec] + [any_spec] * 8 + [vmem_spec] * 2,
        out_specs=[any_spec] * 2,
        scratch_shapes=[
            vmem((8, 128), jnp.int32),
            smem((8, 128), jnp.int32),
            vmem((2, 2, BLOCK, HD), bf16),
            vmem((2, 2, BLOCK, HD), bf16),
            vmem((2, 2, BLOCK, HD), bf16),
            vmem((2, 2, BLOCK, HD), bf16),
            vmem((16, BLOCK, HD), f32),
            vmem((32, BLOCK, HD), f32),
            vmem((2, 2, BLOCK, HD), f32),
            vmem((2, 2, BLOCK, HD), bf16),
            vmem((16, BLOCK, HD), bf16),
            vmem((32, BLOCK, HD), bf16),
            vmem((2, BLOCK, HD), bf16),
            dma,
            dma((2, 2, 4)),
            dma((2,)),
            dma((2, 32)),
            dma((2, 32)),
        ],
        compiler_params=pltpu.CompilerParams(vmem_limit_bytes=VMEM),
        name="pairs",
    )(selected.T, kz, vz, qz, gz, qy, gy, ky, vy, sz, sy)
    piece = (BLK_DEV, 3, BLOCK, HD)
    out_q, out_k, out_v = pl.pallas_call(
        scatter_kernel,
        out_shape=[shape(blocked, bf16)] * 3,
        in_specs=[any_spec] * 6,
        out_specs=[vmem_spec] * 3,
        scratch_shapes=[
            vmem((4,) + piece, bf16),
            vmem((4,) + piece, bf16),
            vmem((2, 2, 3, BLOCK, HD), bf16),
            vmem((2,) + piece, bf16),
            vmem((4,) + piece, bf16),
            vmem((2, 2, 3, BLOCK, HD), bf16),
            vmem((2,) + piece, bf16),
            vmem(blocked, f32),
            vmem(blocked, f32),
            vmem(blocked, f32),
            vmem((BLOCK, WIDTH), bf16),
            vmem((6, BLOCK, WIDTH), bf16),
            vmem((BLOCK, WIDTH), f32),
            vmem((2, BLOCK, WIDTH), bf16),
            dma((26,)),
            dma((26,)),
            dma((24, 2)),
            dma((24, 2)),
            dma((12,)),
        ],
        compiler_params=pltpu.CompilerParams(
            collective_id=1, has_side_effects=True, vmem_limit_bytes=VMEM
        ),
        name="scatter",
    )(pz, py, own_q, own_k, own_v, own_f)
    out_q, out_k, out_v = pl.pallas_call(
        keep_kernel,
        out_shape=[shape(blocked, bf16)] * 3,
        in_specs=[any_spec] * 3,
        out_specs=[any_spec] * 3,
        scratch_shapes=[vmem((3,) + blocked, bf16), dma((3, 2)), dma((3, 2))],
        compiler_params=pltpu.CompilerParams(vmem_limit_bytes=VMEM),
        name="keep",
    )(out_q, out_k, out_v)
    flat = (BLK_DEV * BLOCK, WIDTH)
    return out_q.reshape(flat), out_k.reshape(flat), out_v.reshape(flat)


def solution(mesh):
    in_specs = (
        P("seq", "head"),
        P("seq", "head"),
        P("seq", "head"),
        P("seq", "head"),
        P(("seq", "head"), None),
        P("head", "seq"),
        P(),
    )
    out_specs = (P("seq", "head"), P("seq", "head"), P("seq", "head"))
    return jax.shard_map(body, mesh=mesh, in_specs=in_specs, out_specs=out_specs, check_vma=False)
```

```python
import functools
import math

import jax
import jax.numpy as jnp
from jax import lax
from jax.experimental import pallas as pl
from jax.experimental.pallas import tpu as pltpu
from jax.sharding import PartitionSpec as P

MESH = pl.DeviceIdType.MESH
BLOCK = 512
HD = 128
WIDTH = 256
BLK_DEV = 4
RING = 4
NSLOT = 32
LOG2E = math.log2(math.e)
VMEM = 60 * 1024 * 1024


def place():
    seq = lax.axis_index("seq")
    return lax.div(seq, 8), lax.rem(lax.div(seq, 2), 4), lax.rem(seq, 2), lax.axis_index("head")


def device(z, y, c, x):
    return ((z * 4 + y) * 2 + c, x)


def after(index, step):
    return lax.rem(index + step, RING)


def neighbours(z, y, c, x):
    return {
        "sib": device(z, y, 1 - c, x),
        "zr": device(after(z, 1), y, c, x),
        "zl": device(after(z, 3), y, c, x),
        "yr": device(z, after(y, 1), c, x),
        "yl": device(z, after(y, 3), c, x),
    }


def greet(devices):
    barrier = pltpu.get_barrier_semaphore()
    for target in devices:
        pl.semaphore_signal(barrier, inc=1, device_id=target, device_id_type=MESH)
    pl.semaphore_wait(barrier, len(devices))


NT = (((1,), (1,)), ((), ()))
NN = (((1,), (0,)), ((), ()))
TN = (((0,), (0,)), ((), ()))


def dot(a, b, dims):
    return lax.dot_general(a, b, dims, preferred_element_type=jnp.float32)


def gather_kernel(
    keys, values, query, d_out, output, logsum,
    kz, vz, qz, gz, sz, qy, gy, ky, vy, sy, own_q, own_k, own_v, own_f,
    grad, outv, kv, vv, qv, stats, accq, acck, accv, fblk, accf, fout,
    send, recv, bulk_send, bulk_recv, local,
):
    z, y, c, x = place()
    near = neighbours(z, y, c, x)
    others = [((z * 4 + y) * 2 + c, after(x, step)) for step in (1, 2, 3)]
    greet(list(near.values()) + others)
    started = []

    def remote(index, src, dst, target):
        return pltpu.make_async_remote_copy(
            src_ref=src, dst_ref=dst, send_sem=send.at[index], recv_sem=recv.at[index],
            device_id=target, device_id_type=MESH,
        )

    def go(index, src, dst, target):
        copy = remote(index, src, dst, target)
        copy.start()
        started.append(copy)

    def bulk(array, kind, chunk, src, dst, target):
        return pltpu.make_async_remote_copy(
            src_ref=src, dst_ref=dst,
            send_sem=bulk_send.at[array * 7 + kind, chunk],
            recv_sem=bulk_recv.at[array * 7 + kind, chunk],
            device_id=target, device_id_type=MESH,
        )

    started_if = []

    def start_if(condition, copies):
        @pl.when(condition)
        def _():
            for copy in copies:
                copy.start()

        started_if.append((condition, copies))

    def spread(array, kind, src, head, dst, piece, target, condition):
        start_if(condition, [
            bulk(
                array, kind, chunk,
                src.at[pl.ds(2 * chunk, 2), :, pl.ds(head * HD, HD)],
                dst.at[pl.ds(piece + 2 * chunk, 2)],
                target,
            )
            for chunk in range(2)
        ])

    def relay(array, kind, ref, piece, condition, *onward):
        for chunk in range(2):
            at = ref.at[pl.ds(piece + 2 * chunk, 2)]

            @pl.when(condition)
            def _(at=at, chunk=chunk):
                bulk(array, kind, chunk, at, at, near["sib"]).wait_recv()

            for kind_on, target, condition_on in onward:
                start_if(condition_on, [bulk(array, kind_on, chunk, at, at, target)])

    def column(z_at, c_at):
        return (z_at * 2 + c_at) * BLK_DEV

    def row(y_at):
        return y_at * BLK_DEV

    def four(start):
        return pl.ds(start, BLK_DEV)

    zl, zr, zo = after(z, 3), after(z, 1), after(z, 2)
    yl, yr = after(y, 3), after(y, 1)
    top = (z == 0) & (y == 0)
    root = top & (c == 0)

    first_own = [
        pltpu.make_async_copy(keys.at[0], fblk.at[0], local.at[0]),
        pltpu.make_async_copy(values.at[0], fblk.at[1], local.at[1]),
    ]

    def first_copy(part, send_at, recv_at, target):
        return pltpu.make_async_remote_copy(
            src_ref=fblk.at[part], dst_ref=fblk.at[part],
            send_sem=send.at[send_at], recv_sem=recv.at[recv_at],
            device_id=target, device_id_type=MESH,
        )

    first_sends = [
        ((z == 0) & (y <= 1), first_copy(c, 28, 26, near["yr"])),
        ((z == 0) & (y == 0), first_copy(c, 29, 26, near["yl"])),
        (z <= 1, first_copy(c, 30, 26, near["zr"])),
        (z == 0, first_copy(c, 31, 26, near["zl"])),
        (jnp.logical_not(top & (c == 1)), first_copy(c, 32, 27, near["sib"])),
    ]
    first_start = first_copy(1, 33, 26, near["sib"])

    def send_first():
        for condition, copy in first_sends:
            @pl.when(condition)
            def _(copy=copy):
                copy.start()

    def pass_first(condition):
        @pl.when(condition)
        def _():
            first_copy(c, 28, 26, near["sib"]).wait_recv()
            send_first()

    @pl.when(root)
    def _():
        for copy in first_own:
            copy.start()
        for copy in first_own:
            copy.wait()
        first_start.start()
        send_first()

    pass_first(top & (c == 1))

    for step in (1, 2, 3):
        to = after(x, step)
        go(
            22 + step,
            d_out.at[:, pl.ds(pl.multiple_of(to * WIDTH, WIDTH), WIDTH)],
            grad.at[x],
            others[step - 1],
        )
    to_vmem = [
        pltpu.make_async_copy(
            d_out.at[:, pl.ds(pl.multiple_of(x * WIDTH, WIDTH), WIDTH)], grad.at[x], local.at[2]
        ),
        pltpu.make_async_copy(output, outv, local.at[3]),
        pltpu.make_async_copy(keys, kv, local.at[4]),
        pltpu.make_async_copy(values, vv, local.at[5]),
        pltpu.make_async_copy(query, qv, local.at[6]),
    ]
    kept = []
    for copy in to_vmem:
        copy.start()

    own_z, own_y = column(z, c), row(y)
    z_set = ((keys, 0, kz, 0), (values, 0, vz, 1), (query, 1, qz, 0), (grad, 1, gz, 1))
    y_set = ((query, 0, qy, 0), (grad, 0, gy, 1), (keys, 1, ky, 0), (values, 1, vy, 1))
    z_ways, y_ways = (near["zr"], near["zl"]), (near["yr"], near["yl"])

    def wanted(array, src, dst):
        if array < 2:
            return dst > src
        if array < 4:
            return dst < src
        if array < 6:
            return (dst < src) | (z > 0)
        return (dst > src) | (z < 3)

    def sent(array, kind, src):
        way = (z_set + y_set)[array][3]
        step = (1, 3)[way]
        if kind == 0:
            return wanted(array, src, after(src, step)) | wanted(array, src, after(src, 2))
        if kind == 1:
            return wanted(array, src, after(src, 4 - step))
        return wanted(array, src, after(src, 2))

    def spread_all(kind, arrays):
        for array in arrays:
            src, head, ref, way = (z_set + y_set)[array]
            piece, at, ways = (own_z, z, z_ways) if array < 4 else (own_y, y, y_ways)
            spread(
                array, kind, src, head, ref, piece, ways[(way + kind) % 2], sent(array, kind, at)
            )

    spread_all(0, (4, 7, 6, 0, 1, 2))
    spread_all(1, (4, 7, 6, 0, 1, 2))
    for array in (0, 1, 2):
        src, head, ref, _ = z_set[array]
        spread(array, 3, src, head, ref, own_z, near["sib"], z >= 0)

    pass_first((z == 0) & ((y == 1) | (y == 3)))
    to_vmem[0].wait()
    to_vmem[1].wait()
    for step in (1, 2, 3):
        remote(22 + step, grad.at[x], grad.at[x], others[step - 1]).wait_recv()
    spread_all(0, (5, 3))
    spread_all(1, (5, 3))
    spread(3, 3, grad, 1, gz, own_z, near["sib"], z >= 0)
    pass_first((z == 0) & (y == 2))
    stats[...] = jnp.zeros_like(stats)

    ones = jnp.ones((8, HD), jnp.bfloat16)
    for block in range(BLK_DEV):
        for head in range(2):
            part = pl.ds(head * HD, HD)
            product = grad[block, :, part].astype(jnp.float32) * outv[block, :, part].astype(jnp.float32)
            high = product.astype(jnp.bfloat16)
            low = (product - high.astype(jnp.float32)).astype(jnp.bfloat16)
            total = dot(ones, high, NT) + dot(ones, low, NT)
            stats[block, pl.ds(2 + head, 1), :] = total[0:1]
            stats[block, pl.ds(head, 1), :] = (
                logsum[pl.ds(head, 1), pl.ds(block * BLOCK, BLOCK)] * LOG2E
            )
    go(18, stats, sy.at[four(own_y)], near["yr"])
    go(19, stats, sy.at[four(own_y)], near["yl"])
    go(34, stats, sz.at[four(own_z)], near["zr"])
    go(35, stats, sz.at[four(own_z)], near["zl"])
    go(36, stats, sz.at[four(own_z)], near["sib"])

    for copy in to_vmem[2:]:
        copy.wait()
    held = {0: kv, 1: vv, 2: qv, 3: grad}
    keep = [(held[(0, 1, 2, 3)[at]], z_set[at][1], z_set[at][2].at[four(own_z)]) for at in range(4)]
    keep += [(held[(2, 3, 0, 1)[at]], y_set[at][1], y_set[at][2].at[four(own_y)]) for at in range(4)]
    keep += [(stats, None, sz.at[four(own_z)]), (stats, None, sy.at[four(own_y)])]
    for index, (src, head, dst) in enumerate(keep):
        part = src if head is None else src.at[:, :, pl.ds(head * HD, HD)]
        kept.append(pltpu.make_async_copy(part, dst, local.at[16 + index]))
        kept[-1].start()
    scale = 1.0 / math.sqrt(HD)

    def own_block(block, carry):
        for head in range(2):
            part = pl.ds(head * HD, HD)
            k, v, q, g = kv[block, :, part], vv[block, :, part], qv[block, :, part], grad[block, :, part]
            lse = stats[block, pl.ds(head, 1), :]
            delta = stats[block, pl.ds(2 + head, 1), :]
            p = jnp.exp2(dot(k, q, NT) * (scale * LOG2E) - lse)
            key_at = lax.broadcasted_iota(jnp.int32, (BLOCK, BLOCK), 0)
            query_at = lax.broadcasted_iota(jnp.int32, (BLOCK, BLOCK), 1)
            p = jnp.where(key_at <= query_at, p, 0.0)
            ds = (p * (dot(v, g, NT) - delta)).astype(jnp.bfloat16)
            accv[block, :, part] = dot(p.astype(jnp.bfloat16), g, NN)
            acck[block, :, part] = dot(ds, q, NN) * scale
            accq[block, :, part] = dot(ds, k, TN) * scale
        return carry

    def first_block(block, carry):
        for head in range(2):
            part = pl.ds(head * HD, HD)
            k, v, q, g = fblk[0, :, part], fblk[1, :, part], qv[block, :, part], grad[block, :, part]
            lse = stats[block, pl.ds(head, 1), :]
            delta = stats[block, pl.ds(2 + head, 1), :]
            p = jnp.exp2(dot(k, q, NT) * (scale * LOG2E) - lse)
            ds = (p * (dot(v, g, NT) - delta)).astype(jnp.bfloat16)
            accf[1, :, part] += dot(p.astype(jnp.bfloat16), g, NN)
            accf[0, :, part] += dot(ds, q, NN) * scale
            accq[block, :, part] += dot(ds, k, TN) * scale
        return carry

    lax.fori_loop(0, BLK_DEV, own_block, 0)
    for index, (src, dst) in enumerate(((acck, own_k), (accv, own_v))):
        kept.append(pltpu.make_async_copy(src, dst, local.at[12 + index]))
        kept[-1].start()
    pass_first((z == 1) | (z == 3))

    def pieces(array):
        _, _, ref, way = (z_set + y_set)[array]
        if array < 4:
            at = (zl, zr, zo) if way == 0 else (zr, zl, zo)
            return ref, at, [column(one, c) for one in at], z_ways[way]
        at = (yl, yr, after(y, 2)) if way == 0 else (yr, yl, after(y, 2))
        return ref, at, [row(one) for one in at], y_ways[way]

    def onward(array, kind):
        ref, at, piece, way = pieces(array)
        came = sent(array, kind, at[kind])
        sends = [(2, way, sent(array, 2, at[0]))] if kind == 0 else []
        if array < 4:
            sends.append((4 + kind, near["sib"], came))
        relay(array, kind, ref, piece[kind], came, *sends)

    for array in (4, 7, 6, 0, 1, 2):
        onward(array, 0)
    sy_in = [sy.at[four(row(after(y, step)))] for step in (3, 1, 2)]
    sz_in = [sz.at[four(column(after(z, step), c))] for step in (3, 1, 2)]

    def stat_in(index, ref):
        remote(index, ref, ref, near["sib"]).wait_recv()

    stat_in(18, sy_in[0])
    go(22, sy_in[0], sy_in[0], near["yr"])
    stat_in(34, sz_in[0])
    go(37, sz_in[0], sz_in[0], near["zr"])
    go(38, sz_in[0], sz_in[0], near["sib"])
    for array in (5, 3):
        onward(array, 0)
    pass_first(z == 2)

    @pl.when(jnp.logical_not(root))
    def _():
        first_copy(1 - c, 32, 27, near["sib"]).wait_recv()

    accf[...] = jnp.zeros_like(accf)
    lax.fori_loop(jnp.where(root, 1, 0), BLK_DEV, first_block, 0)
    fout[...] = accf[...].astype(jnp.bfloat16)
    for index, (src, dst) in enumerate(((accq, own_q), (fout, own_f))):
        kept.append(pltpu.make_async_copy(src, dst, local.at[14 + index]))
        kept[-1].start()
    stat_in(35, sz_in[1])
    go(39, sz_in[1], sz_in[1], near["sib"])
    for kind in (1, 2):
        for array in (0, 1, 4, 7, 2, 6, 3, 5):
            onward(array, kind)
    stat_in(37, sz_in[2])
    go(40, sz_in[2], sz_in[2], near["sib"])
    stat_in(19, sy_in[1])
    stat_in(22, sy_in[2])
    for array in range(4):
        ref, at, _, _ = pieces(array)
        relay(array, 3, ref, column(z, 1 - c), z >= 0)
        for kind in range(3):
            relay(array, 4 + kind, ref, column(at[kind], 1 - c), sent(array, kind, at[kind]))
    for index, at in ((36, z), (38, zl), (39, zr), (40, zo)):
        stat_in(index, sz.at[four(column(at, 1 - c))])
    for copy in kept:
        copy.wait()
    for condition, copies in started_if:
        @pl.when(condition)
        def _(copies=copies):
            for copy in copies:
                copy.wait_send()

    for copy in started:
        copy.wait_send()

    @pl.when(root)
    def _():
        first_start.wait_send()

    for condition, copy in first_sends:
        @pl.when(condition)
        def _(copy=copy):
            copy.wait_send()


def choose(selected, z, y, c, head):
    row_at = lax.broadcasted_iota(jnp.int32, (32, 1), 0)
    group, core, block = row_at >> 3, (row_at >> 2) & 1, row_at & 3
    if head == 0:
        token_block = row_at + z * 32
    else:
        token_block = group * 32 + y * 8 + (row_at & 7)
    lane = lax.broadcasted_iota(jnp.int32, (32, 128), 1)
    found = jnp.zeros((32, 128), jnp.int32)
    for pick in range(3):
        row = selected[pl.ds(pick, 1), :]
        chosen = jnp.sum(jnp.where(lane == token_block, row, 0), axis=1, keepdims=True)
        z_of, y_of, c_of, b_of = chosen >> 5, (chosen >> 3) & 3, (chosen >> 2) & 1, chosen & 3
        if head == 0:
            here = (chosen > 0) & (y_of == y) & (core == c)
            target = ((z_of * 2 + c_of) * 4 + b_of) * 4 + group
            value = 1 + group * 4 + block
        else:
            here = (chosen > 0) & (z_of == z) & (c_of == c)
            target = (y_of * 4 + b_of) * 8 + group * 2 + core
            value = 1 + (group * 2 + core) * 4 + block
        found += jnp.where(here & (lane == target), value, 0)
    table = jnp.sum(found, axis=0, keepdims=True)
    down = lax.broadcasted_iota(jnp.int32, (128, 128), 0)
    across = lax.broadcasted_iota(jnp.int32, (128, 128), 1)
    spread = jnp.broadcast_to(table, (128, 128))
    rank = jnp.sum(jnp.where((across < down) & (spread > 0), 1, 0), axis=1, keepdims=True)
    entry = jnp.sum(jnp.where(across == down, spread, 0), axis=1, keepdims=True)
    item = jnp.where(entry > 0, down[:, 0:1] * 128 + entry, 0)
    items = jnp.sum(jnp.where(rank == across, item, 0), axis=0, keepdims=True)
    return items, table


def pair_kernel(
    selected, kz, vz, qz, gz, qy, gy, ky, vy, sz, sy,
    pz, py,
    lists_v, lists, kbuf, vbuf, qbuf, gbuf, dq0, dq1, dkv, kvout, qout0, qout1, zero,
    list_sem, in_sem, out_sem, q_sem, zero_sem,
):
    z, y, c, _ = place()
    scale = 1.0 / math.sqrt(HD)
    for head in range(2):
        items, table = choose(selected, z, y, c, head)
        lists_v[pl.ds(2 * head, 1), :] = items
        lists_v[pl.ds(2 * head + 1, 1), :] = table
    listed = pltpu.make_async_copy(lists_v, lists, list_sem)
    listed.start()
    zero[...] = jnp.zeros_like(zero)
    dq0[...] = jnp.zeros_like(dq0)
    dq1[...] = jnp.zeros_like(dq1)
    listed.wait()

    class Part:
        pass

    parts = []
    for head in range(2):
        part = Part()
        part.head, part.per, part.slots = head, (4, 8)[head], (32, 16)[head]
        part.k, part.v, part.q, part.g = ((kz, vz, qy, gy), (ky, vy, qz, gz))[head]
        part.stat, part.dq, part.qout = ((sy, dq0, qout0), (sz, dq1, qout1))[head]
        part.out, part.at = ((pz, 0), (py, 1))[head]
        part.dq_out, part.dq_at = ((py, 0), (pz, 2))[head]
        parts.append(part)

    def item_of(part, at):
        item = lists[2 * part.head, at]
        return lax.div(item, 128 * part.per), lax.rem(item, 128) - 1, item

    def loads(part, at):
        slot, block, _ = item_of(part, at)
        side = lax.rem(at, 2)
        pairs = ((part.k, kbuf, slot), (part.v, vbuf, slot), (part.q, qbuf, block), (part.g, gbuf, block))
        return [
            pltpu.make_async_copy(
                src.at[where], buf.at[part.head, side], in_sem.at[part.head, side, index]
            )
            for index, (src, buf, where) in enumerate(pairs)
        ]

    for part in parts:
        @pl.when(lists[2 * part.head, 0] > 0)
        def _(part=part):
            for copy in loads(part, 0):
                copy.start()

    def idle(part, slot):
        total = lists[2 * part.head + 1, slot * part.per]
        for at in range(1, part.per):
            total += lists[2 * part.head + 1, slot * part.per + at]
        return total == 0

    def blank(part, slot):
        return pltpu.make_async_copy(
            zero, part.out.at[slot, pl.ds(part.at, 2)], zero_sem.at[part.head, slot]
        )

    def each_idle(part, act):
        def one(slot, carry):
            @pl.when(idle(part, slot))
            def _():
                act(blank(part, slot))
            return carry

        lax.fori_loop(0, part.slots, one, 0)

    for part in parts:
        each_idle(part, lambda copy: copy.start())

    def put(part, slot):
        return pltpu.make_async_copy(
            kvout.at[part.head], part.out.at[slot, pl.ds(part.at, 2)], out_sem.at[part.head]
        )

    def enter(part, at, opened):
        slot, _, _ = item_of(part, at)
        _, _, following = item_of(part, at + 1)

        @pl.when(following > 0)
        def _():
            for copy in loads(part, at + 1):
                copy.start()

        for copy in loads(part, at):
            copy.wait()

        @pl.when(slot != opened)
        def _():
            dkv[part.head] = jnp.zeros(dkv.shape[1:], dkv.dtype)

    def work(part, at):
        _, block, _ = item_of(part, at)
        side = lax.rem(at, 2)
        k, v = kbuf[part.head, side], vbuf[part.head, side]
        q, g = qbuf[part.head, side], gbuf[part.head, side]
        lse = part.stat[block, pl.ds(part.head, 1), :]
        delta = part.stat[block, pl.ds(2 + part.head, 1), :]
        p = jnp.exp2(dot(k, q, NT) * (scale * LOG2E) - lse)
        ds = (p * (dot(v, g, NT) - delta)).astype(jnp.bfloat16)
        dkv[part.head, 1] += dot(p.astype(jnp.bfloat16), g, NN)
        dkv[part.head, 0] += dot(ds, q, NN)
        part.dq[block] += dot(ds, k, TN)

    def leave(part, at, done):
        slot, _, _ = item_of(part, at)
        next_slot, _, following = item_of(part, at + 1)
        closing = (following == 0) | (next_slot != slot)

        @pl.when(closing)
        def _():
            @pl.when(done > 0)
            def _():
                put(part, 0).wait()
            kvout[part.head, 0] = (dkv[part.head, 0] * scale).astype(jnp.bfloat16)
            kvout[part.head, 1] = dkv[part.head, 1].astype(jnp.bfloat16)
            put(part, slot).start()

        return slot, done + jnp.where(closing, 1, 0)

    def both(state):
        at, opened0, done0, opened1, done1 = state
        enter(parts[0], at, opened0)
        enter(parts[1], at, opened1)
        work(parts[0], at)
        work(parts[1], at)
        return (at + 1,) + leave(parts[0], at, done0) + leave(parts[1], at, done1)

    none, nil = jnp.int32(-1), jnp.int32(0)
    at_both, *rest = lax.while_loop(
        lambda state: (lists[0, state[0]] > 0) & (lists[2, state[0]] > 0),
        both,
        (nil, none, nil, none, nil),
    )
    ends = []
    for part in parts:
        def one(state, part=part):
            at, opened, done = state
            enter(part, at, opened)
            work(part, at)
            return (at + 1,) + leave(part, at, done)

        _, _, done = lax.while_loop(
            lambda state, part=part: lists[2 * part.head, state[0]] > 0,
            one,
            (at_both, rest[2 * part.head], rest[2 * part.head + 1]),
        )
        ends.append(done)

        def flush(block, part=part):
            return pltpu.make_async_copy(
                part.qout.at[block], part.dq_out.at[block, part.dq_at], q_sem.at[part.head, block]
            )

        def finish(block, carry, part=part, flush=flush):
            part.qout[block] = (part.dq[block] * scale).astype(jnp.bfloat16)
            flush(block).start()
            return carry

        part.flush = flush
        part.blocks = (16, 32)[part.head]
        lax.fori_loop(0, part.blocks, finish, 0)

    for part in parts:
        @pl.when(ends[part.head] > 0)
        def _(part=part):
            put(part, 0).wait()

    for part in parts:
        def drain(block, carry, part=part):
            part.flush(block).wait()
            return carry

        lax.fori_loop(0, part.blocks, drain, 0)
        each_idle(part, lambda copy: copy.wait())


def scatter_kernel(
    pz, py, own_q, own_k, own_v, own_f,
    out_q, out_k, out_v,
    ownz, sibz, relz, finz, owny, rely, finy, accq, acck, accv,
    fown, frecv, fsum, fsend,
    send, recv, ring_send, ring_recv, local,
):
    z, y, c, x = place()
    near = neighbours(z, y, c, x)
    relz[...] = jnp.zeros_like(relz)
    finz[...] = jnp.zeros_like(finz)
    greet(list(near.values()))
    started = []
    started_if = []

    def remote(index, src, dst, target):
        return pltpu.make_async_remote_copy(
            src_ref=src, dst_ref=dst, send_sem=send.at[index], recv_sem=recv.at[index],
            device_id=target, device_id_type=MESH,
        )

    def go(index, src, dst, target):
        copy = remote(index, src, dst, target)
        copy.start()
        started.append(copy)

    def came(index, dst):
        remote(index, dst, dst, near["sib"]).wait_recv()

    def ring_copies(index, src, dst, target, groups):
        copies = []
        for at, (condition, first, size) in enumerate(groups):
            part = pl.ds(first, size)
            copies.append((condition, pltpu.make_async_remote_copy(
                src_ref=src.at[part], dst_ref=dst.at[part],
                send_sem=ring_send.at[index, at], recv_sem=ring_recv.at[index, at],
                device_id=target, device_id_type=MESH,
            )))
        return copies

    def ring_go(index, src, dst, target, groups):
        for condition, copy in ring_copies(index, src, dst, target, groups):
            @pl.when(condition)
            def _(copy=copy):
                copy.start()

            started_if.append((condition, copy))

    def ring_came(index, dst, groups):
        for condition, copy in ring_copies(index, dst, dst, near["sib"], groups):
            @pl.when(condition)
            def _(copy=copy):
                copy.wait_recv()

    def whole(_):
        return [(z >= 0, 0, 3)]

    def split(low, high):
        return [(low, 0, 2), (high, 2, 1)]

    y_kinds = {kind: whole for kind in ("far", "right", "left", "on_right", "on_left")}
    z_kinds = {
        "far": lambda at: split(at >= 2, at < 2),
        "right": lambda at: split(at == 3, at < 3),
        "left": lambda at: split(at > 0, at == 0),
        "on_right": lambda at: split((at == 0) | (at == 3), at < 3),
        "on_left": lambda at: split(at > 0, (at == 0) | (at == 3)),
    }

    def column(z_at, c_at):
        return pl.ds((z_at * 2 + c_at) * BLK_DEV, BLK_DEV)

    def local_copy(index, src, dst):
        copy = pltpu.make_async_copy(src, dst, local.at[index])
        copy.start()
        return copy

    hops = (2, 1, 3, 0)
    locals_z, locals_y = [], []
    for j, hop in enumerate(hops):
        go(j, pz.at[column(after(z, hop), 1 - c)], sibz.at[j], near["sib"])
        locals_z.append(local_copy(j, pz.at[column(after(z, hop), c)], ownz.at[j]))
        locals_y.append(
            local_copy(4 + j, py.at[pl.ds(after(y, hop) * BLK_DEV, BLK_DEV)], owny.at[j])
        )
        if j == 0:
            remote(20, own_f.at[1 - c], frecv.at[0], near["sib"]).start()
            mine_f = local_copy(8, own_f.at[c], fown)
    locals_own = [
        local_copy(9 + j, src, dst)
        for j, (src, dst) in enumerate(((own_q, accq), (own_k, acck), (own_v, accv)))
    ]

    def add(dst, src):
        for part in range(3):
            dst[part] = (dst[part].astype(jnp.float32) + src[part].astype(jnp.float32)).astype(
                jnp.bfloat16
            )

    def merge(j):
        locals_z[j].wait()
        came(j, sibz.at[j])

        def one(block, carry):
            add(ownz.at[j, block], sibz.at[j, block])
            return carry

        lax.fori_loop(0, BLK_DEV, one, 0)

    rings = (
        (0, ownz, relz, finz, near["zr"], near["zl"], z, z_kinds),
        (12, owny, rely, finy, near["yr"], near["yl"], y, y_kinds),
    )

    def source(base, own, j, block):
        return own.at[j, block] if base == 0 else py.at[after(y, hops[j]) * BLK_DEV + block]


    def ring_far(base, own, rel, fin, right, left, me, kinds):
        groups = kinds["far"](me)
        for block in range(2):
            ring_go(base + block, source(base, own, 0, block), rel.at[0, block], right, groups)
            ring_go(base + 2 + block, source(base, own, 0, 2 + block), rel.at[1, block], left, groups)

    def ring_right(base, own, rel, fin, right, left, me, kinds):
        for block in range(2, 4):
            ring_go(
                base + 2 + block, source(base, own, 1, block), fin.at[0, block], right,
                kinds["right"](me),
            )

    def ring_left(base, own, rel, fin, right, left, me, kinds):
        for block in range(2):
            ring_go(
                base + 6 + block, source(base, own, 2, block), fin.at[1, block], left,
                kinds["left"](me),
            )

    def ring_relay(base, own, rel, fin, right, left, me, kinds):
        before, behind = after(me, 3), after(me, 1)
        for block in range(2):
            ring_came(base + block, rel.at[0, block], kinds["far"](before))
            add(own.at[1, block], rel.at[0, block])
            ring_go(
                base + 8 + block, own.at[1, block], fin.at[0, block], right, kinds["on_right"](me)
            )
            ring_came(base + 2 + block, rel.at[1, block], kinds["far"](behind))
            add(own.at[2, 2 + block], rel.at[1, block])
            ring_go(
                base + 10 + block, own.at[2, 2 + block], fin.at[1, 2 + block], left,
                kinds["on_left"](me),
            )

    def ring_end(base, own, rel, fin, right, left, me, kinds):
        before, behind = after(me, 3), after(me, 1)
        for block in range(2):
            ring_came(base + 4 + block, fin.at[0, 2 + block], kinds["right"](before))
            ring_came(base + 6 + block, fin.at[1, block], kinds["left"](behind))
            ring_came(base + 8 + block, fin.at[0, block], kinds["on_right"](before))
            ring_came(base + 10 + block, fin.at[1, 2 + block], kinds["on_left"](behind))

    ring_far(*rings[1])
    merge(0)
    ring_far(*rings[0])

    f_sends = [
        ((y == 2) | (y == 1), remote(21, fsend.at[0], frecv.at[1], near["yl"])),
        (y == 3, remote(22, fsend.at[0], frecv.at[2], near["yr"])),
        ((y == 0) & ((z == 2) | (z == 1)), remote(23, fsend.at[1], frecv.at[3], near["zl"])),
        ((y == 0) & (z == 3), remote(24, fsend.at[1], frecv.at[4], near["zr"])),
    ]

    def f_take(at):
        came(20 + at, frecv.at[at])
        fsum[...] += frecv[at].astype(jnp.float32)

    def f_send(at):
        condition, copy = f_sends[at]

        @pl.when(condition)
        def _():
            fsend[at // 2] = fsum[...].astype(jnp.bfloat16)
            copy.start()

    mine_f.wait()
    came(20, frecv.at[0])
    fsum[...] = fown[...].astype(jnp.float32) + frecv[0].astype(jnp.float32)

    @pl.when(y == 1)
    def _():
        f_take(1)

    f_send(0)
    f_send(1)

    ring_right(*rings[1])
    ring_left(*rings[1])
    merge(1)
    ring_right(*rings[0])
    merge(2)
    ring_left(*rings[0])

    @pl.when(y == 0)
    def _():
        f_take(1)
        f_take(2)

        @pl.when(z == 1)
        def _():
            f_take(3)

    f_send(2)
    f_send(3)

    merge(3)
    for copy in locals_y:
        copy.wait()
    ring_relay(*rings[0])
    ring_relay(*rings[1])
    top = (z == 0) & (y == 0)

    @pl.when(top)
    def _():
        f_take(3)
        f_take(4)

    for copy in locals_own:
        copy.wait()

    @pl.when(top & (c == 1))
    def _():
        fsend[1] = fsum[...].astype(jnp.bfloat16)
        remote(25, fsend.at[1], frecv.at[5], near["sib"]).start()

    @pl.when(top & (c == 0))
    def _():
        came(25, frecv.at[5])
        acck[0] += fsum[...]
        accv[0] += frecv[5].astype(jnp.float32)

    def total(own, fin, places):
        def one(block, carry):
            for part, (acc, out, head) in enumerate(places):
                lanes = pl.ds(head * HD, HD)
                value = acc[block, :, lanes]
                for ref in (own.at[3], fin.at[0], fin.at[1]):
                    value += ref[block, part].astype(jnp.float32)
                out[block, :, lanes] = value.astype(jnp.bfloat16)
            return carry

        lax.fori_loop(0, BLK_DEV, one, 0)

    ring_end(*rings[0])
    total(ownz, finz, ((acck, out_k, 0), (accv, out_v, 0), (accq, out_q, 1)))
    ring_end(*rings[1])
    total(owny, finy, ((accq, out_q, 0), (acck, out_k, 1), (accv, out_v, 1)))

    for condition, copy in started_if:
        @pl.when(condition)
        def _(copy=copy):
            copy.wait_send()

    for copy in started:
        copy.wait_send()
    remote(20, fown, frecv.at[0], near["sib"]).wait_send()
    for condition, copy in f_sends + [
        (top & (c == 1), remote(25, fsend.at[1], frecv.at[5], near["sib"]))
    ]:
        @pl.when(condition)
        def _(copy=copy):
            copy.wait_send()


def keep_kernel(in_q, in_k, in_v, out_q, out_k, out_v, held, in_sem, out_sem):
    ins, outs = [], []
    for part, (src, dst) in enumerate(((in_q, out_q), (in_k, out_k), (in_v, out_v))):
        for half in range(2):
            piece = pl.ds(2 * half, 2)
            ins.append(
                pltpu.make_async_copy(src.at[piece], held.at[part, piece], in_sem.at[part, half])
            )
            outs.append(
                pltpu.make_async_copy(held.at[part, piece], dst.at[piece], out_sem.at[part, half])
            )
    for copy in ins:
        copy.start()
    for copy, out in zip(ins, outs):
        copy.wait()
        out.start()
    for out in outs:
        out.wait()


def body(query, keys, values, output, d_out, row_logsum, selected):
    bf16, f32 = jnp.bfloat16, jnp.float32
    any_spec = pl.BlockSpec(memory_space=pl.ANY)
    vmem_spec = pl.BlockSpec(memory_space=pltpu.VMEM)
    smem_spec = pl.BlockSpec(memory_space=pltpu.SMEM)
    blocked = (BLK_DEV, BLOCK, WIDTH)
    shape = jax.ShapeDtypeStruct
    dma, vmem, smem = pltpu.SemaphoreType.DMA, pltpu.VMEM, pltpu.SMEM
    zs, ys = shape((32, BLOCK, HD), bf16), shape((16, BLOCK, HD), bf16)
    kz, vz, qz, gz, sz, qy, gy, ky, vy, sy, own_q, own_k, own_v, own_f = pl.pallas_call(
        gather_kernel,
        out_shape=[zs] * 4
        + [shape((32, 8, BLOCK), f32)]
        + [ys] * 4
        + [shape((16, 8, BLOCK), f32)]
        + [shape(blocked, f32)] * 3
        + [shape((2, BLOCK, WIDTH), bf16)],
        in_specs=[any_spec] * 5 + [vmem_spec],
        out_specs=[any_spec] * 14,
        scratch_shapes=[vmem(blocked, bf16)] * 5
        + [vmem((BLK_DEV, 8, BLOCK), f32)]
        + [vmem(blocked, f32)] * 3
        + [
            vmem((2, BLOCK, WIDTH), bf16),
            vmem((2, BLOCK, WIDTH), f32),
            vmem((2, BLOCK, WIDTH), bf16),
            dma((41,)),
            dma((41,)),
            dma((56, 2)),
            dma((56, 2)),
            dma((26,)),
        ],
        compiler_params=pltpu.CompilerParams(
            collective_id=0, has_side_effects=True, vmem_limit_bytes=VMEM
        ),
        name="gather",
    )(
        keys.reshape(blocked), values.reshape(blocked), query.reshape(blocked),
        d_out, output.reshape(blocked), row_logsum,
    )
    pz, py = pl.pallas_call(
        pair_kernel,
        out_shape=[shape((32, 3, BLOCK, HD), bf16), shape((16, 3, BLOCK, HD), bf16)],
        in_specs=[vmem_spec] + [any_spec] * 8 + [vmem_spec] * 2,
        out_specs=[any_spec] * 2,
        scratch_shapes=[
            vmem((8, 128), jnp.int32),
            smem((8, 128), jnp.int32),
            vmem((2, 2, BLOCK, HD), bf16),
            vmem((2, 2, BLOCK, HD), bf16),
            vmem((2, 2, BLOCK, HD), bf16),
            vmem((2, 2, BLOCK, HD), bf16),
            vmem((16, BLOCK, HD), f32),
            vmem((32, BLOCK, HD), f32),
            vmem((2, 2, BLOCK, HD), f32),
            vmem((2, 2, BLOCK, HD), bf16),
            vmem((16, BLOCK, HD), bf16),
            vmem((32, BLOCK, HD), bf16),
            vmem((2, BLOCK, HD), bf16),
            dma,
            dma((2, 2, 4)),
            dma((2,)),
            dma((2, 32)),
            dma((2, 32)),
        ],
        compiler_params=pltpu.CompilerParams(vmem_limit_bytes=VMEM),
        name="pairs",
    )(selected.T, kz, vz, qz, gz, qy, gy, ky, vy, sz, sy)
    piece = (BLK_DEV, 3, BLOCK, HD)
    out_q, out_k, out_v = pl.pallas_call(
        scatter_kernel,
        out_shape=[shape(blocked, bf16)] * 3,
        in_specs=[any_spec] * 6,
        out_specs=[vmem_spec] * 3,
        scratch_shapes=[
            vmem((4,) + piece, bf16),
            vmem((4,) + piece, bf16),
            vmem((2, 2, 3, BLOCK, HD), bf16),
            vmem((2,) + piece, bf16),
            vmem((4,) + piece, bf16),
            vmem((2, 2, 3, BLOCK, HD), bf16),
            vmem((2,) + piece, bf16),
            vmem(blocked, f32),
            vmem(blocked, f32),
            vmem(blocked, f32),
            vmem((BLOCK, WIDTH), bf16),
            vmem((6, BLOCK, WIDTH), bf16),
            vmem((BLOCK, WIDTH), f32),
            vmem((2, BLOCK, WIDTH), bf16),
            dma((26,)),
            dma((26,)),
            dma((24, 2)),
            dma((24, 2)),
            dma((12,)),
        ],
        compiler_params=pltpu.CompilerParams(
            collective_id=1, has_side_effects=True, vmem_limit_bytes=VMEM
        ),
        name="scatter",
    )(pz, py, own_q, own_k, own_v, own_f)
    out_q, out_k, out_v = pl.pallas_call(
        keep_kernel,
        out_shape=[shape(blocked, bf16)] * 3,
        in_specs=[any_spec] * 3,
        out_specs=[any_spec] * 3,
        scratch_shapes=[vmem((3,) + blocked, bf16), dma((3, 2)), dma((3, 2))],
        compiler_params=pltpu.CompilerParams(vmem_limit_bytes=VMEM),
        name="keep",
    )(out_q, out_k, out_v)
    flat = (BLK_DEV * BLOCK, WIDTH)
    return out_q.reshape(flat), out_k.reshape(flat), out_v.reshape(flat)


def solution(mesh):
    in_specs = (
        P("seq", "head"),
        P("seq", "head"),
        P("seq", "head"),
        P("seq", "head"),
        P(("seq", "head"), None),
        P("head", "seq"),
        P(),
    )
    out_specs = (P("seq", "head"), P("seq", "head"), P("seq", "head"))
    return jax.shard_map(body, mesh=mesh, in_specs=in_specs, out_specs=out_specs, check_vma=False)
```
